512 devices in a mesh: gx: 16 (over x, z_hi), gy: 32 (over y, z_lo, core).
Axes of the slice: x: 4, y: 8, z: 8 (z_hi: 4, z_lo: 2; z = z_hi * 2 + z_lo), core: 2. Of those that a mesh axis runs over, the one named last changes fastest.
Arguments:
- right_sides: float32 [65536, 64], P(('gx', 'gy')), may hold values from -6 to 6
- factor_u: float32 [8, 65536, 128], P(None, ('gx', 'gy')), may hold values from -6 to 6
- factor_v: float32 [8, 65536, 128], P(None, ('gx', 'gy')), may hold values from -1 to 1, as said below
Outputs:
- solution: float32 [65536, 64], P(('gx', 'gy'))
The draws below stay inside these ranges and needn't reach their ends.
Inputs may be any that keep to these rules, and one draw needn't show every extreme that they name: `factor_v`: entries of level k are independent with standard deviation 0.02 / sqrt(2**(k + 1) * 128).
All inputs are finite; a program needn't handle non-finite values.
Results may differ from the reference program's by a relative error of at most 0.0001.
Values sent between devices are 32-bit elements; how exact they have to be, the bound alone decides.
No kernel may reach another device: no remote copies, remote signals or barrier semaphores. Data moves between devices by JAX's collectives and lax.ppermute only.
A program may use at most 64 MiB of HBM per device.

```python
import jax
import jax.numpy as jnp
from jax import lax

ROWS = 128
RANK = 128
NRHS = 64
LEVELS = 8
ORDER = 65536


def draw_factor_v(key, part):
    key = jax.random.fold_in(key, 7)
    level_ids = jnp.arange(LEVELS, dtype=jnp.float32)[:, None, None]
    spread = 0.02 * jax.lax.rsqrt(ROWS * 2.0 ** (level_ids + 1.0))
    values = jnp.clip(jax.random.normal(key, (LEVELS, ORDER, RANK), jnp.float32), -5.0, 5.0)
    return (values * spread).astype(jnp.float32)


def shard_levels(stream_key, shape, shards, low, high):
    def one(position, shards_of):
        steps = jax.random.uniform(jax.random.fold_in(jax.random.fold_in(stream_key, 6), position), (shards_of,), jnp.float32, low / len(shards), high / len(shards))
        return jnp.repeat(jnp.exp(steps), shape[position] // shards_of).reshape((-1,) + (1,) * (len(shape) - position - 1))

    gain = one(*shards[0])
    for cut in shards[1:]:
        gain = gain * one(*cut)
    return gain


def scatter_about(stream_key, dims, scale, limit, shards=(), kind=jnp.bfloat16):
    level = shard_levels(stream_key, dims, shards, -0.22, 0.18) if shards else 1.0
    entries = jax.random.normal(stream_key, dims, jnp.float32) * scale * level
    return jnp.minimum(jnp.maximum(entries, -limit), limit).astype(kind)


def setup_inputs(seed: int = 0) -> dict:
    key_list = jax.random.split(jax.random.key(seed), 4)
    right_sides = scatter_about(key_list[0], (ORDER, NRHS), 1.0, 6.0, ((0, 512),), jnp.float32)
    factor_u = scatter_about(key_list[1], (LEVELS, ORDER, RANK), 1.0, 6.0, ((1, 512),), jnp.float32)
    factor_v = draw_factor_v(jax.random.fold_in(key_list[3], 71), 0)
    return {"right_sides": right_sides, "factor_u": factor_u, "factor_v": factor_v}


def reference(right_sides, factor_u, factor_v):
    highest = lax.Precision.HIGHEST
    solution = right_sides
    carried = [factor_u[level] for level in range(LEVELS)]
    total_rows = right_sides.shape[0]
    for level in range(LEVELS):
        half = ROWS * 2 ** (level + 1)
        nodes = total_rows // (2 * half)
        rest = jnp.concatenate([solution] + carried[level + 1:], axis=1)
        width = rest.shape[1]
        left = carried[level].reshape(nodes, 2, half, RANK)
        right = factor_v[level].reshape(nodes, 2, half, RANK)
        stacked = rest.reshape(nodes, 2, half, width)
        gram = jnp.einsum('nshr,nshq->nsrq', right, left, precision=highest)
        projected = jnp.einsum('nshr,nshc->nsrc', right, stacked, precision=highest)
        identity = jnp.broadcast_to(jnp.eye(RANK, dtype=jnp.float32), (nodes, RANK, RANK)).astype(gram.dtype)
        coupling = jnp.concatenate([jnp.concatenate([identity, gram[:, 1]], axis=2), jnp.concatenate([gram[:, 0], identity], axis=2)], axis=1)
        target = jnp.concatenate([projected[:, 1], projected[:, 0]], axis=1)
        solved = jnp.linalg.solve(coupling, target)
        first = jnp.einsum('nhr,nrc->nhc', left[:, 0], solved[:, :RANK], precision=highest)
        second = jnp.einsum('nhr,nrc->nhc', left[:, 1], solved[:, RANK:], precision=highest)
        rest = (stacked - jnp.stack([first, second], axis=1)).reshape(total_rows, width)
        solution = rest[:, :NRHS]
        newer = [rest[:, NRHS + RANK * j:NRHS + RANK * (j + 1)] for j in range(LEVELS - level - 1)]
        carried = carried[:level + 1] + newer
    return solution
```

```python
import jax
import jax.numpy as jnp
from jax import lax
from jax.sharding import PartitionSpec as P

HIGHEST = lax.Precision.HIGHEST


def dot(a, b):
    return jnp.dot(a, b, precision=HIGHEST)


def partner(value, bit, gy_bits):
    axis, shift = ("gy", bit) if bit < gy_bits else ("gx", bit - gy_bits)
    mask = 1 << shift
    return lax.ppermute(value, axis, [(s, s ^ mask) for s in range(lax.axis_size(axis))])


def groups_of(count, size):
    return [list(range(i, i + size)) for i in range(0, count, size)]


def inverse_of(error):
    rank = error.shape[0]
    total = jnp.eye(rank, dtype=jnp.float32) + error
    power = error
    for step in range(6):
        power = dot(power, power)
        total = total + dot(total, power)
    return total


def solve_own(gram_own, gram_sib, proj_own, proj_sib):
    inverse = inverse_of(dot(gram_own, gram_sib))
    return dot(proj_sib - dot(proj_own, gram_sib), inverse)


def chip_halves(core, mine, other):
    first = jnp.where(core == 0, mine, other)
    second = jnp.where(core == 0, other, mine)
    return jnp.concatenate([first, second], axis=0)


def shards(right_sides, factor_u, factor_v):
    gy_size = lax.axis_size("gy")
    gy_bits = gy_size.bit_length() - 1
    levels, rows, rank = factor_u.shape
    gy = lax.axis_index("gy")
    core = gy & 1
    pairs = groups_of(gy_size, 2)
    quads = groups_of(gy_size, 4)
    same_core = [list(range(c, gy_size, 2)) for c in range(2)]
    chips = gy_size // 2

    carried = jnp.concatenate(
        [factor_u[j].T for j in range(levels)] + [right_sides.T], axis=0
    )

    for level in range(gy_bits - 2):
        local = dot(carried, factor_v[level])
        half = (local.shape[0] - rank) // 2
        keep = lax.dynamic_slice_in_dim(local, rank + core * half, half, 0)
        give = lax.dynamic_slice_in_dim(local, rank + (1 - core) * half, half, 0)
        gram = local[:rank]
        summed = jnp.concatenate([gram, keep], axis=0) + partner(
            jnp.concatenate([gram, give], axis=0), 0, gy_bits
        )
        for bit in range(1, level + 1):
            summed = summed + partner(summed, bit, gy_bits)
        sibling = partner(summed, level + 1, gy_bits)
        part = solve_own(summed[:rank], sibling[:rank], summed[rank:], sibling[rank:])
        z = lax.all_gather(part, "gy", axis_index_groups=pairs, axis=0, tiled=True)
        carried = carried[rank:] - dot(z, carried[:rank])

    level = gy_bits - 2
    local = dot(carried, factor_v[level])
    half = local.shape[0] // 2
    keep = lax.dynamic_slice_in_dim(local, core * half, half, 0)
    give = lax.dynamic_slice_in_dim(local, (1 - core) * half, half, 0)
    chip_sum = keep + partner(give, 0, gy_bits)
    share = -(-half // (8 * chips)) * 8
    chip_sum = jnp.pad(chip_sum, ((0, share * chips - half), (0, 0)))
    pieces = lax.all_to_all(
        chip_sum.reshape(chips, share, rank), "gy", 0, 0, axis_index_groups=same_core
    )
    both = pieces.reshape(2, chips // 2, share, rank).sum(axis=1)
    everyone = jnp.broadcast_to(both, (chips, 2, share, rank))
    gathered = lax.all_to_all(everyone, "gy", 0, 0, axis_index_groups=same_core)
    second_side = (gy >> (gy_bits - 1)) & 1 == 1
    first = gathered[:, 0].reshape(chips * share, rank)[:half]
    second = gathered[:, 1].reshape(chips * share, rank)[:half]
    own = jnp.where(second_side, second, first)
    sib = jnp.where(second_side, first, second)
    other = partner(jnp.concatenate([own, sib], axis=0), 0, gy_bits)
    own = chip_halves(core, own, other[:half])
    sib = chip_halves(core, sib, other[half:])
    z = solve_own(own[:rank], sib[:rank], own[rank:], sib[rank:])
    carried = carried[rank:] - dot(z, carried[:rank])

    level = gy_bits - 1
    count = levels - level
    width = carried.shape[0]
    state = jnp.concatenate([dot(carried, factor_v[j]) for j in range(level, levels)], axis=0)
    half = count * width // 2
    keep = lax.dynamic_slice_in_dim(state, core * half, half, 0)
    give = lax.dynamic_slice_in_dim(state, (1 - core) * half, half, 0)
    chip_sum = keep + partner(give, 0, gy_bits)
    share = half // chips
    pieces = lax.all_to_all(
        chip_sum.reshape(chips, share, rank), "gy", 0, 0, axis_index_groups=same_core
    )
    piece = pieces.sum(axis=0)
    both = jnp.stack([piece, partner(piece, level + 1, gy_bits)])
    everyone = jnp.broadcast_to(both, (chips, 2, share, rank))
    gathered = lax.all_to_all(everyone, "gy", 0, 0, axis_index_groups=same_core)
    own = gathered[:, 0].reshape(half, rank)
    sib = gathered[:, 1].reshape(half, rank)
    other = partner(jnp.concatenate([own, sib], axis=0), 0, gy_bits)
    own = chip_halves(core, own, other[:half])
    sib = chip_halves(core, sib, other[half:])

    while True:
        own = own.reshape(count, width, rank)
        sib = sib.reshape(count, width, rank)
        gram_own = own[0, :rank]
        z = solve_own(gram_own, sib[0, :rank], own[0, rank:], sib[0, rank:])
        if count > 1:
            z_sib = own[0, rank:] - dot(z, gram_own)
            z_both = jnp.concatenate([z, z_sib], axis=1)
            node = []
            for j in range(1, count):
                left = jnp.concatenate([own[j, :rank], sib[j, :rank]], axis=0)
                node.append(own[j, rank:] + sib[j, rank:] - dot(z_both, left))
        carried = carried[rank:] - dot(z, carried[:rank])
        if count == 1:
            break
        level, count, width = level + 1, count - 1, width - rank
        own = jnp.concatenate(node, axis=0)
        total = own.shape[0]
        if total > 1024:
            quarter = total // 4
            part = lax.dynamic_slice_in_dim(own, (gy & 3) * quarter, quarter, 0)
            sib = lax.all_gather(
                partner(part, level + 1, gy_bits), "gy", axis_index_groups=quads, axis=0, tiled=True
            )
        elif total > 512:
            part = lax.dynamic_slice_in_dim(own, core * (total // 2), total // 2, 0)
            sib = lax.all_gather(
                partner(part, level + 1, gy_bits), "gy", axis_index_groups=pairs, axis=0, tiled=True
            )
        else:
            sib = partner(own, level + 1, gy_bits)
    return carried.T


def solution(mesh):
    placed = (P(("gx", "gy"), None), P(None, ("gx", "gy"), None), P(None, ("gx", "gy"), None))
    return jax.shard_map(
        shards, mesh=mesh, in_specs=placed, out_specs=P(("gx", "gy"), None), check_vma=False
    )
```

```python
import functools

import jax
import jax.numpy as jnp
from jax import lax
from jax.experimental import pallas as pl
from jax.experimental.pallas import tpu as pltpu
from jax.sharding import PartitionSpec as P

VMEM_BYTES = 40 * 2**20


def dot(a, b):
    return jnp.dot(a, b, precision=lax.Precision.HIGH)


def split(value):
    high = value.astype(jnp.bfloat16)
    low = (value - high.astype(jnp.float32)).astype(jnp.bfloat16)
    return high, low


def dot_split(a, b):
    def part(x, y):
        return jnp.dot(x, y, preferred_element_type=jnp.float32)

    return part(a[0], b[0]) + (part(a[0], b[1]) + part(a[1], b[0]))


def kdot(a, b):
    return dot_split(split(a), split(b))


def inverse_of(error):
    total = jnp.eye(error.shape[0], dtype=jnp.float32) + error
    power = error
    for step in range(6):
        parts = split(power)
        power = dot_split(parts, parts)
        total = total + kdot(total, power)
    return total


def solve_own(gram_own, gram_sib, proj_own, proj_sib):
    inverse = inverse_of(kdot(gram_own, gram_sib))
    return kdot(proj_sib - kdot(proj_own, gram_sib), inverse)


def leaf_kernel(own, sib, z_out):
    rank = own.shape[1]
    z_out[...] = solve_own(own[:rank], sib[:rank], own[rank:], sib[rank:])


def node_kernel(count, own, sib, ops_own, ops_sib, sums, z_out, node_out):
    rank = own.shape[1]
    width = own.shape[0] - rank
    gram_own = own[:rank]
    proj_own = own[rank:]
    z = solve_own(gram_own, sib[:rank], proj_own, sib[rank:])
    z_out[...] = z
    z_sib = proj_own - kdot(z, gram_own)
    z_both = split(jnp.concatenate([z, z_sib], axis=1))
    for j in range(count):
        at = slice(j * rank, (j + 1) * rank)
        left = split(jnp.concatenate([ops_own[at], ops_sib[at]], axis=0))
        rows = slice(j * width, (j + 1) * width)
        node_out[rows] = sums[rows] - dot_split(z_both, left)


def call(kernel, outs, *args):
    flops = 2 * 3 * 128 * 128 * (sum(a.shape[0] for a in args) + 14 * 128)
    return pl.pallas_call(
        kernel,
        out_shape=[jax.ShapeDtypeStruct(o, jnp.float32) for o in outs],
        compiler_params=pltpu.CompilerParams(vmem_limit_bytes=VMEM_BYTES),
        cost_estimate=pl.CostEstimate(
            flops=flops, bytes_accessed=4 * sum(a.size for a in args), transcendentals=0
        ),
    )(*args)


def solve_leaf(own, sib):
    rank = own.shape[1]
    return call(leaf_kernel, [(own.shape[0] - rank, rank)], own, sib)[0]


def solve_node(own, sib, ops_own, ops_sib, sums):
    rank = own.shape[1]
    count = ops_own.shape[0] // rank
    outs = [(own.shape[0] - rank, rank), sums.shape]
    return call(functools.partial(node_kernel, count), outs, own, sib, ops_own, ops_sib, sums)


def partner(value, bit, gy_bits):
    axis, shift = ("gy", bit) if bit < gy_bits else ("gx", bit - gy_bits)
    mask = 1 << shift
    return lax.ppermute(value, axis, [(s, s ^ mask) for s in range(lax.axis_size(axis))])


def groups_of(count, size):
    return [list(range(i, i + size)) for i in range(0, count, size)]


def chip_groups(count, chips):
    size = 2 * chips
    return [
        list(range(start + c, start + size, 2)) for start in range(0, count, size) for c in range(2)
    ]


def pad_rows(value, rows):
    return jnp.pad(value, ((0, rows - value.shape[0]), (0, 0)))


def up8(value):
    return -(-value // 8) * 8


def reduce_shares(both, sums, chips, groups):
    rank = both.shape[1]
    share_both = up8(-(-both.shape[0] // chips))
    share_sums = up8(-(-sums.shape[0] // chips))
    sent = jnp.concatenate(
        [
            pad_rows(both, share_both * chips).reshape(chips, share_both, rank),
            pad_rows(sums, share_sums * chips).reshape(chips, share_sums, rank),
        ],
        axis=1,
    )
    pieces = lax.all_to_all(sent, "gy", 0, 0, axis_index_groups=groups)
    return pieces, share_both


def gather_shares(first, second, sums, rows_both, rows_sums, chips, groups):
    rank = sums.shape[1]
    n = first.shape[0]
    share = jnp.concatenate([first, second, sums], axis=0)
    out = lax.all_to_all(
        jnp.broadcast_to(share, (chips,) + share.shape), "gy", 0, 0, axis_index_groups=groups
    )
    return (
        out[:, :n].reshape(-1, rank)[:rows_both],
        out[:, n : 2 * n].reshape(-1, rank)[:rows_both],
        out[:, 2 * n :].reshape(-1, rank)[:rows_sums],
    )


def half_of(value, core):
    rows = value.shape[0] // 2
    return lax.dynamic_slice_in_dim(value, core * rows, rows, 0)


def from_cores(gathered, at, rows, size):
    return [gathered[c * size + at : c * size + at + rows] for c in range(2)]


def shards(right_sides, factor_u, factor_v):
    gy_size = lax.axis_size("gy")
    gy_bits = gy_size.bit_length() - 1
    levels, _, rank = factor_u.shape
    gy = lax.axis_index("gy")
    core = gy & 1
    pairs = groups_of(gy_size, 2)
    quads = groups_of(gy_size, 4)

    carried = jnp.concatenate([factor_u[j].T for j in range(levels)] + [right_sides.T], axis=0)

    for level in (0, 2):
        lower = dot(carried, factor_v[level])
        upper = dot(carried, factor_v[level + 1])
        shared = 2 * rank
        rest = (carried.shape[0] - shared) // 2

        def rows_for(side):
            both = [lower[:shared], half_of(lower[shared:], side), upper[:rank]]
            sums = [upper[rank:shared], half_of(upper[shared:], side)]
            return jnp.concatenate(both + sums, axis=0)

        chip = rows_for(core) + partner(rows_for(1 - core), 0, gy_bits)
        top = shared + rest
        n_both = top + rank
        n_sums = rank + rest
        if level == 0:
            near = partner(chip, 1, gy_bits)
            own, sib = chip[:n_both], near[:n_both]
            sums = chip[n_both:] + near[n_both:]
        else:
            chips = 8
            groups = chip_groups(gy_size, chips)
            pieces, share = reduce_shares(chip[:n_both], chip[n_both:], chips, groups)
            side_sums = pieces.reshape((2, chips // 2) + pieces.shape[1:]).sum(axis=1)
            first, second, sums = gather_shares(
                side_sums[0, :share],
                side_sums[1, :share],
                side_sums[0, share:] + side_sums[1, share:],
                n_both,
                n_sums,
                chips,
                groups,
            )
            second_side = (gy >> (level + 1)) & 1 == 1
            own = jnp.where(second_side, second, first)
            sib = jnp.where(second_side, first, second)
        z_low, node = solve_node(own[:top], sib[:top], own[top:], sib[top:], sums)
        z_up = solve_leaf(node, partner(node, level + 2, gy_bits))
        halves = lax.all_gather(
            jnp.concatenate([z_low[rank:], z_up], axis=0),
            "gy",
            axis_index_groups=pairs,
            axis=0,
            tiled=True,
        )
        z_rest = jnp.concatenate(
            [
                jnp.concatenate(from_cores(halves, 0, rest, 2 * rest), axis=0),
                jnp.concatenate(from_cores(halves, rest, rest, 2 * rest), axis=0),
            ],
            axis=1,
        )
        left = carried[:rank]
        next_left = carried[rank:shared] - dot(z_low[:rank], left)
        carried = carried[shared:] - dot(z_rest, jnp.concatenate([left, next_left], axis=0))

    level = gy_bits - 1
    count = levels - level
    width = carried.shape[0]
    first = dot(carried, factor_v[level])
    higher = [dot(carried, factor_v[j]) for j in range(level + 1, levels)]
    both = jnp.concatenate([first] + [h[:rank] for h in higher], axis=0)
    sums = jnp.concatenate([h[rank:] for h in higher], axis=0)
    n_both = both.shape[0] // 2
    n_sums = sums.shape[0] // 2

    def state_for(side):
        return jnp.concatenate([half_of(both, side), half_of(sums, side)], axis=0)

    chip = state_for(core) + partner(state_for(1 - core), 0, gy_bits)
    chips = gy_size // 2
    groups = chip_groups(gy_size, chips)
    pieces, share = reduce_shares(chip[:n_both], chip[n_both:], chips, groups)
    piece = pieces.sum(axis=0)
    near = partner(piece, level + 1, gy_bits)
    mine = jnp.concatenate(
        gather_shares(
            piece[:share], near[:share], piece[share:] + near[share:], n_both, n_sums, chips, groups
        ),
        axis=0,
    )
    other = partner(mine, 0, gy_bits)
    front = jnp.where(core == 0, mine, other)
    back = jnp.where(core == 0, other, mine)

    def joined(at, rows):
        return jnp.concatenate([front[at : at + rows], back[at : at + rows]], axis=0)

    own = joined(0, n_both)
    sib = joined(n_both, n_both)
    sums = joined(2 * n_both, n_sums)
    z, node = solve_node(own[:width], sib[:width], own[width:], sib[width:], sums)
    carried = carried[rank:] - dot(z, carried[:rank])

    while True:
        level, count, width = level + 1, count - 1, width - rank
        total = node.shape[0]
        if total > 1024:
            quarter = total // 4
            part = lax.dynamic_slice_in_dim(node, (gy & 3) * quarter, quarter, 0)
            near = lax.all_gather(
                partner(part, level + 1, gy_bits), "gy", axis_index_groups=quads, axis=0, tiled=True
            )
        elif total > 512:
            near = lax.all_gather(
                partner(half_of(node, core), level + 1, gy_bits),
                "gy",
                axis_index_groups=pairs,
                axis=0,
                tiled=True,
            )
        else:
            near = partner(node, level + 1, gy_bits)
        if count == 1:
            z = solve_leaf(node, near)
            return (carried[rank:] - dot(z, carried[:rank])).T
        node = node.reshape(count, width, rank)
        near = near.reshape(count, width, rank)
        ops_own = node[1:, :rank].reshape(-1, rank)
        ops_sib = near[1:, :rank].reshape(-1, rank)
        sums = (node[1:, rank:] + near[1:, rank:]).reshape(-1, rank)
        z, node = solve_node(node[0], near[0], ops_own, ops_sib, sums)
        carried = carried[rank:] - dot(z, carried[:rank])


def solution(mesh):
    placed = (P(("gx", "gy"), None), P(None, ("gx", "gy"), None), P(None, ("gx", "gy"), None))
    return jax.shard_map(
        shards, mesh=mesh, in_specs=placed, out_specs=P(("gx", "gy"), None), check_vma=False
    )
```

```python
import functools

import jax
import jax.numpy as jnp
from jax import lax
from jax.experimental import pallas as pl
from jax.experimental.pallas import tpu as pltpu
from jax.sharding import PartitionSpec as P

VMEM_BYTES = 40 * 2**20


def split(value):
    high = value.astype(jnp.bfloat16)
    low = (value - high.astype(jnp.float32)).astype(jnp.bfloat16)
    return high, low


def dot_split(a, b):
    def part(x, y):
        return jnp.dot(x, y, preferred_element_type=jnp.float32)

    return part(a[0], b[0]) + (part(a[0], b[1]) + part(a[1], b[0]))


def kdot(a, b):
    return dot_split(split(a), split(b))


def inverse_of(error):
    total = jnp.eye(error.shape[0], dtype=jnp.float32) + error
    power = error
    for step in range(6):
        parts = split(power)
        power = dot_split(parts, parts)
        total = total + kdot(total, power)
    return total


def solve_own(gram_own, gram_sib, proj_own, proj_sib):
    inverse = inverse_of(kdot(gram_own, gram_sib))
    return kdot(proj_sib - kdot(proj_own, gram_sib), inverse)


def solve_node(own, sib, ops_own, ops_sib, sums):
    rank = own.shape[1]
    width = own.shape[0] - rank
    gram_own, proj_own = own[:rank], own[rank:]
    z = solve_own(gram_own, sib[:rank], proj_own, sib[rank:])
    z_sib = proj_own - kdot(z, gram_own)
    z_both = split(jnp.concatenate([z, z_sib], axis=1))
    node = []
    for j in range(ops_own.shape[0] // rank):
        at = slice(j * rank, (j + 1) * rank)
        left = split(jnp.concatenate([ops_own[at], ops_sib[at]], axis=0))
        node.append(sums[j * width : (j + 1) * width] - dot_split(z_both, left))
    return z, jnp.concatenate(node, axis=0)


def put_rows(out, base, size, start, value):
    at, rows = 0, value.shape[0]
    while at < rows:
        i, r = divmod(start + at, size)
        n = min(size - r, rows - at)
        out[i, base + r : base + r + n] = value[at : at + n]
        at += n


def get_rows(ref, base, size):
    return jnp.concatenate([ref[i, pl.ds(base, size)] for i in range(ref.shape[0])], axis=0)


def bit_of(axis, bit):
    return (lax.axis_index(axis) >> bit) & 1


def times8(value, rows):
    return pl.multiple_of(value * rows, 8)


def project_pair(carried, v, keep, give, low, up, shares):
    rank = v.shape[1]
    parts = split(carried)
    low[...] = dot_split(parts, split(v[0]))
    up[...] = dot_split(parts, split(v[1]))
    shared = 2 * rank
    rest = (carried.shape[0] - shared) // 2
    size_both = (shared + rest + rank) // shares
    size_sums = (rank + rest) // shares
    core = bit_of("gy", 0)
    for out, side in ((keep, core), (give, 1 - core)):
        half = pl.ds(shared + times8(side, rest), rest)
        put_rows(out, 0, size_both, 0, low[:shared])
        put_rows(out, 0, size_both, shared, low[half])
        put_rows(out, 0, size_both, shared + rest, up[:rank])
        put_rows(out, size_both, size_sums, 0, up[rank:shared])
        put_rows(out, size_both, size_sums, rank, up[half])


def start_kernel(shares, u, v, y, carried, keep, give, low, up):
    levels, _, rank = u.shape
    for j in range(levels):
        carried[j * rank : (j + 1) * rank] = u[j].T
    carried[levels * rank :] = y[...].T
    project_pair(carried[...], v, keep, give, low, up, shares)


def lower_node_kernel(bit, n_both, rest, pieces, z_out, node_out):
    side = bit_of("gy", bit)
    rank = z_out.shape[1]
    if n_both is None:
        top = 2 * rank + rest
        own = pieces[side, :top]
        sib = pieces[1 - side, :top]
        ops_own = pieces[side, top : top + rank]
        ops_sib = pieces[1 - side, top : top + rank]
        sums = pieces[0, top + rank :] + pieces[1, top + rank :]
    else:
        top = 2 * rank + rest
        own = get_rows(pieces, times8(side, n_both), n_both)
        sib = get_rows(pieces, times8(1 - side, n_both), n_both)
        own, ops_own = own[:top], own[top:]
        sib, ops_sib = sib[:top], sib[top:]
        sums = get_rows(pieces, 2 * n_both, pieces.shape[1] - 2 * n_both)
    z, node = solve_node(own, sib, ops_own, ops_sib, sums)
    z_out[...] = z
    node_out[...] = node


def lower_leaf_kernel(bit, pair, z_low, out):
    side = bit_of("gy", bit)
    rank = pair.shape[2]
    rest = z_low.shape[0] - rank
    own, sib = pair[side], pair[1 - side]
    out[:rest] = z_low[rank:]
    out[rest:] = solve_own(own[:rank], sib[:rank], own[rank:], sib[rank:])


def advanced(carried, z_low, halves):
    rank = z_low.shape[1]
    rest = halves.shape[1] // 2
    left = carried[:rank]
    next_left = carried[rank : 2 * rank] - kdot(z_low[:rank], left)
    z_rest = jnp.concatenate(
        [
            jnp.concatenate([halves[c, :rest], halves[c, rest:]], axis=1) for c in range(2)
        ],
        axis=0,
    )
    return carried[2 * rank :] - kdot(z_rest, jnp.concatenate([left, next_left], axis=0))


def next_pair_kernel(shares, carried, z_low, halves, v, new, keep, give, low, up):
    value = advanced(carried, z_low, halves)
    new[...] = value
    project_pair(value, v, keep, give, low, up, shares)


def upper_kernel(shares, carried, z_low, halves, v, new, keep, give, both, sums):
    value = advanced(carried, z_low, halves)
    new[...] = value
    rank = v.shape[1]
    count, width = v.shape[0], value.shape[0]
    parts = split(value)
    both[:width] = dot_split(parts, split(v[0]))
    for j in range(1, count):
        rows = dot_split(parts, split(v[j]))
        both[width + (j - 1) * rank : width + j * rank] = rows[:rank]
        sums[(j - 1) * (width - rank) : j * (width - rank)] = rows[rank:]
    half_both, half_sums = both.shape[0] // 2, sums.shape[0] // 2
    core = bit_of("gy", 0)
    for out, side in ((keep, core), (give, 1 - core)):
        put_rows(out, 0, half_both // shares, 0, both[pl.ds(times8(side, half_both), half_both)])
        put_rows(
            out,
            half_both // shares,
            half_sums // shares,
            0,
            sums[pl.ds(times8(side, half_sums), half_sums)],
        )


def updated(carried, z):
    rank = z.shape[1]
    return carried[rank:] - kdot(z, carried[:rank])


def top_node_kernel(width, n_both, n_sums, mine, other, carried, new, node_out, quarter):
    rank = carried.shape[1]
    core = bit_of("gy", 0)
    side = bit_of("gx", 0)
    halves = []
    for c in range(2):
        take = core == c
        halves.append(
            [
                jnp.where(take, get_rows(mine, base, size), get_rows(other, base, size))
                for base, size in (
                    (times8(side, n_both), n_both),
                    (times8(1 - side, n_both), n_both),
                    (2 * n_both, n_sums),
                )
            ]
        )
    own, sib, sums = [jnp.concatenate([a, b], axis=0) for a, b in zip(*halves)]
    z, node = solve_node(own[:width], sib[:width], own[width:], sib[width:], sums)
    node_out[...] = node
    rows = quarter.shape[0]
    at = lax.axis_index("gy") & 3
    quarter[...] = node_out[pl.ds(times8(at, rows), rows)]
    new[...] = updated(carried, z)


def upper_node_kernel(count, own, sib, carried, new, node_out, *part):
    rank = carried.shape[1]
    width = own.shape[0] // count

    def rows(ref, j, low, high):
        return ref[j * width + low : j * width + high]

    ops_own = jnp.concatenate([rows(own, j, 0, rank) for j in range(1, count)], axis=0)
    ops_sib = jnp.concatenate([rows(sib, j, 0, rank) for j in range(1, count)], axis=0)
    sums = jnp.concatenate(
        [rows(own, j, rank, width) + rows(sib, j, rank, width) for j in range(1, count)], axis=0
    )
    z, node = solve_node(own[:width], sib[:width], ops_own, ops_sib, sums)
    node_out[...] = node
    if part:
        n = part[0].shape[0]
        part[0][...] = node_out[pl.ds(times8(bit_of("gy", 0), n), n)]
    new[...] = updated(carried, z)


def last_kernel(axis, bit, pair, carried, out):
    side = bit_of(axis, bit)
    rank = carried.shape[1]
    own, sib = pair[side], pair[1 - side]
    z = solve_own(own[:rank], sib[:rank], own[rank:], sib[rank:])
    out[...] = updated(carried, z).T


def call(kernel, outs, *args, scratch=()):
    rows = sum(a.size // 128 for a in args)
    return pl.pallas_call(
        kernel,
        out_shape=[jax.ShapeDtypeStruct(o, jnp.float32) for o in outs],
        scratch_shapes=[pltpu.VMEM(s, jnp.float32) for s in scratch],
        compiler_params=pltpu.CompilerParams(vmem_limit_bytes=VMEM_BYTES),
        cost_estimate=pl.CostEstimate(
            flops=6 * 128 * 128 * (rows + 14 * 128),
            bytes_accessed=512 * rows,
            transcendentals=0,
        ),
    )(*args)


def bit_groups(count, bits):
    mask = sum(1 << b for b in bits)
    return [
        [
            base | sum(((i >> q) & 1) << b for q, b in enumerate(bits))
            for i in range(1 << len(bits))
        ]
        for base in range(count)
        if not base & mask
    ]


def swap_cores(value):
    return lax.ppermute(value, "gy", [(s, s ^ 1) for s in range(lax.axis_size("gy"))])


def pair_gather(value, axis, bit, tiled=False):
    groups = bit_groups(lax.axis_size(axis), [bit])
    return lax.all_gather(value, axis, axis_index_groups=groups, tiled=tiled)


def exchange(value, axis, bits):
    count = lax.axis_size(axis)
    return lax.all_to_all(value, axis, 0, 0, axis_index_groups=bit_groups(count, bits))


def to_all(value, axis, bits):
    return exchange(jnp.broadcast_to(value, (1 << len(bits),) + value.shape), axis, bits)


def pad_rows(value, rows):
    return jnp.pad(value, ((0, rows - value.shape[0]), (0, 0)))


def up8(value):
    return -(-value // 8) * 8


def shards(right_sides, factor_u, factor_v):
    levels, _, rank = factor_u.shape
    gy_bits = lax.axis_size("gy").bit_length() - 1
    near_chips = [1, 2]

    rows = levels * rank + right_sides.shape[1]
    rest = (rows - 2 * rank) // 2
    top = 2 * rank + rest
    sent = (1, top + rank + rank + rest, rank)
    carried, keep, give = call(
        functools.partial(start_kernel, 1),
        [(rows, rank), sent, sent],
        factor_u,
        factor_v[:2],
        right_sides,
        scratch=[(rows, rank)] * 2,
    )
    chip = (keep + swap_cores(give))[0]
    pieces = to_all(chip, "gy", [1])
    z_low, node = call(
        functools.partial(lower_node_kernel, 1, None, rest),
        [(rank + rest, rank), (rank + rest, rank)],
        pieces,
    )
    pair = pair_gather(node, "gy", 2)
    mine = call(functools.partial(lower_leaf_kernel, 2), [(2 * rest, rank)], pair, z_low)[0]
    halves = pair_gather(mine, "gy", 0)

    rows -= 2 * rank
    rest = (rows - 2 * rank) // 2
    top = 2 * rank + rest
    n_both, n_sums = (top + rank) // 4, (rank + rest) // 4
    sent = (4, n_both + n_sums, rank)
    carried, keep, give = call(
        functools.partial(next_pair_kernel, 4),
        [(rows, rank), sent, sent],
        carried,
        z_low,
        halves,
        factor_v[2:4],
        scratch=[(rows, rank)] * 2,
    )
    chip = keep + swap_cores(give)
    piece = exchange(chip, "gy", near_chips).sum(axis=0)
    pair = pair_gather(piece, "gy", 3)
    share = jnp.concatenate(
        [pair[0, :n_both], pair[1, :n_both], pair[0, n_both:] + pair[1, n_both:]], axis=0
    )
    pieces = to_all(share, "gy", near_chips)
    z_low, node = call(
        functools.partial(lower_node_kernel, 3, n_both, rest),
        [(rank + rest, rank), (rank + rest, rank)],
        pieces,
    )
    pair = pair_gather(node, "gy", 4)
    mine = call(functools.partial(lower_leaf_kernel, 4), [(2 * rest, rank)], pair, z_low)[0]
    halves = pair_gather(mine, "gy", 0)

    rows -= 2 * rank
    level = gy_bits - 1
    count = levels - level
    all_both = rows + (count - 1) * rank
    all_sums = (count - 1) * (rows - rank)
    n_both, n_sums = all_both // 8, all_sums // 8
    sent = (4, n_both + n_sums, rank)
    carried, keep, give = call(
        functools.partial(upper_kernel, 4),
        [(rows, rank), sent, sent],
        carried,
        z_low,
        halves,
        factor_v[level:],
        scratch=[(all_both, rank), (all_sums, rank)],
    )
    chip = keep + swap_cores(give)
    piece = exchange(chip, "gy", near_chips).sum(axis=0)
    s_both, s_sums = up8(-(-n_both // 8)), up8(-(-n_sums // 8))
    sent = jnp.concatenate(
        [
            pad_rows(piece[:n_both], 8 * s_both).reshape(8, s_both, rank),
            pad_rows(piece[n_both:], 8 * s_sums).reshape(8, s_sums, rank),
        ],
        axis=1,
    )
    far = [3, 4, 5]
    sides = exchange(sent, ("gx", "gy"), far)
    sides = sides.reshape((2, 4) + sides.shape[1:]).sum(axis=1)
    share = jnp.concatenate(
        [sides[0, :s_both], sides[1, :s_both], sides[0, s_both:] + sides[1, s_both:]], axis=0
    )
    pieces = to_all(share, ("gx", "gy"), far)
    share = jnp.concatenate(
        [
            pieces[:, :s_both].reshape(-1, rank)[:n_both],
            pieces[:, s_both : 2 * s_both].reshape(-1, rank)[:n_both],
            pieces[:, 2 * s_both :].reshape(-1, rank)[:n_sums],
        ],
        axis=0,
    )
    mine = to_all(share, "gy", near_chips)
    other = swap_cores(mine)
    carried, node, part = call(
        functools.partial(top_node_kernel, rows, n_both, n_sums),
        [(rows - rank, rank), (all_sums, rank), (all_sums // 4, rank)],
        mine,
        other,
        carried,
    )

    gx = lax.axis_index("gx")

    def of_sibling(value, bit):
        pair = pair_gather(value, "gx", bit)
        return lax.dynamic_index_in_dim(pair, 1 - ((gx >> bit) & 1), 0, keepdims=False)

    quads = bit_groups(lax.axis_size("gy"), [0, 1])
    near = lax.all_gather(of_sibling(part, 1), "gy", axis_index_groups=quads, tiled=True)
    rows, count = rows - rank, count - 1
    out_rows = (count - 1) * (rows - rank)
    carried, node, part = call(
        functools.partial(upper_node_kernel, count),
        [(rows - rank, rank), (out_rows, rank), (out_rows // 2, rank)],
        node,
        near,
        carried,
    )
    near = pair_gather(of_sibling(part, 2), "gy", 0, tiled=True)
    rows, count = rows - rank, count - 1
    out_rows = (count - 1) * (rows - rank)
    carried, node = call(
        functools.partial(upper_node_kernel, count),
        [(rows - rank, rank), (out_rows, rank)],
        node,
        near,
        carried,
    )
    pair = pair_gather(node, "gx", 3)
    return call(functools.partial(last_kernel, "gx", 3), [right_sides.shape], pair, carried)[0]


def solution(mesh):
    placed = (P(("gx", "gy"), None), P(None, ("gx", "gy"), None), P(None, ("gx", "gy"), None))
    return jax.shard_map(
        shards, mesh=mesh, in_specs=placed, out_specs=P(("gx", "gy"), None), check_vma=False
    )
```

```python
import functools

import jax
import jax.numpy as jnp
from jax import lax
from jax.experimental import pallas as pl
from jax.experimental.pallas import tpu as pltpu
from jax.sharding import PartitionSpec as P

VMEM_BYTES = 40 * 2**20


def split(value):
    high = value.astype(jnp.bfloat16)
    low = (value - high.astype(jnp.float32)).astype(jnp.bfloat16)
    return high, low


def dot_split(a, b):
    def part(x, y):
        return jnp.dot(x, y, preferred_element_type=jnp.float32)

    return part(a[0], b[0]) + (part(a[0], b[1]) + part(a[1], b[0]))


def kdot(a, b):
    return dot_split(split(a), split(b))


def inverse_of(error):
    total = jnp.eye(error.shape[0], dtype=jnp.float32) + error
    power = error
    for step in range(6):
        parts = split(power)
        power = dot_split(parts, parts)
        total = total + kdot(total, power)
    return total


def solve_own(gram_own, gram_sib, proj_own, proj_sib):
    inverse = inverse_of(kdot(gram_own, gram_sib))
    return kdot(proj_sib - kdot(proj_own, gram_sib), inverse)


def solve_node(own, sib, ops_own, ops_sib, sums):
    rank = own.shape[1]
    width = own.shape[0] - rank
    gram_own, proj_own = own[:rank], own[rank:]
    z = solve_own(gram_own, sib[:rank], proj_own, sib[rank:])
    z_sib = proj_own - kdot(z, gram_own)
    z_both = split(jnp.concatenate([z, z_sib], axis=1))
    node = []
    for j in range(ops_own.shape[0] // rank):
        at = slice(j * rank, (j + 1) * rank)
        left = split(jnp.concatenate([ops_own[at], ops_sib[at]], axis=0))
        node.append(sums[j * width : (j + 1) * width] - dot_split(z_both, left))
    return z, jnp.concatenate(node, axis=0)


def put_rows(out, base, size, start, value):
    at, rows = 0, value.shape[0]
    while at < rows:
        i, r = divmod(start + at, size)
        n = min(size - r, rows - at)
        out[i, base + r : base + r + n] = value[at : at + n]
        at += n


def get_rows(ref, base, size):
    return jnp.concatenate([ref[i, pl.ds(base, size)] for i in range(ref.shape[0])], axis=0)


def bit_of(axis, bit):
    return (lax.axis_index(axis) >> bit) & 1


def times8(value, rows):
    return pl.multiple_of(value * rows, 8)


def start_kernel(u, v, y, carried, keep, give, low, up):
    levels, _, rank = u.shape
    for j in range(levels):
        carried[j * rank : (j + 1) * rank] = u[j].T
    carried[levels * rank :] = y[...]
    parts = split(carried[...])
    low[...] = dot_split(parts, split(v[0]))
    up[...] = dot_split(parts, split(v[1]))
    shared = 2 * rank
    rest = (carried.shape[0] - shared) // 2
    core = bit_of("gy", 0)
    for out, side in ((keep, core), (give, 1 - core)):
        half = pl.ds(shared + times8(side, rest), rest)
        out[:shared] = low[:shared]
        out[shared : shared + rest] = low[half]
        out[shared + rest : 2 * shared + rest] = up[:shared]
        out[2 * shared + rest :] = up[half]


def lower_node_kernel(bit, top, pieces, z_out, node_out):
    side = bit_of("gy", bit)
    rank = z_out.shape[1]
    ops = slice(top, top + rank)
    z, node = solve_node(
        pieces[side, :top],
        pieces[1 - side, :top],
        pieces[side, ops],
        pieces[1 - side, ops],
        pieces[0, top + rank :] + pieces[1, top + rank :],
    )
    z_out[...] = z
    node_out[...] = node


def lower_leaf_kernel(bit, pair, z_low, out):
    side = bit_of("gy", bit)
    rank = pair.shape[2]
    rest = z_low.shape[0] - rank
    own, sib = pair[side], pair[1 - side]
    out[:rest] = z_low[rank:]
    out[rest:] = solve_own(own[:rank], sib[:rank], own[rank:], sib[rank:])


def advanced(carried, z_low, halves):
    rank = z_low.shape[1]
    rest = halves.shape[1] // 2
    left = carried[:rank]
    next_left = carried[rank : 2 * rank] - kdot(z_low[:rank], left)
    z_rest = jnp.concatenate(
        [
            jnp.concatenate([halves[c, :rest], halves[c, rest:]], axis=1) for c in range(2)
        ],
        axis=0,
    )
    return carried[2 * rank :] - kdot(z_rest, jnp.concatenate([left, next_left], axis=0))


def upper_kernel(shares, carried, z_low, halves, v, new, keep, give, both, sums):
    value = advanced(carried, z_low, halves)
    new[...] = value
    rank = v.shape[1]
    count, width = v.shape[0], value.shape[0]
    parts = split(value)
    both[:width] = dot_split(parts, split(v[0]))
    for j in range(1, count):
        rows = dot_split(parts, split(v[j]))
        both[width + (j - 1) * rank : width + j * rank] = rows[:rank]
        sums[(j - 1) * (width - rank) : j * (width - rank)] = rows[rank:]
    half_both, half_sums = both.shape[0] // 2, sums.shape[0] // 2
    core = bit_of("gy", 0)
    for out, side in ((keep, core), (give, 1 - core)):
        put_rows(out, 0, half_both // shares, 0, both[pl.ds(times8(side, half_both), half_both)])
        put_rows(
            out,
            half_both // shares,
            half_sums // shares,
            0,
            sums[pl.ds(times8(side, half_sums), half_sums)],
        )


def updated(carried, z):
    rank = z.shape[1]
    return carried[rank:] - kdot(z, carried[:rank])


def share_kernel(n_both, pair, out):
    rows = [pair[0, :n_both], pair[1, :n_both], pair[0, n_both:] + pair[1, n_both:]]
    value = jnp.concatenate(rows, axis=0)
    for i in range(out.shape[0]):
        out[i] = value


def joined(mine, other):
    take = bit_of("gy", 0) == 0
    return jnp.concatenate([jnp.where(take, mine, other), jnp.where(take, other, mine)], axis=0)


def put_part(node_out, part):
    n = part.shape[0]
    gy = lax.axis_index("gy")
    part[...] = node_out[pl.ds(times8((gy & 1) * 4 + ((gy >> 1) & 3), n), n)]


def top_node_kernel(bit, width, n_both, n_sums, mine, other, carried, new, node_out, part):
    side = bit_of("gy", bit)
    own, sib, sums = [
        joined(get_rows(mine, base, size), get_rows(other, base, size))
        for base, size in (
            (times8(side, n_both), n_both),
            (times8(1 - side, n_both), n_both),
            (2 * n_both, n_sums),
        )
    ]
    z, node = solve_node(own[:width], sib[:width], own[width:], sib[width:], sums)
    node_out[...] = node
    put_part(node_out, part)
    new[...] = updated(carried, z)


def children_rows(own, sib, count):
    rank = own.shape[1]
    width = own.shape[0] // count
    at = [slice(j * width, j * width + rank) for j in range(1, count)]
    rest = [slice(j * width + rank, (j + 1) * width) for j in range(1, count)]
    return (
        own[:width],
        sib[:width],
        jnp.concatenate([own[s] for s in at], axis=0),
        jnp.concatenate([sib[s] for s in at], axis=0),
        jnp.concatenate([own[s] + sib[s] for s in rest], axis=0),
    )


def halves_node_kernel(count, own, mine, other, carried, new, node_out, part):
    shape = (-1, own.shape[1])
    sib = joined(mine[...].reshape(shape), other[...].reshape(shape))
    z, node = solve_node(*children_rows(own[...], sib, count))
    node_out[...] = node
    put_part(node_out, part)
    new[...] = updated(carried, z)


def upper_node_kernel(count, own, sib, carried, new, node_out, *part):
    z, node = solve_node(*children_rows(own[...], sib[...], count))
    node_out[...] = node
    if part:
        n = part[0].shape[0]
        part[0][...] = node_out[pl.ds(times8(bit_of("gy", 0), n), n)]
    new[...] = updated(carried, z)


def last_kernel(axis, bit, pair, carried, out):
    side = bit_of(axis, bit)
    rank = carried.shape[1]
    own, sib = pair[side], pair[1 - side]
    z = solve_own(own[:rank], sib[:rank], own[rank:], sib[rank:])
    out[...] = updated(carried, z)


def call(kernel, outs, *args, scratch=()):
    rows = sum(a.size // 128 for a in args)
    return pl.pallas_call(
        kernel,
        out_shape=[jax.ShapeDtypeStruct(o, jnp.float32) for o in outs],
        scratch_shapes=[pltpu.VMEM(s, jnp.float32) for s in scratch],
        compiler_params=pltpu.CompilerParams(vmem_limit_bytes=VMEM_BYTES),
        cost_estimate=pl.CostEstimate(
            flops=6 * 128 * 128 * (rows + 14 * 128),
            bytes_accessed=512 * rows,
            transcendentals=0,
        ),
    )(*args)


def bit_groups(count, bits):
    mask = sum(1 << b for b in bits)
    return [
        [
            base | sum(((i >> q) & 1) << b for q, b in enumerate(bits))
            for i in range(1 << len(bits))
        ]
        for base in range(count)
        if not base & mask
    ]


def swap_cores(value):
    return lax.ppermute(value, "gy", [(s, s ^ 1) for s in range(lax.axis_size("gy"))])


def pair_gather(value, axis, bit, tiled=False):
    groups = bit_groups(lax.axis_size(axis), [bit])
    return lax.all_gather(value, axis, axis_index_groups=groups, tiled=tiled)


def exchange(value, axis, bits):
    count = lax.axis_size(axis)
    return lax.all_to_all(value, axis, 0, 0, axis_index_groups=bit_groups(count, bits))


def to_all(value, axis, bits):
    return exchange(jnp.broadcast_to(value, (1 << len(bits),) + value.shape), axis, bits)


def shards(right_sides, factor_u, factor_v):
    levels, _, rank = factor_u.shape
    gx = lax.axis_index("gx")
    near_chips = [1, 2]

    rows = levels * rank + right_sides.shape[1]
    rest = (rows - 2 * rank) // 2
    sent = (4 * rank + 2 * rest, rank)
    carried, keep, give = call(
        start_kernel,
        [(rows, rank), sent, sent],
        factor_u,
        factor_v[:2],
        right_sides.T,
        scratch=[(rows, rank)] * 2,
    )
    pieces = to_all(keep + swap_cores(give), "gy", [1])
    z_low, node = call(
        functools.partial(lower_node_kernel, 1, 2 * rank + rest),
        [(rank + rest, rank), (rank + rest, rank)],
        pieces,
    )
    pair = pair_gather(node, "gy", 2)
    mine = call(functools.partial(lower_leaf_kernel, 2), [(2 * rest, rank)], pair, z_low)[0]
    halves = pair_gather(mine, "gy", 0)

    level = 2
    rows -= level * rank
    count = levels - level
    all_both = rows + (count - 1) * rank
    all_sums = (count - 1) * (rows - rank)
    n_both, n_sums = all_both // 8, all_sums // 8
    sent = (4, n_both + n_sums, rank)
    carried, keep, give = call(
        functools.partial(upper_kernel, 4),
        [(rows, rank), sent, sent],
        carried,
        z_low,
        halves,
        factor_v[level:],
        scratch=[(all_both, rank), (all_sums, rank)],
    )
    piece = exchange(keep + swap_cores(give), "gy", near_chips).sum(axis=0)
    share = call(
        functools.partial(share_kernel, n_both),
        [(4, 2 * n_both + n_sums, rank)],
        pair_gather(piece, "gy", 3),
    )[0]
    mine = exchange(share, "gy", near_chips)
    other = swap_cores(mine)
    carried, node, part = call(
        functools.partial(top_node_kernel, 3, rows, n_both, n_sums),
        [(rows - rank, rank), (all_sums, rank), (all_sums // 8, rank)],
        mine,
        other,
        carried,
    )

    def of_sibling(value, axis, bit):
        pair = pair_gather(value, axis, bit)
        return lax.dynamic_index_in_dim(pair, 1 - bit_of(axis, bit), 0, keepdims=False)

    for axis, bit in (("gy", 4), ("gx", 0), ("gx", 1), ("gx", 2)):
        rows, count = rows - rank, count - 1
        out_rows = (count - 1) * (rows - rank)
        if count > 2:
            mine = to_all(of_sibling(part, axis, bit), "gy", near_chips)
            outs = [(rows - rank, rank), (out_rows, rank)]
            if count > 3:
                carried, node, part = call(
                    functools.partial(halves_node_kernel, count),
                    outs + [(out_rows // 8, rank)],
                    node,
                    mine,
                    swap_cores(mine),
                    carried,
                )
            else:
                near = pair_gather(mine.reshape(-1, rank), "gy", 0, tiled=True)
                carried, node, part = call(
                    functools.partial(upper_node_kernel, count),
                    outs + [(out_rows // 2, rank)],
                    node,
                    near,
                    carried,
                )
        else:
            near = pair_gather(of_sibling(part, axis, bit), "gy", 0, tiled=True)
            carried, node = call(
                functools.partial(upper_node_kernel, count),
                [(rows - rank, rank), (out_rows, rank)],
                node,
                near,
                carried,
            )
    pair = pair_gather(node, "gx", 3)
    shape = right_sides.shape[::-1]
    return call(functools.partial(last_kernel, "gx", 3), [shape], pair, carried)[0].T


def solution(mesh):
    placed = (P(("gx", "gy"), None), P(None, ("gx", "gy"), None), P(None, ("gx", "gy"), None))
    return jax.shard_map(
        shards, mesh=mesh, in_specs=placed, out_specs=P(("gx", "gy"), None), check_vma=False
    )
```

```python
import functools

import jax
import jax.numpy as jnp
from jax import lax
from jax.experimental import pallas as pl
from jax.experimental.pallas import tpu as pltpu
from jax.sharding import PartitionSpec as P

VMEM_BYTES = 40 * 2**20


def split(value):
    high = value.astype(jnp.bfloat16)
    low = (value - high.astype(jnp.float32)).astype(jnp.bfloat16)
    return high, low


def dot_split(a, b):
    def part(x, y):
        return jnp.dot(x, y, preferred_element_type=jnp.float32)

    return part(a[0], b[0]) + (part(a[0], b[1]) + part(a[1], b[0]))


def kdot(a, b):
    return dot_split(split(a), split(b))


def inverse_of(error):
    total = jnp.eye(error.shape[0], dtype=jnp.float32) + error
    power = error
    for step in range(6):
        parts = split(power)
        power = dot_split(parts, parts)
        total = total + kdot(total, power)
    return total


def solve_own(gram_own, gram_sib, proj_own, proj_sib):
    inverse = inverse_of(kdot(gram_own, gram_sib))
    return kdot(proj_sib - kdot(proj_own, gram_sib), inverse)


def solve_node(own, sib, ops_own, ops_sib, sums):
    rank = own.shape[1]
    width = own.shape[0] - rank
    gram_own, proj_own = own[:rank], own[rank:]
    z = solve_own(gram_own, sib[:rank], proj_own, sib[rank:])
    z_sib = proj_own - kdot(z, gram_own)
    z_both = split(jnp.concatenate([z, z_sib], axis=1))
    node = []
    for j in range(ops_own.shape[0] // rank):
        at = slice(j * rank, (j + 1) * rank)
        left = split(jnp.concatenate([ops_own[at], ops_sib[at]], axis=0))
        node.append(sums[j * width : (j + 1) * width] - dot_split(z_both, left))
    return z, jnp.concatenate(node, axis=0)


def put_rows(out, base, size, start, value):
    at, rows = 0, value.shape[0]
    while at < rows:
        i, r = divmod(start + at, size)
        n = min(size - r, rows - at)
        out[i, base + r : base + r + n] = value[at : at + n]
        at += n


def get_rows(ref, base, size):
    return jnp.concatenate([ref[i, pl.ds(base, size)] for i in range(ref.shape[0])], axis=0)


def bit_of(axis, bit):
    return (lax.axis_index(axis) >> bit) & 1


def times8(value, rows):
    return pl.multiple_of(value * rows, 8)


def pack_kernel(u, v, y, pack):
    levels, _, rank = u.shape
    first = levels * rank + y.shape[0]
    for j in range(levels):
        pack[j * rank : (j + 1) * rank] = u[j].T
        pack[first + j * rank : first + (j + 1) * rank] = v[j]
    pack[levels * rank : first] = y[...]


def first_pair_kernel(levels, mine, other, held, sent, next_v, top_v):
    rank = mine.shape[1]
    half = rank // 2
    core = bit_of("gy", 0)
    first = mine.shape[0] - levels * rank
    last = first - levels * rank
    held[: 2 * rank, :rank] = mine[: 2 * rank]
    held[: 2 * rank, rank:] = other[: 2 * rank]
    for j in range(2, levels + 1):
        n = half if j < levels else last // 2
        at = pl.ds(j * rank + times8(core, n), n)
        to = slice(2 * rank + (j - 2) * half, 2 * rank + (j - 2) * half + n)
        held[to, :rank] = mine[at]
        held[to, rank:] = other[at]
    factors = [
        jnp.concatenate(
            [ref[first + j * rank : first + (j + 1) * rank] for ref in (mine, other)], axis=0
        )
        for j in range(levels)
    ]
    parts = split(held[...])
    rows = held.shape[0]
    for j in range(2):
        value = dot_split(parts, split(factors[j]))
        sent[0, j * rows : (j + 1) * rows] = value
        sent[1, j * rows : (j + 1) * rows] = value
    for j in range(2, 4):
        next_v[j - 2] = factors[j]
    for j in range(4, levels):
        top_v[j - 4] = factors[j]


def lower_node_kernel(bit, n_both, rest, pieces, z_out, node_out):
    side = bit_of("gy", bit)
    rank = z_out.shape[1]
    top = 2 * rank + rest
    if n_both is None:
        own = pieces[side, :top]
        sib = pieces[1 - side, :top]
        ops_own = pieces[side, top : top + rank]
        ops_sib = pieces[1 - side, top : top + rank]
        sums = pieces[0, top + rank :] + pieces[1, top + rank :]
    else:
        own = get_rows(pieces, times8(side, n_both), n_both)
        sib = get_rows(pieces, times8(1 - side, n_both), n_both)
        own, ops_own = own[:top], own[top:]
        sib, ops_sib = sib[:top], sib[top:]
        sums = get_rows(pieces, 2 * n_both, pieces.shape[1] - 2 * n_both)
    z, node = solve_node(own, sib, ops_own, ops_sib, sums)
    z_out[...] = z
    node_out[...] = node


def after_pair(bit, pair, z_low, held):
    side = bit_of("gy", bit)
    rank = pair.shape[2]
    own, sib = pair[side], pair[1 - side]
    z_up = solve_own(own[:rank], sib[:rank], own[rank:], sib[rank:])
    left = held[:rank]
    next_left = held[rank : 2 * rank] - kdot(z_low[:rank], left)
    z_both = jnp.concatenate([z_low[rank:], z_up], axis=1)
    return held[2 * rank :] - kdot(z_both, jnp.concatenate([left, next_left], axis=0))


def between_kernel(bit, pair, z_low, held, rest, halves):
    value = after_pair(bit, pair, z_low, held)
    rest[...] = value
    halves[...] = value[: halves.shape[0]]


def second_pair_kernel(shares, rest, gathered, v, held, sent):
    rank = v.shape[2]
    half = rank // 2
    core = bit_of("gy", 0)
    parts = []
    for c in range(2):
        value = gathered[c]
        turned = jnp.concatenate([value[:, rank:], value[:, :rank]], axis=1)
        parts.append(jnp.where(core == c, value, turned))
    for j in range(2):
        for c in range(2):
            at = j * rank + c * half
            held[at : at + half] = parts[c][j * half : (j + 1) * half]
    held[2 * rank :] = rest[rank:]
    rows = held.shape[0]
    value = split(held[...])
    low = dot_split(value, split(v[0]))
    up = dot_split(value, split(v[1]))
    n_both = (rows + rank) // shares
    put_rows(sent, 0, n_both, 0, low)
    put_rows(sent, 0, n_both, rows, up[:rank])
    put_rows(sent, n_both, (rows - rank) // shares, 0, up[rank:])


def upper_kernel(bit, shares, pair, z_low, held, v, mine, other, sent):
    value = after_pair(bit, pair, z_low, held)
    rank = v.shape[2]
    half = rank // 2
    mine[...] = value[:, :rank]
    other[...] = value[:, rank:]
    count, width = v.shape[0], value.shape[0]
    n_both = (width + (count - 1) * half) // shares
    n_sums = (count - 1) * (width - half) // shares
    parts = split(value)
    put_rows(sent, 0, n_both, 0, dot_split(parts, split(v[0])))
    for j in range(1, count):
        rows = dot_split(parts, split(v[j]))
        put_rows(sent, 0, n_both, width + (j - 1) * half, rows[:half])
        put_rows(sent, n_both, n_sums, (j - 1) * (width - half), rows[half:])


def share_kernel(n_both, pair, out):
    rows = [pair[0, :n_both], pair[1, :n_both], pair[0, n_both:] + pair[1, n_both:]]
    value = jnp.concatenate(rows, axis=0)
    for i in range(out.shape[0]):
        out[i] = value


def interleaved(first, second, block):
    out, at, rows = [], 0, first.shape[0]
    while at < rows:
        n = min(block, rows - at)
        out += [first[at : at + n], second[at : at + n]]
        at += n
    return jnp.concatenate(out, axis=0)


def updated(carried, z):
    rank = z.shape[1]
    return carried[rank:] - kdot(z, carried[:rank])


def top_node_kernel(count, n_both, n_sums, gathered, swapped, held, new, node_out, quarter):
    rank = held.shape[1]
    half = rank // 2
    width = held.shape[0]
    core = bit_of("gy", 0)
    side = bit_of("gx", 0)
    shares, size = gathered.shape[0], gathered.shape[1]

    def rows_of(base, n):
        here = get_rows(gathered, base, n)
        there = jnp.concatenate(
            [swapped[pl.ds(pl.multiple_of(i * size + base, 8), n)] for i in range(shares)], axis=0
        )
        return jnp.where(core == 0, here, there), jnp.where(core == 0, there, here)

    def child(which):
        first, second = rows_of(times8(which, n_both), n_both)
        ops = interleaved(first[width:], second[width:], half)
        return interleaved(first[:width], second[:width], half), ops

    own, ops_own = child(side)
    sib, ops_sib = child(1 - side)
    first, second = rows_of(2 * n_both, n_sums)
    w = width - half
    sums = jnp.concatenate(
        [
            interleaved(first[j * w : (j + 1) * w], second[j * w : (j + 1) * w], half)
            for j in range(count - 1)
        ],
        axis=0,
    )
    z, node = solve_node(own, sib, ops_own, ops_sib, sums)
    node_out[...] = node
    n = quarter.shape[0]
    quarter[...] = node_out[pl.ds(times8(lax.axis_index("gy") & 3, n), n)]
    here, there = held[...], swapped[shares * size :]
    carried = interleaved(
        jnp.where(core == 0, here, there), jnp.where(core == 0, there, here), half
    )
    new[...] = updated(carried, z)


def children_rows(own, sib, count):
    rank = own.shape[1]
    width = own.shape[0] // count
    at = [slice(j * width, j * width + rank) for j in range(1, count)]
    rest = [slice(j * width + rank, (j + 1) * width) for j in range(1, count)]
    return (
        own[:width],
        sib[:width],
        jnp.concatenate([own[s] for s in at], axis=0),
        jnp.concatenate([sib[s] for s in at], axis=0),
        jnp.concatenate([own[s] + sib[s] for s in rest], axis=0),
    )


def upper_node_kernel(count, bit, own, sib, carried, new, node_out):
    value = sib[...] if bit is None else sib[1 - bit_of("gx", bit)]
    z, node = solve_node(*children_rows(own[...], value, count))
    node_out[...] = node
    new[...] = updated(carried, z)


def last_kernel(axis, bit, pair, carried, out):
    side = bit_of(axis, bit)
    rank = carried.shape[1]
    own, sib = pair[side], pair[1 - side]
    z = solve_own(own[:rank], sib[:rank], own[rank:], sib[rank:])
    out[...] = updated(carried, z)


def call(kernel, outs, *args, scratch=()):
    rows = sum(a.size // 128 for a in args)
    return pl.pallas_call(
        kernel,
        out_shape=[jax.ShapeDtypeStruct(o, jnp.float32) for o in outs],
        scratch_shapes=[pltpu.VMEM(s, jnp.float32) for s in scratch],
        compiler_params=pltpu.CompilerParams(vmem_limit_bytes=VMEM_BYTES),
        cost_estimate=pl.CostEstimate(
            flops=6 * 128 * 128 * (rows + 14 * 128),
            bytes_accessed=512 * rows,
            transcendentals=0,
        ),
    )(*args)


def bit_groups(count, bits):
    mask = sum(1 << b for b in bits)
    return [
        [
            base | sum(((i >> q) & 1) << b for q, b in enumerate(bits))
            for i in range(1 << len(bits))
        ]
        for base in range(count)
        if not base & mask
    ]


def swap_cores(value):
    return lax.ppermute(value, "gy", [(s, s ^ 1) for s in range(lax.axis_size("gy"))])


def pair_gather(value, axis, bit, tiled=False):
    groups = bit_groups(lax.axis_size(axis), [bit])
    return lax.all_gather(value, axis, axis_index_groups=groups, tiled=tiled)


def exchange(value, axis, bits):
    count = lax.axis_size(axis)
    return lax.all_to_all(value, axis, 0, 0, axis_index_groups=bit_groups(count, bits))


def to_all(value, axis, bits):
    return exchange(jnp.broadcast_to(value, (1 << len(bits),) + value.shape), axis, bits)


def pad_rows(value, rows):
    return jnp.pad(value, ((0, rows - value.shape[0]), (0, 0)))


def up8(value):
    return -(-value // 8) * 8


def shards(right_sides, factor_u, factor_v):
    levels, _, rank = factor_u.shape
    half = rank // 2
    near_chips = [1, 2]

    all_rows = levels * rank + right_sides.shape[1]
    pack = call(
        pack_kernel,
        [(all_rows + levels * rank, rank)],
        factor_u,
        factor_v,
        right_sides.T,
    )[0]
    rest = (all_rows - 2 * rank) // 2
    rows = 2 * rank + rest
    held, sent, next_v, top_v = call(
        functools.partial(first_pair_kernel, levels),
        [
            (rows, 2 * rank),
            (2, 2 * rows, rank),
            (2, 2 * rank, rank),
            (levels - 4, 2 * rank, rank),
        ],
        pack,
        swap_cores(pack),
    )
    z_low, node = call(
        functools.partial(lower_node_kernel, 1, None, rest),
        [(rank + rest, rank), (rank + rest, rank)],
        exchange(sent, "gy", [1]),
    )
    own_rest, halves = call(
        functools.partial(between_kernel, 2),
        [(rest, 2 * rank), (rank, 2 * rank)],
        pair_gather(node, "gy", 2),
        z_low,
        held,
    )

    rest -= rank
    rows = 2 * rank + rest
    n_both, n_sums = (rows + rank) // 4, (rows - rank) // 4
    held, sent = call(
        functools.partial(second_pair_kernel, 4),
        [(rows, 2 * rank), (4, n_both + n_sums, rank)],
        own_rest,
        pair_gather(halves, "gy", 0),
        next_v,
    )
    piece = exchange(sent, "gy", near_chips).sum(axis=0)
    share = call(
        functools.partial(share_kernel, n_both),
        [(4, 2 * n_both + n_sums, rank)],
        pair_gather(piece, "gy", 3),
    )[0]
    z_low, node = call(
        functools.partial(lower_node_kernel, 3, n_both, rest),
        [(rank + rest, rank), (rank + rest, rank)],
        exchange(share, "gy", near_chips),
    )

    count = levels - 4
    n_both = (rest + (count - 1) * half) // 4
    n_sums = (count - 1) * (rest - half) // 4
    mine, other, sent = call(
        functools.partial(upper_kernel, 4, 4),
        [(rest, rank), (rest, rank), (4, n_both + n_sums, rank)],
        pair_gather(node, "gy", 4),
        z_low,
        held,
        top_v,
    )
    piece = exchange(sent, "gy", near_chips).sum(axis=0)
    s_both, s_sums = up8(-(-n_both // 8)), up8(-(-n_sums // 8))
    sent = jnp.concatenate(
        [
            pad_rows(piece[:n_both], 8 * s_both).reshape(8, s_both, rank),
            pad_rows(piece[n_both:], 8 * s_sums).reshape(8, s_sums, rank),
        ],
        axis=1,
    )
    far = [3, 4, 5]
    sides = exchange(sent, ("gx", "gy"), far)
    sides = sides.reshape((2, 4) + sides.shape[1:]).sum(axis=1)
    share = jnp.concatenate(
        [sides[0, :s_both], sides[1, :s_both], sides[0, s_both:] + sides[1, s_both:]], axis=0
    )
    pieces = to_all(share, ("gx", "gy"), far)
    share = jnp.concatenate(
        [
            pieces[:, :s_both].reshape(-1, rank)[:n_both],
            pieces[:, s_both : 2 * s_both].reshape(-1, rank)[:n_both],
            pieces[:, 2 * s_both :].reshape(-1, rank)[:n_sums],
        ],
        axis=0,
    )
    gathered = to_all(share, "gy", near_chips)
    swapped = swap_cores(jnp.concatenate([gathered.reshape(-1, rank), other], axis=0))
    rows = 2 * rest
    out_rows = (count - 1) * (rows - rank)
    carried, node, part = call(
        functools.partial(top_node_kernel, count, n_both, n_sums),
        [(rows - rank, rank), (out_rows, rank), (out_rows // 4, rank)],
        gathered,
        swapped,
        mine,
    )

    pair = pair_gather(part, "gx", 1)
    part = lax.dynamic_index_in_dim(pair, 1 - bit_of("gx", 1), 0, keepdims=False)
    quads = bit_groups(lax.axis_size("gy"), [0, 1])
    near = lax.all_gather(part, "gy", axis_index_groups=quads, tiled=True)
    for bit in (None, 2):
        rows, count = rows - rank, count - 1
        carried, node = call(
            functools.partial(upper_node_kernel, count, bit),
            [(rows - rank, rank), ((count - 1) * (rows - rank), rank)],
            node,
            near,
            carried,
        )
        near = pair_gather(node, "gx", 2 if bit is None else 3)
    shape = right_sides.shape[::-1]
    return call(functools.partial(last_kernel, "gx", 3), [shape], near, carried)[0].T


def solution(mesh):
    placed = (P(("gx", "gy"), None), P(None, ("gx", "gy"), None), P(None, ("gx", "gy"), None))
    return jax.shard_map(
        shards, mesh=mesh, in_specs=placed, out_specs=P(("gx", "gy"), None), check_vma=False
    )
```

```python
import functools

import jax
import jax.numpy as jnp
from jax import lax
from jax.experimental import pallas as pl
from jax.experimental.pallas import tpu as pltpu
from jax.sharding import PartitionSpec as P

VMEM_BYTES = 40 * 2**20
ALL_VMEM_BYTES = 62_000_000


def split(value):
    high = value.astype(jnp.bfloat16)
    low = (value - high.astype(jnp.float32)).astype(jnp.bfloat16)
    return high, low


def dot_split(a, b):
    def part(x, y):
        return jnp.dot(x, y, preferred_element_type=jnp.float32)

    return part(a[0], b[0]) + (part(a[0], b[1]) + part(a[1], b[0]))


def kdot(a, b):
    return dot_split(split(a), split(b))


def solve_own(gram_own, gram_sib, proj_own, proj_sib):
    power = kdot(gram_own, gram_sib)
    right = proj_sib - kdot(proj_own, gram_sib)
    total = jnp.eye(power.shape[0], dtype=jnp.float32) + power
    for step in range(5):
        parts = split(power)
        power = dot_split(parts, parts)
        total = total + kdot(total, power)
    parts = split(power)
    power = dot_split(parts, parts)
    right = kdot(right, total)
    return right + kdot(right, power)


def solve_node(own, sib, ops_own, ops_sib, sums):
    rank = own.shape[1]
    width = own.shape[0] - rank
    gram_own, proj_own = own[:rank], own[rank:]
    z = solve_own(gram_own, sib[:rank], proj_own, sib[rank:])
    z_sib = proj_own - kdot(z, gram_own)
    z_both = split(jnp.concatenate([z, z_sib], axis=1))
    node = []
    for j in range(ops_own.shape[0] // rank):
        at = slice(j * rank, (j + 1) * rank)
        left = split(jnp.concatenate([ops_own[at], ops_sib[at]], axis=0))
        node.append(sums[j * width : (j + 1) * width] - dot_split(z_both, left))
    return z, jnp.concatenate(node, axis=0)


def put_rows(out, base, size, start, value):
    at, rows = 0, value.shape[0]
    while at < rows:
        i, r = divmod(start + at, size)
        n = min(size - r, rows - at)
        out[i, base + r : base + r + n] = value[at : at + n]
        at += n


def get_rows(ref, base, size):
    return jnp.concatenate([ref[i, pl.ds(base, size)] for i in range(ref.shape[0])], axis=0)


def bit_of(axis, bit):
    return (lax.axis_index(axis) >> bit) & 1


def times8(value, rows):
    return pl.multiple_of(value * rows, 8)


def pack_kernel(u, v, y, pack, u_held, sems):
    levels, _, rank = u.shape
    first = levels * rank + y.shape[0]
    copies = [pltpu.make_async_copy(u.at[j], u_held.at[j], sems.at[j]) for j in range(levels)]
    copies.append(
        pltpu.make_async_copy(y, pack.at[pl.ds(levels * rank, y.shape[0])], sems.at[levels])
    )
    for j in range(levels):
        rows = pl.ds(first + j * rank, rank)
        copies.append(pltpu.make_async_copy(v.at[j], pack.at[rows], sems.at[levels + 1 + j]))
    for copy in copies:
        copy.start()
    for j in range(levels):
        copies[j].wait()
        pack[j * rank : (j + 1) * rank] = u_held[j].T
    for copy in copies[levels:]:
        copy.wait()


def first_pair_kernel(levels, mine, other, held, sent, next_v, top_v):
    rank = mine.shape[1]
    half = rank // 2
    core = bit_of("gy", 0)
    first = mine.shape[0] - levels * rank
    last = first - levels * rank
    held[: 2 * rank, :rank] = mine[: 2 * rank]
    held[: 2 * rank, rank:] = other[: 2 * rank]
    for j in range(2, levels + 1):
        n = half if j < levels else last // 2
        at = pl.ds(j * rank + times8(core, n), n)
        to = slice(2 * rank + (j - 2) * half, 2 * rank + (j - 2) * half + n)
        held[to, :rank] = mine[at]
        held[to, rank:] = other[at]
    factors = [
        jnp.concatenate(
            [ref[first + j * rank : first + (j + 1) * rank] for ref in (mine, other)], axis=0
        )
        for j in range(levels)
    ]
    parts = split(held[...])
    rows = held.shape[0]
    for j in range(2):
        value = dot_split(parts, split(factors[j]))
        sent[0, j * rows : (j + 1) * rows] = value
        sent[1, j * rows : (j + 1) * rows] = value
    for j in range(2, 4):
        next_v[j - 2] = factors[j]
    for j in range(4, levels):
        top_v[j - 4] = factors[j]


def first_node_kernel(bit, top, pieces, z_out, node_out):
    side = bit_of("gy", bit)
    rank = z_out.shape[1]
    ops = slice(top, top + rank)
    z, node = solve_node(
        pieces[side, :top],
        pieces[1 - side, :top],
        pieces[side, ops],
        pieces[1 - side, ops],
        pieces[0, top + rank :] + pieces[1, top + rank :],
    )
    z_out[...] = z
    node_out[...] = node


def after_pair(bit, pair, z_low, held):
    side = bit_of("gy", bit)
    rank = pair.shape[2]
    own, sib = pair[side], pair[1 - side]
    z_up = solve_own(own[:rank], sib[:rank], own[rank:], sib[rank:])
    left = held[:rank]
    next_left = held[rank : 2 * rank] - kdot(z_low[:rank], left)
    z_both = jnp.concatenate([z_low[rank:], z_up], axis=1)
    return held[2 * rank :] - kdot(z_both, jnp.concatenate([left, next_left], axis=0))


def between_kernel(bit, shares, pair, z_low, held, v, rest, sent):
    value = after_pair(bit, pair, z_low, held)
    rest[...] = value
    rows = value.shape[0]
    half = v.shape[2] // 2
    parts = split(value)
    low = dot_split(parts, split(v[0]))
    up = dot_split(parts, split(v[1]))
    n_both = (rows + half) // shares
    put_rows(sent, 0, n_both, 0, low)
    put_rows(sent, 0, n_both, rows, up[:half])
    put_rows(sent, n_both, (rows - half) // shares, 0, up[half:])


def second_shared_kernel(n_both, n_sums, rows, pieces, rest, out):
    rank = out.shape[1]
    half = rank // 2
    for c in range(2):
        both = get_rows(pieces, c * n_both, n_both)
        out[3 * half * c : 3 * half * c + rank] = both[:rank]
        out[3 * half * c + rank : 3 * half * (c + 1)] = both[rows:]
    out[6 * half : 7 * half] = get_rows(pieces, 2 * n_both, n_sums)[:half]
    out[7 * half : 9 * half] = rest[:rank, :rank]
    out[9 * half : 11 * half] = rest[:rank, rank:]


def both_cores(ref, at, n):
    return [ref[c, pl.ds(at, n)] for c in range(2)]


def full_rows(ref, at, n):
    return jnp.concatenate(both_cores(ref, at, n), axis=0)


def second_node_kernel(bit, n_both, n_sums, rows, pieces, shared, z_out, node_out):
    side = bit_of("gy", bit)
    rank = z_out.shape[1]
    half = rank // 2
    children = []
    for which in (side, 1 - side):
        at = times8(which, 3 * half)
        both = get_rows(pieces, times8(which, n_both), n_both)
        children.append(
            (
                jnp.concatenate(
                    [
                        full_rows(shared, at, half),
                        full_rows(shared, at + half, half),
                        both[rank:rows],
                    ],
                    axis=0,
                ),
                full_rows(shared, at + rank, half),
            )
        )
    (own, ops_own), (sib, ops_sib) = children
    sums = get_rows(pieces, 2 * n_both, n_sums)
    sums = jnp.concatenate([full_rows(shared, 6 * half, half), sums[half:]], axis=0)
    z, node = solve_node(own, sib, ops_own, ops_sib, sums)
    z_out[...] = z
    node_out[...] = node


def upper_kernel(bit, shares, pair, z_low, shared, rest, v, mine, other, sent):
    rank = v.shape[2]
    half = rank // 2
    core = bit_of("gy", 0)
    factors = []
    for c in range(2):
        a, b = shared[c, 7 * half : 9 * half], shared[c, 9 * half : 11 * half]
        here = core == c
        factors.append(
            jnp.concatenate([jnp.where(here, a, b), jnp.where(here, b, a)], axis=1)
        )
    held = jnp.concatenate(
        [factors[0][:half], factors[1][:half], factors[0][half:], factors[1][half:], rest[rank:]],
        axis=0,
    )
    value = after_pair(bit, pair, z_low, held)
    mine[...] = value[:, :rank]
    other[...] = value[:, rank:]
    count, width = v.shape[0], value.shape[0]
    n_both = (width + (count - 1) * half) // shares
    n_sums = (count - 1) * (width - half) // shares
    parts = split(value)
    put_rows(sent, 0, n_both, 0, dot_split(parts, split(v[0])))
    for j in range(1, count):
        rows = dot_split(parts, split(v[j]))
        put_rows(sent, 0, n_both, width + (j - 1) * half, rows[:half])
        put_rows(sent, n_both, n_sums, (j - 1) * (width - half), rows[half:])


def share_kernel(n_both, pair, out):
    rows = [pair[0, :n_both], pair[1, :n_both], pair[0, n_both:] + pair[1, n_both:]]
    value = jnp.concatenate(rows, axis=0)
    for i in range(out.shape[0]):
        out[i] = value


def interleaved(first, second, block):
    out, at, rows = [], 0, first.shape[0]
    while at < rows:
        n = min(block, rows - at)
        out += [first[at : at + n], second[at : at + n]]
        at += n
    return jnp.concatenate(out, axis=0)


def updated(carried, z):
    rank = z.shape[1]
    return carried[rank:] - kdot(z, carried[:rank])


def top_shared_kernel(n_both, width, gathered, other, out):
    half = out.shape[1] // 2
    n = half + 4 * n_both - width
    for c in range(2):
        both = get_rows(gathered, c * n_both, n_both)
        out[n * c : n * c + half] = both[:half]
        out[n * c + half : n * (c + 1)] = both[width:]
    out[2 * n :] = other[...]


def child_rows(shared, at, half, count, projections):
    own = jnp.concatenate([full_rows(shared, at, half), projections], axis=0)
    ops = [full_rows(shared, at + half * j, half) for j in range(1, count)]
    return own, jnp.concatenate(ops, axis=0)


def top_node_kernel(count, n_both, n_sums, gathered, shared, held, z_out, node_out, part, carried):
    rank = held.shape[1]
    half = rank // 2
    width = held.shape[0]
    core = bit_of("gy", 0)
    side = bit_of("gx", 0)
    children = []
    for which in (side, 1 - side):
        both = get_rows(gathered, times8(which, n_both), n_both)
        at = times8(which, half * count)
        children.append(child_rows(shared, at, half, count, both[half:width]))
    (own, ops_own), (sib, ops_sib) = children
    sums = get_rows(gathered, 2 * n_both, n_sums)
    z, node = solve_node(own, sib, ops_own, ops_sib, sums)
    z_out[...] = z
    node_out[...] = node
    n = part.shape[0]
    part[...] = node_out[pl.ds(times8((lax.axis_index("gy") >> 1) & 3, n), n)]
    swapped = [shared[c, 2 * half * count :] for c in range(2)]
    halves = [jnp.where(core == c, held[...], swapped[c]) for c in range(2)]
    carried[...] = interleaved(halves[0], halves[1], half)


def sibling_kernel(bit, pair, out):
    value = pair[1 - bit_of("gx", bit)]
    for i in range(out.shape[0]):
        out[i] = value


def upper_shared_kernel(count, bit, own, sib, out):
    half = out.shape[1] // 2
    width = own.shape[0] // count
    value = sib[...].reshape(own.shape) if bit is None else sib[1 - bit_of("gx", bit)]
    for j in range(count):
        at = slice(j * width, j * width + half)
        out[j * half : (j + 1) * half] = own[at]
        out[(count + j) * half : (count + j + 1) * half] = value[at]


def upper_node_kernel(count, bit, own, sib, shared, z_out, node_out):
    half = own.shape[1] // 2
    width = own.shape[0] // count
    here = own[...]
    there = sib[...].reshape(own.shape) if bit is None else sib[1 - bit_of("gx", bit)]
    rows_own, ops_own = child_rows(shared, 0, half, count, here[half:width])
    rows_sib, ops_sib = child_rows(shared, half * count, half, count, there[half:width])
    sums = jnp.concatenate(
        [
            here[j * width + half : (j + 1) * width] + there[j * width + half : (j + 1) * width]
            for j in range(1, count)
        ],
        axis=0,
    )
    z, node = solve_node(rows_own, rows_sib, ops_own, ops_sib, sums)
    z_out[...] = z
    node_out[...] = node


def last_kernel(bit, sizes, gathered, carried, out):
    rank = carried.shape[1]
    half = rank // 2
    side = bit_of("gx", bit)
    n = half + out.shape[0] // 2

    def child(which):
        return interleaved(*both_cores(gathered, times8(which, n), n), half)

    value, at = carried[...], 2 * n
    for size in sizes:
        value = updated(value, interleaved(*both_cores(gathered, at, size), half))
        at += size
    own, sib = child(side), child(1 - side)
    z = solve_own(own[:rank], sib[:rank], own[rank:], sib[rank:])
    out[...] = updated(value, z)


def call(kernel, outs, *args, vmem_bytes=VMEM_BYTES, **options):
    rows = sum(a.size // 128 for a in args)
    return pl.pallas_call(
        kernel,
        out_shape=[jax.ShapeDtypeStruct(o, jnp.float32) for o in outs],
        compiler_params=pltpu.CompilerParams(vmem_limit_bytes=vmem_bytes),
        cost_estimate=pl.CostEstimate(
            flops=6 * 128 * 128 * (rows + 14 * 128),
            bytes_accessed=512 * rows,
            transcendentals=0,
        ),
        **options,
    )(*args)


def bit_groups(count, bits):
    mask = sum(1 << b for b in bits)
    return [
        [
            base | sum(((i >> q) & 1) << b for q, b in enumerate(bits))
            for i in range(1 << len(bits))
        ]
        for base in range(count)
        if not base & mask
    ]


def swap_cores(value):
    return lax.ppermute(value, "gy", [(s, s ^ 1) for s in range(lax.axis_size("gy"))])


def pair_gather(value, axis, bit, tiled=False):
    groups = bit_groups(lax.axis_size(axis), [bit])
    return lax.all_gather(value, axis, axis_index_groups=groups, tiled=tiled)


def exchange(value, axis, bits):
    count = lax.axis_size(axis)
    return lax.all_to_all(value, axis, 0, 0, axis_index_groups=bit_groups(count, bits))


def to_all(value, axis, bits):
    return exchange(jnp.broadcast_to(value, (1 << len(bits),) + value.shape), axis, bits)


def pad_rows(value, rows):
    return jnp.pad(value, ((0, rows - value.shape[0]), (0, 0)))


def up8(value):
    return -(-value // 8) * 8


def shards(right_sides, factor_u, factor_v):
    levels, _, rank = factor_u.shape
    half = rank // 2
    near_chips = [1, 2]

    all_rows = levels * rank + right_sides.shape[1]
    pack = call(
        pack_kernel,
        [(all_rows + levels * rank, rank)],
        factor_u,
        factor_v,
        right_sides.T,
        vmem_bytes=ALL_VMEM_BYTES,
        in_specs=[pl.BlockSpec(memory_space=pltpu.HBM)] * 3,
        scratch_shapes=[
            pltpu.VMEM(factor_u.shape, jnp.float32),
            pltpu.SemaphoreType.DMA((2 * levels + 1,)),
        ],
    )[0]
    rest = (all_rows - 2 * rank) // 2
    rows = 2 * rank + rest
    held, sent, next_v, top_v = call(
        functools.partial(first_pair_kernel, levels),
        [
            (rows, 2 * rank),
            (2, 2 * rows, rank),
            (2, 2 * rank, rank),
            (levels - 4, 2 * rank, rank),
        ],
        pack,
        swap_cores(pack),
    )
    z_low, node = call(
        functools.partial(first_node_kernel, 1, rows),
        [(rank + rest, rank), (rank + rest, rank)],
        exchange(sent, "gy", [1]),
    )

    rows = rest
    rest -= rank
    n_both, n_sums = (rows + half) // 4, (rows - half) // 4
    held, sent = call(
        functools.partial(between_kernel, 2, 4),
        [(rows, 2 * rank), (4, n_both + n_sums, rank)],
        pair_gather(node, "gy", 2),
        z_low,
        held,
        next_v,
    )
    piece = exchange(sent, "gy", near_chips).sum(axis=0)
    share = call(
        functools.partial(share_kernel, n_both),
        [(4, 2 * n_both + n_sums, rank)],
        pair_gather(piece, "gy", 3),
    )[0]
    pieces = exchange(share, "gy", near_chips)
    shared = call(
        functools.partial(second_shared_kernel, n_both, n_sums, rows),
        [(11 * half, rank)],
        pieces,
        held,
    )[0]
    shared = pair_gather(shared, "gy", 0)
    z_low, node = call(
        functools.partial(second_node_kernel, 3, n_both, n_sums, rows),
        [(rank + rest, rank), (rank + rest, rank)],
        pieces,
        shared,
    )

    count = levels - 4
    n_both = (rest + (count - 1) * half) // 4
    n_sums = (count - 1) * (rest - half) // 4
    mine, other, sent = call(
        functools.partial(upper_kernel, 4, 4),
        [(rest, rank), (rest, rank), (4, n_both + n_sums, rank)],
        pair_gather(node, "gy", 4),
        z_low,
        shared,
        held,
        top_v,
    )
    piece = exchange(sent, "gy", near_chips).sum(axis=0)
    s_both, s_sums = up8(-(-n_both // 8)), up8(-(-n_sums // 8))
    sent = jnp.concatenate(
        [
            pad_rows(piece[:n_both], 8 * s_both).reshape(8, s_both, rank),
            pad_rows(piece[n_both:], 8 * s_sums).reshape(8, s_sums, rank),
        ],
        axis=1,
    )
    far = [3, 4, 5]
    sides = exchange(sent, ("gx", "gy"), far)
    sides = sides.reshape((2, 4) + sides.shape[1:]).sum(axis=1)
    share = jnp.concatenate(
        [sides[0, :s_both], sides[1, :s_both], sides[0, s_both:] + sides[1, s_both:]], axis=0
    )
    pieces = to_all(share, ("gx", "gy"), far)
    share = jnp.concatenate(
        [
            pieces[:, :s_both].reshape(-1, rank)[:n_both],
            pieces[:, s_both : 2 * s_both].reshape(-1, rank)[:n_both],
            pieces[:, 2 * s_both :].reshape(-1, rank)[:n_sums],
        ],
        axis=0,
    )
    gathered = to_all(share, "gy", near_chips)
    shared = call(
        functools.partial(top_shared_kernel, n_both, rest),
        [(2 * count * half + rest, rank)],
        gathered,
        other,
    )[0]
    width = rest - half
    z, node, part, carried = call(
        functools.partial(top_node_kernel, count, n_both, n_sums),
        [
            (width, rank),
            ((count - 1) * width, rank),
            ((count - 1) * width // 4, rank),
            (2 * rest, rank),
        ],
        gathered,
        pair_gather(shared, "gy", 0),
        mine,
    )
    solved = [z]

    for bit in (1, 2):
        count -= 1
        pair = pair_gather(part, "gx", bit)
        if bit == 1:
            near = call(functools.partial(sibling_kernel, bit), [(4,) + part.shape], pair)[0]
            near, pick = exchange(near, "gy", near_chips), None
        else:
            near, pick = pair, bit
        shared = call(
            functools.partial(upper_shared_kernel, count, pick),
            [(2 * count * half, rank)],
            node,
            near,
        )[0]
        width -= half
        z, node = call(
            functools.partial(upper_node_kernel, count, pick),
            [(width, rank), ((count - 1) * width, rank)],
            node,
            near,
            pair_gather(shared, "gy", 0),
        )
        part = node
        solved.append(z)

    pair = pair_gather(node, "gx", 3)
    gathered = pair_gather(jnp.concatenate([pair.reshape(-1, rank)] + solved, axis=0), "gy", 0)
    return call(
        functools.partial(last_kernel, 3, [v.shape[0] for v in solved]),
        [right_sides.shape[::-1]],
        gathered,
        carried,
    )[0].T


def solution(mesh):
    placed = (P(("gx", "gy"), None), P(None, ("gx", "gy"), None), P(None, ("gx", "gy"), None))
    return jax.shard_map(
        shards, mesh=mesh, in_specs=placed, out_specs=P(("gx", "gy"), None), check_vma=False
    )
```

```python
import functools

import jax
import jax.numpy as jnp
from jax import lax
from jax.experimental import pallas as pl
from jax.experimental.pallas import tpu as pltpu
from jax.sharding import PartitionSpec as P

VMEM_BYTES = 40 * 2**20


def split(value):
    high = value.astype(jnp.bfloat16)
    low = (value - high.astype(jnp.float32)).astype(jnp.bfloat16)
    return high, low


def dot_split(a, b):
    def part(x, y):
        return jnp.dot(x, y, preferred_element_type=jnp.float32)

    return part(a[0], b[0]) + (part(a[0], b[1]) + part(a[1], b[0]))


def kdot(a, b):
    return dot_split(split(a), split(b))


def inverse_of(error):
    total = jnp.eye(error.shape[0], dtype=jnp.float32) + error
    power = error
    for step in range(6):
        parts = split(power)
        power = dot_split(parts, parts)
        total = total + kdot(total, power)
    return total


def solve_own(gram_own, gram_sib, proj_own, proj_sib):
    inverse = inverse_of(kdot(gram_own, gram_sib))
    return kdot(proj_sib - kdot(proj_own, gram_sib), inverse)


def solve_node(own, sib, ops_own, ops_sib, sums):
    rank = own.shape[1]
    width = own.shape[0] - rank
    gram_own, proj_own = own[:rank], own[rank:]
    z = solve_own(gram_own, sib[:rank], proj_own, sib[rank:])
    z_sib = proj_own - kdot(z, gram_own)
    z_both = split(jnp.concatenate([z, z_sib], axis=1))
    node = []
    for j in range(ops_own.shape[0] // rank):
        at = slice(j * rank, (j + 1) * rank)
        left = split(jnp.concatenate([ops_own[at], ops_sib[at]], axis=0))
        node.append(sums[j * width : (j + 1) * width] - dot_split(z_both, left))
    return z, jnp.concatenate(node, axis=0)


def put_rows(out, base, size, start, value):
    at, rows = 0, value.shape[0]
    while at < rows:
        i, r = divmod(start + at, size)
        n = min(size - r, rows - at)
        out[i, base + r : base + r + n] = value[at : at + n]
        at += n


def get_rows(ref, base, size):
    return jnp.concatenate([ref[i, pl.ds(base, size)] for i in range(ref.shape[0])], axis=0)


def bit_of(axis, bit):
    return (lax.axis_index(axis) >> bit) & 1


def times8(value, rows):
    return pl.multiple_of(value * rows, 8)


def first_pair_kernel(u, u_other, v, v_other, held, low, up, next_v, top_v):
    levels, _, rank = u.shape
    half = rank // 2
    first = bit_of("gy", 0) == 0
    last = (v.shape[0] - levels * rank) // 2
    lanes = (slice(0, rank), slice(rank, 2 * rank))
    for lane, w in zip(lanes, (u, u_other)):
        for j in range(levels):
            value = w[j].T
            if j < 2:
                held[j * rank : (j + 1) * rank, lane] = value
            else:
                at = 2 * rank + (j - 2) * half
                held[at : at + half, lane] = jnp.where(first, value[:half], value[half:])
    rows = pl.ds(levels * rank + times8(bit_of("gy", 0), last), last)
    for lane, ref in zip(lanes, (v, v_other)):
        held[held.shape[0] - last :, lane] = ref[rows]
    factors = [
        jnp.concatenate([ref[j * rank : (j + 1) * rank] for ref in (v, v_other)], axis=0)
        for j in range(levels)
    ]
    parts = split(held[...])
    low[...] = dot_split(parts, split(factors[0]))
    up[...] = dot_split(parts, split(factors[1]))
    for j in range(2, 4):
        next_v[j - 2] = factors[j]
    for j in range(4, levels):
        top_v[j - 4] = factors[j]


def first_node_kernel(bit, pair, up, z_out, out):
    side = bit_of("gy", bit)
    rank = up.shape[1]
    own, sib = pair[side], pair[1 - side]
    z = solve_own(own[:rank], sib[:rank], own[rank:], sib[rank:])
    z_out[...] = z
    value = up[rank:] - kdot(z, up[:rank])
    for i in range(out.shape[0]):
        out[i] = value


def after_pair(own, sib, z_low, held):
    rank = own.shape[1]
    z_up = solve_own(own[:rank], sib[:rank], own[rank:], sib[rank:])
    left = held[:rank]
    next_left = held[rank : 2 * rank] - kdot(z_low[:rank], left)
    z_both = jnp.concatenate([z_low[rank:], z_up], axis=1)
    return held[2 * rank :] - kdot(z_both, jnp.concatenate([left, next_left], axis=0))


def between_kernel(bit, shares, parts, z_low, held, v, rest, sent):
    side = bit_of("gy", bit)
    own, sib = [parts[2 * c] + parts[2 * c + 1] for c in (side, 1 - side)]
    value = after_pair(own, sib, z_low, held)
    rest[...] = value
    rows = value.shape[0]
    half = v.shape[2] // 2
    parts = split(value)
    low = dot_split(parts, split(v[0]))
    up = dot_split(parts, split(v[1]))
    n_both = (rows + half) // shares
    put_rows(sent, 0, n_both, 0, low)
    put_rows(sent, 0, n_both, rows, up[:half])
    put_rows(sent, n_both, (rows - half) // shares, 0, up[half:])


def second_shared_kernel(n_both, n_sums, rows, pieces, rest, out):
    rank = out.shape[1]
    half = rank // 2
    for c in range(2):
        both = get_rows(pieces, c * n_both, n_both)
        out[3 * half * c : 3 * half * c + rank] = both[:rank]
        out[3 * half * c + rank : 3 * half * (c + 1)] = both[rows:]
    out[6 * half : 7 * half] = get_rows(pieces, 2 * n_both, n_sums)[:half]
    out[7 * half : 9 * half] = rest[:rank, :rank]
    out[9 * half : 11 * half] = rest[:rank, rank:]


def both_cores(ref, at, n):
    return [ref[c, pl.ds(at, n)] for c in range(2)]


def full_rows(ref, at, n):
    return jnp.concatenate(both_cores(ref, at, n), axis=0)


def second_node_kernel(bit, n_both, n_sums, rows, pieces, shared, z_out, node_out):
    side = bit_of("gy", bit)
    rank = z_out.shape[1]
    half = rank // 2
    children = []
    for which in (side, 1 - side):
        at = times8(which, 3 * half)
        both = get_rows(pieces, times8(which, n_both), n_both)
        children.append(
            (
                jnp.concatenate(
                    [
                        full_rows(shared, at, half),
                        full_rows(shared, at + half, half),
                        both[rank:rows],
                    ],
                    axis=0,
                ),
                full_rows(shared, at + rank, half),
            )
        )
    (own, ops_own), (sib, ops_sib) = children
    sums = get_rows(pieces, 2 * n_both, n_sums)
    sums = jnp.concatenate([full_rows(shared, 6 * half, half), sums[half:]], axis=0)
    z, node = solve_node(own, sib, ops_own, ops_sib, sums)
    z_out[...] = z
    node_out[...] = node


def upper_kernel(bit, shares, pair, z_low, shared, rest, v, mine, other, sent):
    rank = v.shape[2]
    half = rank // 2
    core = bit_of("gy", 0)
    factors = []
    for c in range(2):
        a, b = shared[c, 7 * half : 9 * half], shared[c, 9 * half : 11 * half]
        here = core == c
        factors.append(
            jnp.concatenate([jnp.where(here, a, b), jnp.where(here, b, a)], axis=1)
        )
    held = jnp.concatenate(
        [factors[0][:half], factors[1][:half], factors[0][half:], factors[1][half:], rest[rank:]],
        axis=0,
    )
    side = bit_of("gy", bit)
    value = after_pair(pair[side], pair[1 - side], z_low, held)
    mine[...] = value[:, :rank]
    other[...] = value[:, rank:]
    count, width = v.shape[0], value.shape[0]
    n_both = (width + (count - 1) * half) // shares
    n_sums = (count - 1) * (width - half) // shares
    parts = split(value)
    put_rows(sent, 0, n_both, 0, dot_split(parts, split(v[0])))
    for j in range(1, count):
        rows = dot_split(parts, split(v[j]))
        put_rows(sent, 0, n_both, width + (j - 1) * half, rows[:half])
        put_rows(sent, n_both, n_sums, (j - 1) * (width - half), rows[half:])


def share_kernel(n_both, pair, out):
    rows = [pair[0, :n_both], pair[1, :n_both], pair[0, n_both:] + pair[1, n_both:]]
    value = jnp.concatenate(rows, axis=0)
    for i in range(out.shape[0]):
        out[i] = value


def interleaved(first, second, block):
    out, at, rows = [], 0, first.shape[0]
    while at < rows:
        n = min(block, rows - at)
        out += [first[at : at + n], second[at : at + n]]
        at += n
    return jnp.concatenate(out, axis=0)


def updated(carried, z):
    rank = z.shape[1]
    return carried[rank:] - kdot(z, carried[:rank])


def top_shared_kernel(n_both, width, gathered, other, out):
    half = out.shape[1] // 2
    n = half + 4 * n_both - width
    for c in range(2):
        both = get_rows(gathered, c * n_both, n_both)
        out[n * c : n * c + half] = both[:half]
        out[n * c + half : n * (c + 1)] = both[width:]
    out[2 * n :] = other[...]


def child_rows(shared, at, half, count, projections):
    own = jnp.concatenate([full_rows(shared, at, half), projections], axis=0)
    ops = [full_rows(shared, at + half * j, half) for j in range(1, count)]
    return own, jnp.concatenate(ops, axis=0)


def top_node_kernel(count, n_both, n_sums, gathered, shared, held, z_out, node_out, part, carried):
    rank = held.shape[1]
    half = rank // 2
    width = held.shape[0]
    core = bit_of("gy", 0)
    side = bit_of("gx", 0)
    children = []
    for which in (side, 1 - side):
        both = get_rows(gathered, times8(which, n_both), n_both)
        at = times8(which, half * count)
        children.append(child_rows(shared, at, half, count, both[half:width]))
    (own, ops_own), (sib, ops_sib) = children
    sums = get_rows(gathered, 2 * n_both, n_sums)
    z, node = solve_node(own, sib, ops_own, ops_sib, sums)
    z_out[...] = z
    node_out[...] = node
    n = part.shape[0]
    part[...] = node_out[pl.ds(times8((lax.axis_index("gy") >> 1) & 3, n), n)]
    swapped = [shared[c, 2 * half * count :] for c in range(2)]
    halves = [jnp.where(core == c, held[...], swapped[c]) for c in range(2)]
    carried[...] = interleaved(halves[0], halves[1], half)


def sibling_kernel(bit, pair, out):
    value = pair[1 - bit_of("gx", bit)]
    for i in range(out.shape[0]):
        out[i] = value


def upper_shared_kernel(count, bit, own, sib, out):
    half = out.shape[1] // 2
    width = own.shape[0] // count
    value = sib[...].reshape(own.shape) if bit is None else sib[1 - bit_of("gx", bit)]
    for j in range(count):
        at = slice(j * width, j * width + half)
        out[j * half : (j + 1) * half] = own[at]
        out[(count + j) * half : (count + j + 1) * half] = value[at]


def upper_node_kernel(count, bit, own, sib, shared, z_out, node_out):
    half = own.shape[1] // 2
    width = own.shape[0] // count
    here = own[...]
    there = sib[...].reshape(own.shape) if bit is None else sib[1 - bit_of("gx", bit)]
    rows_own, ops_own = child_rows(shared, 0, half, count, here[half:width])
    rows_sib, ops_sib = child_rows(shared, half * count, half, count, there[half:width])
    sums = jnp.concatenate(
        [
            here[j * width + half : (j + 1) * width] + there[j * width + half : (j + 1) * width]
            for j in range(1, count)
        ],
        axis=0,
    )
    z, node = solve_node(rows_own, rows_sib, ops_own, ops_sib, sums)
    z_out[...] = z
    node_out[...] = node


def last_kernel(bit, sizes, gathered, carried, out):
    rank = carried.shape[1]
    half = rank // 2
    side = bit_of("gx", bit)
    n = half + out.shape[0] // 2

    def child(which):
        return interleaved(*both_cores(gathered, times8(which, n), n), half)

    value, at = carried[...], 2 * n
    for size in sizes:
        value = updated(value, interleaved(*both_cores(gathered, at, size), half))
        at += size
    own, sib = child(side), child(1 - side)
    z = solve_own(own[:rank], sib[:rank], own[rank:], sib[rank:])
    out[...] = updated(value, z)


def call(kernel, outs, *args):
    rows = sum(a.size // 128 for a in args)
    return pl.pallas_call(
        kernel,
        out_shape=[jax.ShapeDtypeStruct(o, jnp.float32) for o in outs],
        compiler_params=pltpu.CompilerParams(vmem_limit_bytes=VMEM_BYTES),
        cost_estimate=pl.CostEstimate(
            flops=6 * 128 * 128 * (rows + 14 * 128),
            bytes_accessed=512 * rows,
            transcendentals=0,
        ),
    )(*args)


def bit_groups(count, bits):
    mask = sum(1 << b for b in bits)
    return [
        [
            base | sum(((i >> q) & 1) << b for q, b in enumerate(bits))
            for i in range(1 << len(bits))
        ]
        for base in range(count)
        if not base & mask
    ]


def swap_cores(value):
    return lax.ppermute(value, "gy", [(s, s ^ 1) for s in range(lax.axis_size("gy"))])


def pair_gather(value, axis, bit, tiled=False):
    groups = bit_groups(lax.axis_size(axis), [bit])
    return lax.all_gather(value, axis, axis_index_groups=groups, tiled=tiled)


def exchange(value, axis, bits):
    count = lax.axis_size(axis)
    return lax.all_to_all(value, axis, 0, 0, axis_index_groups=bit_groups(count, bits))


def to_all(value, axis, bits):
    return exchange(jnp.broadcast_to(value, (1 << len(bits),) + value.shape), axis, bits)


def pad_rows(value, rows):
    return jnp.pad(value, ((0, rows - value.shape[0]), (0, 0)))


def up8(value):
    return -(-value // 8) * 8


def shards(right_sides, factor_u, factor_v):
    levels, _, rank = factor_u.shape
    half = rank // 2
    near_chips = [1, 2]

    factors = jnp.concatenate([factor_v.reshape(-1, rank), right_sides.T], axis=0)
    rest = ((levels - 2) * rank + right_sides.shape[1]) // 2
    rows = 2 * rank + rest
    held, low, up, next_v, top_v = call(
        first_pair_kernel,
        [
            (rows, 2 * rank),
            (rows, rank),
            (rows, rank),
            (2, 2 * rank, rank),
            (levels - 4, 2 * rank, rank),
        ],
        factor_u,
        swap_cores(factor_u),
        factors,
        swap_cores(factors),
    )
    z_low, node = call(
        functools.partial(first_node_kernel, 1),
        [(rank + rest, rank), (4, rank + rest, rank)],
        pair_gather(low, "gy", 1),
        up,
    )

    rows = rest
    rest -= rank
    n_both, n_sums = (rows + half) // 4, (rows - half) // 4
    held, sent = call(
        functools.partial(between_kernel, 2, 4),
        [(rows, 2 * rank), (4, n_both + n_sums, rank)],
        exchange(node, "gy", near_chips),
        z_low,
        held,
        next_v,
    )
    piece = exchange(sent, "gy", near_chips).sum(axis=0)
    share = call(
        functools.partial(share_kernel, n_both),
        [(4, 2 * n_both + n_sums, rank)],
        pair_gather(piece, "gy", 3),
    )[0]
    pieces = exchange(share, "gy", near_chips)
    shared = call(
        functools.partial(second_shared_kernel, n_both, n_sums, rows),
        [(11 * half, rank)],
        pieces,
        held,
    )[0]
    shared = pair_gather(shared, "gy", 0)
    z_low, node = call(
        functools.partial(second_node_kernel, 3, n_both, n_sums, rows),
        [(rank + rest, rank), (rank + rest, rank)],
        pieces,
        shared,
    )

    count = levels - 4
    n_both = (rest + (count - 1) * half) // 4
    n_sums = (count - 1) * (rest - half) // 4
    mine, other, sent = call(
        functools.partial(upper_kernel, 4, 4),
        [(rest, rank), (rest, rank), (4, n_both + n_sums, rank)],
        pair_gather(node, "gy", 4),
        z_low,
        shared,
        held,
        top_v,
    )
    piece = exchange(sent, "gy", near_chips).sum(axis=0)
    s_both, s_sums = up8(-(-n_both // 8)), up8(-(-n_sums // 8))
    sent = jnp.concatenate(
        [
            pad_rows(piece[:n_both], 8 * s_both).reshape(8, s_both, rank),
            pad_rows(piece[n_both:], 8 * s_sums).reshape(8, s_sums, rank),
        ],
        axis=1,
    )
    far = [3, 4, 5]
    sides = exchange(sent, ("gx", "gy"), far)
    sides = sides.reshape((2, 4) + sides.shape[1:]).sum(axis=1)
    share = jnp.concatenate(
        [sides[0, :s_both], sides[1, :s_both], sides[0, s_both:] + sides[1, s_both:]], axis=0
    )
    pieces = to_all(share, ("gx", "gy"), far)
    share = jnp.concatenate(
        [
            pieces[:, :s_both].reshape(-1, rank)[:n_both],
            pieces[:, s_both : 2 * s_both].reshape(-1, rank)[:n_both],
            pieces[:, 2 * s_both :].reshape(-1, rank)[:n_sums],
        ],
        axis=0,
    )
    gathered = to_all(share, "gy", near_chips)
    shared = call(
        functools.partial(top_shared_kernel, n_both, rest),
        [(2 * count * half + rest, rank)],
        gathered,
        other,
    )[0]
    width = rest - half
    z, node, part, carried = call(
        functools.partial(top_node_kernel, count, n_both, n_sums),
        [
            (width, rank),
            ((count - 1) * width, rank),
            ((count - 1) * width // 4, rank),
            (2 * rest, rank),
        ],
        gathered,
        pair_gather(shared, "gy", 0),
        mine,
    )
    solved = [z]

    for bit in (1, 2):
        count -= 1
        pair = pair_gather(part, "gx", bit)
        if bit == 1:
            near = call(functools.partial(sibling_kernel, bit), [(4,) + part.shape], pair)[0]
            near, pick = exchange(near, "gy", near_chips), None
        else:
            near, pick = pair, bit
        shared = call(
            functools.partial(upper_shared_kernel, count, pick),
            [(2 * count * half, rank)],
            node,
            near,
        )[0]
        width -= half
        z, node = call(
            functools.partial(upper_node_kernel, count, pick),
            [(width, rank), ((count - 1) * width, rank)],
            node,
            near,
            pair_gather(shared, "gy", 0),
        )
        part = node
        solved.append(z)

    pair = pair_gather(node, "gx", 3)
    gathered = pair_gather(jnp.concatenate([pair.reshape(-1, rank)] + solved, axis=0), "gy", 0)
    return call(
        functools.partial(last_kernel, 3, [v.shape[0] for v in solved]),
        [right_sides.shape[::-1]],
        gathered,
        carried,
    )[0].T


def solution(mesh):
    placed = (P(("gx", "gy"), None), P(None, ("gx", "gy"), None), P(None, ("gx", "gy"), None))
    return jax.shard_map(
        shards, mesh=mesh, in_specs=placed, out_specs=P(("gx", "gy"), None), check_vma=False
    )
```

```python
import functools

import jax
import jax.numpy as jnp
from jax import lax
from jax.experimental import pallas as pl
from jax.experimental.pallas import tpu as pltpu
from jax.sharding import PartitionSpec as P

VMEM_BYTES = 40 * 2**20


def split(value):
    high = value.astype(jnp.bfloat16)
    low = (value - high.astype(jnp.float32)).astype(jnp.bfloat16)
    return high, low


def dot_split(a, b):
    def part(x, y):
        return jnp.dot(x, y, preferred_element_type=jnp.float32)

    return part(a[0], b[0]) + (part(a[0], b[1]) + part(a[1], b[0]))


def kdot(a, b):
    return dot_split(split(a), split(b))


def inverse_of(error):
    total = jnp.eye(error.shape[0], dtype=jnp.float32) + error
    power = error
    for step in range(6):
        parts = split(power)
        power = dot_split(parts, parts)
        total = total + kdot(total, power)
    return total


def solve_own(gram_own, gram_sib, proj_own, proj_sib):
    inverse = inverse_of(kdot(gram_own, gram_sib))
    return kdot(proj_sib - kdot(proj_own, gram_sib), inverse)


def solve_node(own, sib, ops_own, ops_sib, sums):
    rank = own.shape[1]
    width = own.shape[0] - rank
    gram_own, proj_own = split(own[:rank]), split(own[rank:])
    base, lefts = [], []
    for j in range(ops_own.shape[0] // rank):
        at = slice(j * rank, (j + 1) * rank)
        op_sib = split(ops_sib[at])
        base.append(sums[j * width : (j + 1) * width] - dot_split(proj_own, op_sib))
        lefts.append(split(ops_own[at] - dot_split(gram_own, op_sib)))
    z = solve_own(own[:rank], sib[:rank], own[rank:], sib[rank:])
    parts = split(z)
    node = [b - dot_split(parts, left) for b, left in zip(base, lefts)]
    return z, jnp.concatenate(node, axis=0)


def put_rows(out, base, size, start, value):
    at, rows = 0, value.shape[0]
    while at < rows:
        i, r = divmod(start + at, size)
        n = min(size - r, rows - at)
        out[i, base + r : base + r + n] = value[at : at + n]
        at += n


def get_rows(ref, base, size):
    return jnp.concatenate([ref[i, pl.ds(base, size)] for i in range(ref.shape[0])], axis=0)


def bit_of(axis, bit):
    return (lax.axis_index(axis) >> bit) & 1


def times8(value, rows):
    return pl.multiple_of(value * rows, 8)


def first_pair_kernel(levels, mine, other, held, low, up, next_v, top_v):
    rank = mine.shape[1]
    half = rank // 2
    core = bit_of("gy", 0)
    last = (mine.shape[0] - 2 * levels * rank) // 2
    rows = pl.ds(2 * levels * rank + times8(core, last), last)
    for c, ref in enumerate((mine, other)):
        lane = slice(c * rank, (c + 1) * rank)
        for j in range(levels):
            value = ref[j * rank : (j + 1) * rank].T
            if j < 2:
                held[j * rank : (j + 1) * rank, lane] = value
            else:
                at = 2 * rank + (j - 2) * half
                held[at : at + half, lane] = jnp.where(core == 0, value[:half], value[half:])
        held[held.shape[0] - last :, lane] = ref[rows]
    factors = [
        jnp.concatenate([ref[j * rank : (j + 1) * rank] for ref in (mine, other)], axis=0)
        for j in range(levels, 2 * levels)
    ]
    parts = split(held[...])
    low[...] = dot_split(parts, split(factors[0]))
    up[...] = dot_split(parts, split(factors[1]))
    for j in range(2, 4):
        next_v[j - 2] = factors[j]
    for j in range(4, levels):
        top_v[j - 4] = factors[j]


def first_node_kernel(bit, pair, up, z_out, out):
    side = bit_of("gy", bit)
    rank = up.shape[1]
    own, sib = pair[side], pair[1 - side]
    z = solve_own(own[:rank], sib[:rank], own[rank:], sib[rank:])
    z_out[...] = z
    value = up[rank:] - kdot(z, up[:rank])
    for i in range(out.shape[0]):
        out[i] = value


def after_pair(own, sib, z_low, held):
    rank = own.shape[1]
    z_up = solve_own(own[:rank], sib[:rank], own[rank:], sib[rank:])
    left = held[:rank]
    next_left = held[rank : 2 * rank] - kdot(z_low[:rank], left)
    z_both = jnp.concatenate([z_low[rank:], z_up], axis=1)
    return held[2 * rank :] - kdot(z_both, jnp.concatenate([left, next_left], axis=0))


def between_kernel(bit, shares, parts, z_low, held, v, rest, sent):
    side = bit_of("gy", bit)
    own, sib = [parts[2 * c] + parts[2 * c + 1] for c in (side, 1 - side)]
    value = after_pair(own, sib, z_low, held)
    rest[...] = value
    rows = value.shape[0]
    half = v.shape[2] // 2
    parts = split(value)
    low = dot_split(parts, split(v[0]))
    up = dot_split(parts, split(v[1]))
    n_both = (rows + half) // shares
    put_rows(sent, 0, n_both, 0, low)
    put_rows(sent, 0, n_both, rows, up[:half])
    put_rows(sent, n_both, (rows - half) // shares, 0, up[half:])


def second_shared_kernel(n_both, n_sums, rows, pieces, rest, out):
    rank = out.shape[1]
    half = rank // 2
    for c in range(2):
        both = get_rows(pieces, c * n_both, n_both)
        out[3 * half * c : 3 * half * c + rank] = both[:rank]
        out[3 * half * c + rank : 3 * half * (c + 1)] = both[rows:]
    out[6 * half : 7 * half] = get_rows(pieces, 2 * n_both, n_sums)[:half]
    out[7 * half : 9 * half] = rest[:rank, :rank]
    out[9 * half : 11 * half] = rest[:rank, rank:]


def both_cores(ref, at, n):
    return [ref[c, pl.ds(at, n)] for c in range(2)]


def full_rows(ref, at, n):
    return jnp.concatenate(both_cores(ref, at, n), axis=0)


def second_node_kernel(bit, n_both, n_sums, rows, pieces, shared, z_out, node_out):
    side = bit_of("gy", bit)
    rank = z_out.shape[1]
    half = rank // 2
    children = []
    for which in (side, 1 - side):
        at = times8(which, 3 * half)
        both = get_rows(pieces, times8(which, n_both), n_both)
        children.append(
            (
                jnp.concatenate(
                    [
                        full_rows(shared, at, half),
                        full_rows(shared, at + half, half),
                        both[rank:rows],
                    ],
                    axis=0,
                ),
                full_rows(shared, at + rank, half),
            )
        )
    (own, ops_own), (sib, ops_sib) = children
    sums = get_rows(pieces, 2 * n_both, n_sums)
    sums = jnp.concatenate([full_rows(shared, 6 * half, half), sums[half:]], axis=0)
    z, node = solve_node(own, sib, ops_own, ops_sib, sums)
    z_out[...] = z
    node_out[...] = node


def upper_kernel(bit, shares, pair, z_low, shared, rest, v, mine, other, sent):
    rank = v.shape[2]
    half = rank // 2
    core = bit_of("gy", 0)
    factors = []
    for c in range(2):
        a, b = shared[c, 7 * half : 9 * half], shared[c, 9 * half : 11 * half]
        here = core == c
        factors.append(
            jnp.concatenate([jnp.where(here, a, b), jnp.where(here, b, a)], axis=1)
        )
    held = jnp.concatenate(
        [factors[0][:half], factors[1][:half], factors[0][half:], factors[1][half:], rest[rank:]],
        axis=0,
    )
    side = bit_of("gy", bit)
    value = after_pair(pair[side], pair[1 - side], z_low, held)
    mine[...] = value[:, :rank]
    other[...] = value[:, rank:]
    count, width = v.shape[0], value.shape[0]
    n_both = (width + (count - 1) * half) // shares
    n_sums = (count - 1) * (width - half) // shares
    parts = split(value)
    put_rows(sent, 0, n_both, 0, dot_split(parts, split(v[0])))
    for j in range(1, count):
        rows = dot_split(parts, split(v[j]))
        put_rows(sent, 0, n_both, width + (j - 1) * half, rows[:half])
        put_rows(sent, n_both, n_sums, (j - 1) * (width - half), rows[half:])


def share_kernel(n_both, pair, out):
    rows = [pair[0, :n_both], pair[1, :n_both], pair[0, n_both:] + pair[1, n_both:]]
    value = jnp.concatenate(rows, axis=0)
    for i in range(out.shape[0]):
        out[i] = value


def interleaved(first, second, block):
    out, at, rows = [], 0, first.shape[0]
    while at < rows:
        n = min(block, rows - at)
        out += [first[at : at + n], second[at : at + n]]
        at += n
    return jnp.concatenate(out, axis=0)


def updated(carried, z):
    rank = z.shape[1]
    return carried[rank:] - kdot(z, carried[:rank])


def top_shared_kernel(n_both, width, gathered, other, out):
    half = out.shape[1] // 2
    n = half + 4 * n_both - width
    for c in range(2):
        both = get_rows(gathered, c * n_both, n_both)
        out[n * c : n * c + half] = both[:half]
        out[n * c + half : n * (c + 1)] = both[width:]
    out[2 * n :] = other[...]


def child_rows(shared, at, half, count, projections):
    own = jnp.concatenate([full_rows(shared, at, half), projections], axis=0)
    ops = [full_rows(shared, at + half * j, half) for j in range(1, count)]
    return own, jnp.concatenate(ops, axis=0)


def top_node_kernel(count, n_both, n_sums, gathered, shared, held, z_out, node_out, part, carried):
    rank = held.shape[1]
    half = rank // 2
    width = held.shape[0]
    core = bit_of("gy", 0)
    side = bit_of("gx", 0)
    children = []
    for which in (side, 1 - side):
        both = get_rows(gathered, times8(which, n_both), n_both)
        at = times8(which, half * count)
        children.append(child_rows(shared, at, half, count, both[half:width]))
    (own, ops_own), (sib, ops_sib) = children
    sums = get_rows(gathered, 2 * n_both, n_sums)
    z, node = solve_node(own, sib, ops_own, ops_sib, sums)
    z_out[...] = z
    node_out[...] = node
    n = part.shape[0]
    part[...] = node_out[pl.ds(times8((lax.axis_index("gy") >> 1) & 3, n), n)]
    swapped = [shared[c, 2 * half * count :] for c in range(2)]
    halves = [jnp.where(core == c, held[...], swapped[c]) for c in range(2)]
    carried[...] = interleaved(halves[0], halves[1], half)


def sibling_kernel(bit, pair, out):
    value = pair[1 - bit_of("gx", bit)]
    for i in range(out.shape[0]):
        out[i] = value


def quarter_shared_kernel(count, own, sib, z, out):
    half = out.shape[1] // 2
    width = own.shape[0] // count
    value = sib[...].reshape(own.shape)
    for j in range(count):
        at = slice(j * width, j * width + half)
        out[j * half : (j + 1) * half] = own[at]
        out[(count + j) * half : (count + j + 1) * half] = value[at]
    out[2 * count * half :] = z[...]


def quarter_node_kernel(count, own, sib, shared, carried, z_out, node_out, new):
    half = own.shape[1] // 2
    width = own.shape[0] // count
    here, there = own[...], sib[...].reshape(own.shape)
    rows_own, ops_own = child_rows(shared, 0, half, count, here[half:width])
    rows_sib, ops_sib = child_rows(shared, half * count, half, count, there[half:width])
    sums = jnp.concatenate(
        [
            here[j * width + half : (j + 1) * width] + there[j * width + half : (j + 1) * width]
            for j in range(1, count)
        ],
        axis=0,
    )
    z, node = solve_node(rows_own, rows_sib, ops_own, ops_sib, sums)
    z_out[...] = z
    node_out[...] = node
    below = both_cores(shared, 2 * count * half, shared.shape[1] - 2 * count * half)
    new[...] = updated(carried, interleaved(*below, half))


def whole_shared_kernel(bit, own, pair, z, out):
    rows = own.shape[0]
    out[:rows] = own[...]
    out[rows : 2 * rows] = pair[1 - bit_of("gx", bit)]
    out[2 * rows :] = z[...]


def whole_node_kernel(count, rows, shared, carried, node_out, new):
    half = carried.shape[1] // 2
    rank = 2 * half
    width = rows // count

    def child(at):
        return [
            interleaved(*both_cores(shared, at + j * width, width), half) for j in range(count)
        ]

    own, sib = child(0), child(rows)
    z, node = solve_node(
        own[0],
        sib[0],
        jnp.concatenate([v[:rank] for v in own[1:]], axis=0),
        jnp.concatenate([v[:rank] for v in sib[1:]], axis=0),
        jnp.concatenate([v[rank:] + w[rank:] for v, w in zip(own[1:], sib[1:])], axis=0),
    )
    node_out[...] = node
    below = both_cores(shared, 2 * rows, shared.shape[1] - 2 * rows)
    new[...] = updated(updated(carried, interleaved(*below, half)), z)


def last_kernel(bit, pair, carried, out):
    side = bit_of("gx", bit)
    rank = carried.shape[1]
    own, sib = pair[side], pair[1 - side]
    z = solve_own(own[:rank], sib[:rank], own[rank:], sib[rank:])
    out[...] = updated(carried, z)


def call(kernel, outs, *args):
    rows = sum(a.size // 128 for a in args)
    return pl.pallas_call(
        kernel,
        out_shape=[jax.ShapeDtypeStruct(o, jnp.float32) for o in outs],
        compiler_params=pltpu.CompilerParams(vmem_limit_bytes=VMEM_BYTES),
        cost_estimate=pl.CostEstimate(
            flops=6 * 128 * 128 * (rows + 14 * 128),
            bytes_accessed=512 * rows,
            transcendentals=0,
        ),
    )(*args)


def bit_groups(count, bits):
    mask = sum(1 << b for b in bits)
    return [
        [
            base | sum(((i >> q) & 1) << b for q, b in enumerate(bits))
            for i in range(1 << len(bits))
        ]
        for base in range(count)
        if not base & mask
    ]


def swap_cores(value):
    return lax.ppermute(value, "gy", [(s, s ^ 1) for s in range(lax.axis_size("gy"))])


def pair_gather(value, axis, bit, tiled=False):
    groups = bit_groups(lax.axis_size(axis), [bit])
    return lax.all_gather(value, axis, axis_index_groups=groups, tiled=tiled)


def exchange(value, axis, bits):
    count = lax.axis_size(axis)
    return lax.all_to_all(value, axis, 0, 0, axis_index_groups=bit_groups(count, bits))


def shards(right_sides, factor_u, factor_v):
    levels, _, rank = factor_u.shape
    half = rank // 2
    near_chips = [1, 2]

    packed = jnp.concatenate(
        [factor_u.reshape(-1, rank), factor_v.reshape(-1, rank), right_sides.T], axis=0
    )
    rest = ((levels - 2) * rank + right_sides.shape[1]) // 2
    rows = 2 * rank + rest
    held, low, up, next_v, top_v = call(
        functools.partial(first_pair_kernel, levels),
        [
            (rows, 2 * rank),
            (rows, rank),
            (rows, rank),
            (2, 2 * rank, rank),
            (levels - 4, 2 * rank, rank),
        ],
        packed,
        swap_cores(packed),
    )
    z_low, node = call(
        functools.partial(first_node_kernel, 1),
        [(rank + rest, rank), (4, rank + rest, rank)],
        pair_gather(low, "gy", 1),
        up,
    )

    rows = rest
    rest -= rank
    n_both, n_sums = (rows + half) // 4, (rows - half) // 4
    held, sent = call(
        functools.partial(between_kernel, 2, 4),
        [(rows, 2 * rank), (4, n_both + n_sums, rank)],
        exchange(node, "gy", near_chips),
        z_low,
        held,
        next_v,
    )
    piece = exchange(sent, "gy", near_chips).sum(axis=0)
    share = call(
        functools.partial(share_kernel, n_both),
        [(4, 2 * n_both + n_sums, rank)],
        pair_gather(piece, "gy", 3),
    )[0]
    pieces = exchange(share, "gy", near_chips)
    shared = call(
        functools.partial(second_shared_kernel, n_both, n_sums, rows),
        [(11 * half, rank)],
        pieces,
        held,
    )[0]
    shared = pair_gather(shared, "gy", 0)
    z_low, node = call(
        functools.partial(second_node_kernel, 3, n_both, n_sums, rows),
        [(rank + rest, rank), (rank + rest, rank)],
        pieces,
        shared,
    )

    count = levels - 4
    n_both = (rest + (count - 1) * half) // 4
    n_sums = (count - 1) * (rest - half) // 4
    mine, other, sent = call(
        functools.partial(upper_kernel, 4, 4),
        [(rest, rank), (rest, rank), (4, n_both + n_sums, rank)],
        pair_gather(node, "gy", 4),
        z_low,
        shared,
        held,
        top_v,
    )
    piece = exchange(sent, "gy", near_chips).sum(axis=0)
    for bit in (3, 4):
        pair = pair_gather(piece, "gy", bit)
        piece = pair[0] + pair[1]
    share = call(
        functools.partial(share_kernel, n_both),
        [(4, 2 * n_both + n_sums, rank)],
        pair_gather(piece, "gx", 0),
    )[0]
    gathered = exchange(share, "gy", near_chips)
    shared = call(
        functools.partial(top_shared_kernel, n_both, rest),
        [(2 * count * half + rest, rank)],
        gathered,
        other,
    )[0]
    width = rest - half
    z, node, part, carried = call(
        functools.partial(top_node_kernel, count, n_both, n_sums),
        [
            (width, rank),
            ((count - 1) * width, rank),
            ((count - 1) * width // 4, rank),
            (2 * rest, rank),
        ],
        gathered,
        pair_gather(shared, "gy", 0),
        mine,
    )

    count -= 1
    rows = 2 * rest
    near = call(
        functools.partial(sibling_kernel, 1), [(4,) + part.shape], pair_gather(part, "gx", 1)
    )[0]
    near = exchange(near, "gy", near_chips)
    shared = call(
        functools.partial(quarter_shared_kernel, count),
        [(2 * count * half + width, rank)],
        node,
        near,
        z,
    )[0]
    width -= half
    rows -= rank
    z, node, carried = call(
        functools.partial(quarter_node_kernel, count),
        [(width, rank), ((count - 1) * width, rank), (rows, rank)],
        node,
        near,
        pair_gather(shared, "gy", 0),
        carried,
    )

    count -= 1
    shared = call(
        functools.partial(whole_shared_kernel, 2),
        [(2 * node.shape[0] + width, rank)],
        node,
        pair_gather(node, "gx", 2),
        z,
    )[0]
    rows -= 2 * rank
    node, carried = call(
        functools.partial(whole_node_kernel, count, node.shape[0]),
        [((count - 1) * rows, rank), (rows, rank)],
        pair_gather(shared, "gy", 0),
        carried,
    )

    return call(
        functools.partial(last_kernel, 3),
        [right_sides.shape[::-1]],
        pair_gather(node, "gx", 3),
        carried,
    )[0].T


def solution(mesh):
    placed = (P(("gx", "gy"), None), P(None, ("gx", "gy"), None), P(None, ("gx", "gy"), None))
    return jax.shard_map(
        shards, mesh=mesh, in_specs=placed, out_specs=P(("gx", "gy"), None), check_vma=False
    )
```

```python
import functools

import jax
import jax.numpy as jnp
from jax import lax
from jax.experimental import pallas as pl
from jax.experimental.pallas import tpu as pltpu
from jax.sharding import PartitionSpec as P

VMEM_BYTES = 40 * 2**20


def split(value):
    high = value.astype(jnp.bfloat16)
    low = (value - high.astype(jnp.float32)).astype(jnp.bfloat16)
    return high, low


def dot_split(a, b):
    def part(x, y):
        return jnp.dot(x, y, preferred_element_type=jnp.float32)

    return part(a[0], b[0]) + (part(a[0], b[1]) + part(a[1], b[0]))


def kdot(a, b):
    return dot_split(split(a), split(b))


def inverse_of(error):
    total = jnp.eye(error.shape[0], dtype=jnp.float32) + error
    power = error
    for step in range(6):
        parts = split(power)
        power = dot_split(parts, parts)
        total = total + kdot(total, power)
    return total


def solve_own(gram_own, gram_sib, proj_own, proj_sib):
    inverse = inverse_of(kdot(gram_own, gram_sib))
    return kdot(proj_sib - kdot(proj_own, gram_sib), inverse)


def solve_node(own, sib, ops_own, ops_sib, sums):
    rank = own.shape[1]
    width = own.shape[0] - rank
    gram_own, proj_own = split(own[:rank]), split(own[rank:])
    base, lefts = [], []
    for j in range(ops_own.shape[0] // rank):
        at = slice(j * rank, (j + 1) * rank)
        op_sib = split(ops_sib[at])
        base.append(sums[j * width : (j + 1) * width] - dot_split(proj_own, op_sib))
        lefts.append(split(ops_own[at] - dot_split(gram_own, op_sib)))
    z = solve_own(own[:rank], sib[:rank], own[rank:], sib[rank:])
    parts = split(z)
    node = [b - dot_split(parts, left) for b, left in zip(base, lefts)]
    return z, jnp.concatenate(node, axis=0)


def put_rows(out, base, size, start, value):
    at, rows = 0, value.shape[0]
    while at < rows:
        i, r = divmod(start + at, size)
        n = min(size - r, rows - at)
        out[i, base + r : base + r + n] = value[at : at + n]
        at += n


def get_rows(ref, base, size):
    return jnp.concatenate([ref[i, pl.ds(base, size)] for i in range(ref.shape[0])], axis=0)


def bit_of(axis, bit):
    return (lax.axis_index(axis) >> bit) & 1


def times8(value, rows):
    return pl.multiple_of(value * rows, 8)


def first_pair_kernel(levels, mine, other, held, low, up, next_v, top_v):
    rank = mine.shape[1]
    half = rank // 2
    core = bit_of("gy", 0)
    last = (mine.shape[0] - 2 * levels * rank) // 2
    rows = pl.ds(2 * levels * rank + times8(core, last), last)
    for c, ref in enumerate((mine, other)):
        lane = slice(c * rank, (c + 1) * rank)
        for j in range(levels):
            value = ref[j * rank : (j + 1) * rank].T
            if j < 2:
                held[j * rank : (j + 1) * rank, lane] = value
            else:
                at = 2 * rank + (j - 2) * half
                held[at : at + half, lane] = jnp.where(core == 0, value[:half], value[half:])
        held[held.shape[0] - last :, lane] = ref[rows]
    factors = [
        jnp.concatenate([ref[j * rank : (j + 1) * rank] for ref in (mine, other)], axis=0)
        for j in range(levels, 2 * levels)
    ]
    parts = split(held[...])
    low[...] = dot_split(parts, split(factors[0]))
    up[...] = dot_split(parts, split(factors[1]))
    for j in range(2, 4):
        next_v[j - 2] = factors[j]
    for j in range(4, levels):
        top_v[j - 4] = factors[j]


def first_node_kernel(bit, pair, up, z_out, out):
    side = bit_of("gy", bit)
    rank = up.shape[1]
    own, sib = pair[side], pair[1 - side]
    z = solve_own(own[:rank], sib[:rank], own[rank:], sib[rank:])
    z_out[...] = z
    out[...] = up[rank:] - kdot(z, up[:rank])


def after_pair(own, sib, z_low, held):
    rank = own.shape[1]
    z_up = solve_own(own[:rank], sib[:rank], own[rank:], sib[rank:])
    left = held[:rank]
    next_left = held[rank : 2 * rank] - kdot(z_low[:rank], left)
    z_both = jnp.concatenate([z_low[rank:], z_up], axis=1)
    return held[2 * rank :] - kdot(z_both, jnp.concatenate([left, next_left], axis=0))


def between_kernel(bit, shares, pair, z_low, held, v, rest, sent):
    side = bit_of("gy", bit)
    value = after_pair(pair[side], pair[1 - side], z_low, held)
    rest[...] = value
    rows = value.shape[0]
    half = v.shape[2] // 2
    parts = split(value)
    low = dot_split(parts, split(v[0]))
    up = dot_split(parts, split(v[1]))
    n_both = (rows + half) // shares
    put_rows(sent, 0, n_both, 0, low)
    put_rows(sent, 0, n_both, rows, up[:half])
    put_rows(sent, n_both, (rows - half) // shares, 0, up[half:])


def second_shared_kernel(n_both, n_sums, rows, pieces, rest, out):
    rank = out.shape[1]
    half = rank // 2
    for c in range(2):
        both = get_rows(pieces, c * n_both, n_both)
        out[3 * half * c : 3 * half * c + rank] = both[:rank]
        out[3 * half * c + rank : 3 * half * (c + 1)] = both[rows:]
    out[6 * half : 7 * half] = get_rows(pieces, 2 * n_both, n_sums)[:half]
    out[7 * half : 9 * half] = rest[:rank, :rank]
    out[9 * half : 11 * half] = rest[:rank, rank:]


def both_cores(ref, at, n):
    return [ref[c, pl.ds(at, n)] for c in range(2)]


def full_rows(ref, at, n):
    return jnp.concatenate(both_cores(ref, at, n), axis=0)


def second_node_kernel(bit, n_both, n_sums, rows, pieces, shared, z_out, node_out):
    side = bit_of("gy", bit)
    rank = z_out.shape[1]
    half = rank // 2
    children = []
    for which in (side, 1 - side):
        at = times8(which, 3 * half)
        both = get_rows(pieces, times8(which, n_both), n_both)
        children.append(
            (
                jnp.concatenate(
                    [
                        full_rows(shared, at, half),
                        full_rows(shared, at + half, half),
                        both[rank:rows],
                    ],
                    axis=0,
                ),
                full_rows(shared, at + rank, half),
            )
        )
    (own, ops_own), (sib, ops_sib) = children
    sums = get_rows(pieces, 2 * n_both, n_sums)
    sums = jnp.concatenate([full_rows(shared, 6 * half, half), sums[half:]], axis=0)
    z, node = solve_node(own, sib, ops_own, ops_sib, sums)
    z_out[...] = z
    node_out[...] = node


def upper_kernel(bit, shares, pair, z_low, shared, rest, v, mine, other, sent):
    rank = v.shape[2]
    half = rank // 2
    core = bit_of("gy", 0)
    factors = []
    for c in range(2):
        a, b = shared[c, 7 * half : 9 * half], shared[c, 9 * half : 11 * half]
        here = core == c
        factors.append(
            jnp.concatenate([jnp.where(here, a, b), jnp.where(here, b, a)], axis=1)
        )
    held = jnp.concatenate(
        [factors[0][:half], factors[1][:half], factors[0][half:], factors[1][half:], rest[rank:]],
        axis=0,
    )
    side = bit_of("gy", bit)
    value = after_pair(pair[side], pair[1 - side], z_low, held)
    mine[...] = value[:, :rank]
    other[...] = value[:, rank:]
    count, width = v.shape[0], value.shape[0]
    n_both = (width + (count - 1) * half) // shares
    n_sums = (count - 1) * (width - half) // shares
    parts = split(value)
    put_rows(sent, 0, n_both, 0, dot_split(parts, split(v[0])))
    for j in range(1, count):
        rows = dot_split(parts, split(v[j]))
        put_rows(sent, 0, n_both, width + (j - 1) * half, rows[:half])
        put_rows(sent, n_both, n_sums, (j - 1) * (width - half), rows[half:])


def share_kernel(n_both, pair, out):
    rows = [pair[0, :n_both], pair[1, :n_both], pair[0, n_both:] + pair[1, n_both:]]
    value = jnp.concatenate(rows, axis=0)
    for i in range(out.shape[0]):
        out[i] = value


def interleaved(first, second, block):
    out, at, rows = [], 0, first.shape[0]
    while at < rows:
        n = min(block, rows - at)
        out += [first[at : at + n], second[at : at + n]]
        at += n
    return jnp.concatenate(out, axis=0)


def updated(carried, z):
    rank = z.shape[1]
    return carried[rank:] - kdot(z, carried[:rank])


def top_shared_kernel(n_both, width, gathered, other, out):
    half = out.shape[1] // 2
    n = half + 4 * n_both - width
    for c in range(2):
        both = get_rows(gathered, c * n_both, n_both)
        out[n * c : n * c + half] = both[:half]
        out[n * c + half : n * (c + 1)] = both[width:]
    out[2 * n :] = other[...]


def child_rows(shared, at, half, count, projections):
    own = jnp.concatenate([full_rows(shared, at, half), projections], axis=0)
    ops = [full_rows(shared, at + half * j, half) for j in range(1, count)]
    return own, jnp.concatenate(ops, axis=0)


def top_node_kernel(count, n_both, n_sums, gathered, shared, held, z_out, node_out, part, carried):
    rank = held.shape[1]
    half = rank // 2
    width = held.shape[0]
    core = bit_of("gy", 0)
    side = bit_of("gx", 0)
    children = []
    for which in (side, 1 - side):
        both = get_rows(gathered, times8(which, n_both), n_both)
        at = times8(which, half * count)
        children.append(child_rows(shared, at, half, count, both[half:width]))
    (own, ops_own), (sib, ops_sib) = children
    sums = get_rows(gathered, 2 * n_both, n_sums)
    z, node = solve_node(own, sib, ops_own, ops_sib, sums)
    z_out[...] = z
    node_out[...] = node
    n = part.shape[0]
    part[...] = node_out[pl.ds(times8((lax.axis_index("gy") >> 1) & 3, n), n)]
    swapped = [shared[c, 2 * half * count :] for c in range(2)]
    halves = [jnp.where(core == c, held[...], swapped[c]) for c in range(2)]
    carried[...] = interleaved(halves[0], halves[1], half)


def sibling_kernel(bit, pair, out):
    value = pair[1 - bit_of("gx", bit)]
    for i in range(out.shape[0]):
        out[i] = value


def quarter_shared_kernel(count, own, sib, z, out):
    half = out.shape[1] // 2
    width = own.shape[0] // count
    value = sib[...].reshape(own.shape)
    for j in range(count):
        at = slice(j * width, j * width + half)
        out[j * half : (j + 1) * half] = own[at]
        out[(count + j) * half : (count + j + 1) * half] = value[at]
    out[2 * count * half :] = z[...]


def quarter_node_kernel(count, own, sib, shared, carried, z_out, node_out, new):
    half = own.shape[1] // 2
    width = own.shape[0] // count
    here, there = own[...], sib[...].reshape(own.shape)
    rows_own, ops_own = child_rows(shared, 0, half, count, here[half:width])
    rows_sib, ops_sib = child_rows(shared, half * count, half, count, there[half:width])
    sums = jnp.concatenate(
        [
            here[j * width + half : (j + 1) * width] + there[j * width + half : (j + 1) * width]
            for j in range(1, count)
        ],
        axis=0,
    )
    z, node = solve_node(rows_own, rows_sib, ops_own, ops_sib, sums)
    z_out[...] = z
    node_out[...] = node
    below = both_cores(shared, 2 * count * half, shared.shape[1] - 2 * count * half)
    new[...] = updated(carried, interleaved(*below, half))


def whole_shared_kernel(bit, own, pair, z, out):
    rows = own.shape[0]
    out[:rows] = own[...]
    out[rows : 2 * rows] = pair[1 - bit_of("gx", bit)]
    out[2 * rows :] = z[...]


def whole_node_kernel(count, rows, shared, carried, node_out, new):
    half = carried.shape[1] // 2
    rank = 2 * half
    width = rows // count

    def child(at):
        return [
            interleaved(*both_cores(shared, at + j * width, width), half) for j in range(count)
        ]

    own, sib = child(0), child(rows)
    z, node = solve_node(
        own[0],
        sib[0],
        jnp.concatenate([v[:rank] for v in own[1:]], axis=0),
        jnp.concatenate([v[:rank] for v in sib[1:]], axis=0),
        jnp.concatenate([v[rank:] + w[rank:] for v, w in zip(own[1:], sib[1:])], axis=0),
    )
    node_out[...] = node
    below = both_cores(shared, 2 * rows, shared.shape[1] - 2 * rows)
    new[...] = updated(updated(carried, interleaved(*below, half)), z)


def last_kernel(bit, pair, carried, out):
    side = bit_of("gx", bit)
    rank = carried.shape[1]
    own, sib = pair[side], pair[1 - side]
    z = solve_own(own[:rank], sib[:rank], own[rank:], sib[rank:])
    out[...] = updated(carried, z)


def call(kernel, outs, *args):
    rows = sum(a.size // 128 for a in args)
    return pl.pallas_call(
        kernel,
        out_shape=[jax.ShapeDtypeStruct(o, jnp.float32) for o in outs],
        compiler_params=pltpu.CompilerParams(vmem_limit_bytes=VMEM_BYTES),
        cost_estimate=pl.CostEstimate(
            flops=6 * 128 * 128 * (rows + 14 * 128),
            bytes_accessed=512 * rows,
            transcendentals=0,
        ),
    )(*args)


def bit_groups(count, bits):
    mask = sum(1 << b for b in bits)
    return [
        [
            base | sum(((i >> q) & 1) << b for q, b in enumerate(bits))
            for i in range(1 << len(bits))
        ]
        for base in range(count)
        if not base & mask
    ]


def swap_cores(value):
    return lax.ppermute(value, "gy", [(s, s ^ 1) for s in range(lax.axis_size("gy"))])


def pair_gather(value, axis, bit, tiled=False):
    groups = bit_groups(lax.axis_size(axis), [bit])
    return lax.all_gather(value, axis, axis_index_groups=groups, tiled=tiled)


def exchange(value, axis, bits):
    count = lax.axis_size(axis)
    return lax.all_to_all(value, axis, 0, 0, axis_index_groups=bit_groups(count, bits))


def to_all(value, axis, bits):
    return exchange(jnp.broadcast_to(value, (1 << len(bits),) + value.shape), axis, bits)


def pad_rows(value, rows):
    return jnp.pad(value, ((0, rows - value.shape[0]), (0, 0)))


def up8(value):
    return -(-value // 8) * 8


def shards(right_sides, factor_u, factor_v):
    levels, _, rank = factor_u.shape
    half = rank // 2
    near_chips = [1, 2]

    packed = jnp.concatenate(
        [factor_u.reshape(-1, rank), factor_v.reshape(-1, rank), right_sides.T], axis=0
    )
    rest = ((levels - 2) * rank + right_sides.shape[1]) // 2
    rows = 2 * rank + rest
    held, low, up, next_v, top_v = call(
        functools.partial(first_pair_kernel, levels),
        [
            (rows, 2 * rank),
            (rows, rank),
            (rows, rank),
            (2, 2 * rank, rank),
            (levels - 4, 2 * rank, rank),
        ],
        packed,
        swap_cores(packed),
    )
    z_low, node = call(
        functools.partial(first_node_kernel, 1),
        [(rank + rest, rank), (rank + rest, rank)],
        pair_gather(low, "gy", 1),
        up,
    )
    pair = pair_gather(node, "gy", 1)
    pair = pair_gather(pair[0] + pair[1], "gy", 2)

    rows = rest
    rest -= rank
    n_both, n_sums = (rows + half) // 4, (rows - half) // 4
    held, sent = call(
        functools.partial(between_kernel, 2, 4),
        [(rows, 2 * rank), (4, n_both + n_sums, rank)],
        pair,
        z_low,
        held,
        next_v,
    )
    piece = exchange(sent, "gy", near_chips).sum(axis=0)
    share = call(
        functools.partial(share_kernel, n_both),
        [(4, 2 * n_both + n_sums, rank)],
        pair_gather(piece, "gy", 3),
    )[0]
    pieces = exchange(share, "gy", near_chips)
    shared = call(
        functools.partial(second_shared_kernel, n_both, n_sums, rows),
        [(11 * half, rank)],
        pieces,
        held,
    )[0]
    shared = pair_gather(shared, "gy", 0)
    z_low, node = call(
        functools.partial(second_node_kernel, 3, n_both, n_sums, rows),
        [(rank + rest, rank), (rank + rest, rank)],
        pieces,
        shared,
    )

    count = levels - 4
    n_both = (rest + (count - 1) * half) // 4
    n_sums = (count - 1) * (rest - half) // 4
    mine, other, sent = call(
        functools.partial(upper_kernel, 4, 4),
        [(rest, rank), (rest, rank), (4, n_both + n_sums, rank)],
        pair_gather(node, "gy", 4),
        z_low,
        shared,
        held,
        top_v,
    )
    piece = exchange(sent, "gy", near_chips).sum(axis=0)
    s_both, s_sums = up8(-(-n_both // 8)), up8(-(-n_sums // 8))
    sent = jnp.concatenate(
        [
            pad_rows(piece[:n_both], 8 * s_both).reshape(8, s_both, rank),
            pad_rows(piece[n_both:], 8 * s_sums).reshape(8, s_sums, rank),
        ],
        axis=1,
    )
    far = [3, 4, 5]
    sides = exchange(sent, ("gx", "gy"), far)
    sides = sides.reshape((2, 4) + sides.shape[1:]).sum(axis=1)
    share = jnp.concatenate(
        [sides[0, :s_both], sides[1, :s_both], sides[0, s_both:] + sides[1, s_both:]], axis=0
    )
    pieces = to_all(share, ("gx", "gy"), far)
    share = jnp.concatenate(
        [
            pieces[:, :s_both].reshape(-1, rank)[:n_both],
            pieces[:, s_both : 2 * s_both].reshape(-1, rank)[:n_both],
            pieces[:, 2 * s_both :].reshape(-1, rank)[:n_sums],
        ],
        axis=0,
    )
    gathered = to_all(share, "gy", near_chips)
    shared = call(
        functools.partial(top_shared_kernel, n_both, rest),
        [(2 * count * half + rest, rank)],
        gathered,
        other,
    )[0]
    width = rest - half
    z, node, part, carried = call(
        functools.partial(top_node_kernel, count, n_both, n_sums),
        [
            (width, rank),
            ((count - 1) * width, rank),
            ((count - 1) * width // 4, rank),
            (2 * rest, rank),
        ],
        gathered,
        pair_gather(shared, "gy", 0),
        mine,
    )

    count -= 1
    rows = 2 * rest
    near = call(
        functools.partial(sibling_kernel, 1), [(4,) + part.shape], pair_gather(part, "gx", 1)
    )[0]
    near = exchange(near, "gy", near_chips)
    shared = call(
        functools.partial(quarter_shared_kernel, count),
        [(2 * count * half + width, rank)],
        node,
        near,
        z,
    )[0]
    width -= half
    rows -= rank
    z, node, carried = call(
        functools.partial(quarter_node_kernel, count),
        [(width, rank), ((count - 1) * width, rank), (rows, rank)],
        node,
        near,
        pair_gather(shared, "gy", 0),
        carried,
    )

    count -= 1
    shared = call(
        functools.partial(whole_shared_kernel, 2),
        [(2 * node.shape[0] + width, rank)],
        node,
        pair_gather(node, "gx", 2),
        z,
    )[0]
    rows -= 2 * rank
    node, carried = call(
        functools.partial(whole_node_kernel, count, node.shape[0]),
        [((count - 1) * rows, rank), (rows, rank)],
        pair_gather(shared, "gy", 0),
        carried,
    )

    return call(
        functools.partial(last_kernel, 3),
        [right_sides.shape[::-1]],
        pair_gather(node, "gx", 3),
        carried,
    )[0].T


def solution(mesh):
    placed = (P(("gx", "gy"), None), P(None, ("gx", "gy"), None), P(None, ("gx", "gy"), None))
    return jax.shard_map(
        shards, mesh=mesh, in_specs=placed, out_specs=P(("gx", "gy"), None), check_vma=False
    )
```

```python
import functools

import jax
import jax.numpy as jnp
from jax import lax
from jax.experimental import pallas as pl
from jax.experimental.pallas import tpu as pltpu
from jax.sharding import PartitionSpec as P

VMEM_BYTES = 40 * 2**20


def split(value):
    high = value.astype(jnp.bfloat16)
    low = (value - high.astype(jnp.float32)).astype(jnp.bfloat16)
    return high, low


def dot_split(a, b):
    def part(x, y):
        return jnp.dot(x, y, preferred_element_type=jnp.float32)

    return part(a[0], b[0]) + (part(a[0], b[1]) + part(a[1], b[0]))


def kdot(a, b):
    return dot_split(split(a), split(b))


def inverse_of(error):
    total = jnp.eye(error.shape[0], dtype=jnp.float32) + error
    power = error
    for step in range(6):
        parts = split(power)
        power = dot_split(parts, parts)
        total = total + kdot(total, power)
    return total


def solve_own(gram_own, gram_sib, proj_own, proj_sib):
    inverse = inverse_of(kdot(gram_own, gram_sib))
    return kdot(proj_sib - kdot(proj_own, gram_sib), inverse)


def solve_node(own, sib, ops_own, ops_sib, sums):
    rank = own.shape[1]
    width = own.shape[0] - rank
    gram_own, proj_own = split(own[:rank]), split(own[rank:])
    base, lefts = [], []
    for j in range(ops_own.shape[0] // rank):
        at = slice(j * rank, (j + 1) * rank)
        op_sib = split(ops_sib[at])
        base.append(sums[j * width : (j + 1) * width] - dot_split(proj_own, op_sib))
        lefts.append(split(ops_own[at] - dot_split(gram_own, op_sib)))
    z = solve_own(own[:rank], sib[:rank], own[rank:], sib[rank:])
    parts = split(z)
    node = [b - dot_split(parts, left) for b, left in zip(base, lefts)]
    return z, jnp.concatenate(node, axis=0)


def put_rows(out, base, size, start, value):
    at, rows = 0, value.shape[0]
    while at < rows:
        i, r = divmod(start + at, size)
        n = min(size - r, rows - at)
        out[i, base + r : base + r + n] = value[at : at + n]
        at += n


def get_rows(ref, base, size):
    return jnp.concatenate([ref[i, pl.ds(base, size)] for i in range(ref.shape[0])], axis=0)


def bit_of(axis, bit):
    return (lax.axis_index(axis) >> bit) & 1


def times8(value, rows):
    return pl.multiple_of(value * rows, 8)


def first_pair_kernel(levels, mine, other, held, low, up, next_v, top_v):
    rank = mine.shape[1]
    half = rank // 2
    core = bit_of("gy", 0)
    last = (mine.shape[0] - 2 * levels * rank) // 2
    rows = pl.ds(2 * levels * rank + times8(core, last), last)
    for c, ref in enumerate((mine, other)):
        lane = slice(c * rank, (c + 1) * rank)
        for j in range(levels):
            value = ref[j * rank : (j + 1) * rank].T
            if j < 2:
                held[j * rank : (j + 1) * rank, lane] = value
            else:
                at = 2 * rank + (j - 2) * half
                held[at : at + half, lane] = jnp.where(core == 0, value[:half], value[half:])
        held[held.shape[0] - last :, lane] = ref[rows]
    factors = [
        jnp.concatenate([ref[j * rank : (j + 1) * rank] for ref in (mine, other)], axis=0)
        for j in range(levels, 2 * levels)
    ]
    parts = split(held[...])
    low[...] = dot_split(parts, split(factors[0]))
    up[...] = dot_split(parts, split(factors[1]))
    for j in range(2, 4):
        next_v[j - 2] = factors[j]
    for j in range(4, levels):
        top_v[j - 4] = factors[j]


def first_node_kernel(bit, pair, up, z_out, out):
    side = bit_of("gy", bit)
    rank = up.shape[1]
    own, sib = pair[side], pair[1 - side]
    z = solve_own(own[:rank], sib[:rank], own[rank:], sib[rank:])
    z_out[...] = z
    out[...] = up[rank:] - kdot(z, up[:rank])


def after_pair(own, sib, z_low, held):
    rank = own.shape[1]
    z_up = solve_own(own[:rank], sib[:rank], own[rank:], sib[rank:])
    left = held[:rank]
    next_left = held[rank : 2 * rank] - kdot(z_low[:rank], left)
    z_both = jnp.concatenate([z_low[rank:], z_up], axis=1)
    return held[2 * rank :] - kdot(z_both, jnp.concatenate([left, next_left], axis=0))


def between_kernel(bit, shares, pair, z_low, held, v, rest, sent):
    side = bit_of("gy", bit)
    value = after_pair(pair[side], pair[1 - side], z_low, held)
    rest[...] = value
    rows = value.shape[0]
    half = v.shape[2] // 2
    parts = split(value)
    low = dot_split(parts, split(v[0]))
    up = dot_split(parts, split(v[1]))
    n_both = (rows + half) // shares
    put_rows(sent, 0, n_both, 0, low)
    put_rows(sent, 0, n_both, rows, up[:half])
    put_rows(sent, n_both, (rows - half) // shares, 0, up[half:])


def second_shared_kernel(n_both, n_sums, rows, pieces, rest, out):
    rank = out.shape[1]
    half = rank // 2
    for c in range(2):
        both = get_rows(pieces, c * n_both, n_both)
        out[3 * half * c : 3 * half * c + rank] = both[:rank]
        out[3 * half * c + rank : 3 * half * (c + 1)] = both[rows:]
    out[6 * half : 7 * half] = get_rows(pieces, 2 * n_both, n_sums)[:half]
    out[7 * half : 9 * half] = rest[:rank, :rank]
    out[9 * half : 11 * half] = rest[:rank, rank:]


def both_cores(ref, at, n):
    return [ref[c, pl.ds(at, n)] for c in range(2)]


def full_rows(ref, at, n):
    return jnp.concatenate(both_cores(ref, at, n), axis=0)


def second_node_kernel(bit, n_both, n_sums, rows, pieces, shared, z_out, node_out):
    side = bit_of("gy", bit)
    rank = z_out.shape[1]
    half = rank // 2
    children = []
    for which in (side, 1 - side):
        at = times8(which, 3 * half)
        both = get_rows(pieces, times8(which, n_both), n_both)
        children.append(
            (
                jnp.concatenate(
                    [
                        full_rows(shared, at, half),
                        full_rows(shared, at + half, half),
                        both[rank:rows],
                    ],
                    axis=0,
                ),
                full_rows(shared, at + rank, half),
            )
        )
    (own, ops_own), (sib, ops_sib) = children
    sums = get_rows(pieces, 2 * n_both, n_sums)
    sums = jnp.concatenate([full_rows(shared, 6 * half, half), sums[half:]], axis=0)
    z, node = solve_node(own, sib, ops_own, ops_sib, sums)
    z_out[...] = z
    node_out[...] = node


def upper_kernel(bit, s_both, pair, z_low, shared, rest, v, mine, other, sent):
    rank = v.shape[2]
    half = rank // 2
    core = bit_of("gy", 0)
    factors = []
    for c in range(2):
        a, b = shared[c, 7 * half : 9 * half], shared[c, 9 * half : 11 * half]
        here = core == c
        factors.append(
            jnp.concatenate([jnp.where(here, a, b), jnp.where(here, b, a)], axis=1)
        )
    held = jnp.concatenate(
        [factors[0][:half], factors[1][:half], factors[0][half:], factors[1][half:], rest[rank:]],
        axis=0,
    )
    side = bit_of("gy", bit)
    value = after_pair(pair[side], pair[1 - side], z_low, held)
    mine[...] = value[:, :rank]
    other[...] = value[:, rank:]
    count, width = v.shape[0], value.shape[0]
    parts = split(value)
    rows = [dot_split(parts, split(v[j])) for j in range(count)]
    both = jnp.concatenate([rows[0]] + [r[:half] for r in rows[1:]], axis=0)
    sums = jnp.concatenate([r[half:] for r in rows[1:]], axis=0)
    far = sent.shape[0] // 4
    for value, base, size in ((both, 0, s_both), (sums, s_both, sent.shape[1] - s_both)):
        n = value.shape[0] // 4
        for c in range(4):
            for f in range(far):
                at, end = min(f * size, n), min((f + 1) * size, n)
                to = base + end - at
                if end > at:
                    sent[4 * f + c, base:to] = value[c * n + at : c * n + end]
                if to < base + size:
                    sent[4 * f + c, to : base + size] = jnp.zeros(
                        (base + size - to, rank), jnp.float32
                    )


def share_kernel(n_both, pair, out):
    rows = [pair[0, :n_both], pair[1, :n_both], pair[0, n_both:] + pair[1, n_both:]]
    value = jnp.concatenate(rows, axis=0)
    for i in range(out.shape[0]):
        out[i] = value


def interleaved(first, second, block):
    out, at, rows = [], 0, first.shape[0]
    while at < rows:
        n = min(block, rows - at)
        out += [first[at : at + n], second[at : at + n]]
        at += n
    return jnp.concatenate(out, axis=0)


def updated(carried, z):
    rank = z.shape[1]
    return carried[rank:] - kdot(z, carried[:rank])


def top_shared_kernel(n_both, width, gathered, other, out):
    half = out.shape[1] // 2
    n = half + 4 * n_both - width
    for c in range(2):
        both = get_rows(gathered, c * n_both, n_both)
        out[n * c : n * c + half] = both[:half]
        out[n * c + half : n * (c + 1)] = both[width:]
    out[2 * n :] = other[...]


def child_rows(shared, at, half, count, projections):
    own = jnp.concatenate([full_rows(shared, at, half), projections], axis=0)
    ops = [full_rows(shared, at + half * j, half) for j in range(1, count)]
    return own, jnp.concatenate(ops, axis=0)


def top_node_kernel(count, n_both, n_sums, gathered, shared, held, z_out, node_out, part, carried):
    rank = held.shape[1]
    half = rank // 2
    width = held.shape[0]
    core = bit_of("gy", 0)
    side = bit_of("gx", 0)
    children = []
    for which in (side, 1 - side):
        both = get_rows(gathered, times8(which, n_both), n_both)
        at = times8(which, half * count)
        children.append(child_rows(shared, at, half, count, both[half:width]))
    (own, ops_own), (sib, ops_sib) = children
    sums = get_rows(gathered, 2 * n_both, n_sums)
    z, node = solve_node(own, sib, ops_own, ops_sib, sums)
    z_out[...] = z
    node_out[...] = node
    n = part.shape[0]
    part[...] = node_out[pl.ds(times8((lax.axis_index("gy") >> 1) & 3, n), n)]
    swapped = [shared[c, 2 * half * count :] for c in range(2)]
    halves = [jnp.where(core == c, held[...], swapped[c]) for c in range(2)]
    carried[...] = interleaved(halves[0], halves[1], half)


def sibling_kernel(bit, pair, out):
    value = pair[1 - bit_of("gx", bit)]
    for i in range(out.shape[0]):
        out[i] = value


def quarter_shared_kernel(count, own, sib, z, out):
    half = out.shape[1] // 2
    width = own.shape[0] // count
    value = sib[...].reshape(own.shape)
    for j in range(count):
        at = slice(j * width, j * width + half)
        out[j * half : (j + 1) * half] = own[at]
        out[(count + j) * half : (count + j + 1) * half] = value[at]
    out[2 * count * half :] = z[...]


def quarter_node_kernel(count, own, sib, shared, carried, z_out, node_out, new):
    half = own.shape[1] // 2
    width = own.shape[0] // count
    here, there = own[...], sib[...].reshape(own.shape)
    rows_own, ops_own = child_rows(shared, 0, half, count, here[half:width])
    rows_sib, ops_sib = child_rows(shared, half * count, half, count, there[half:width])
    sums = jnp.concatenate(
        [
            here[j * width + half : (j + 1) * width] + there[j * width + half : (j + 1) * width]
            for j in range(1, count)
        ],
        axis=0,
    )
    z, node = solve_node(rows_own, rows_sib, ops_own, ops_sib, sums)
    z_out[...] = z
    node_out[...] = node
    below = both_cores(shared, 2 * count * half, shared.shape[1] - 2 * count * half)
    new[...] = updated(carried, interleaved(*below, half))


def whole_shared_kernel(bit, own, pair, z, out):
    rows = own.shape[0]
    out[:rows] = own[...]
    out[rows : 2 * rows] = pair[1 - bit_of("gx", bit)]
    out[2 * rows :] = z[...]


def whole_node_kernel(count, rows, shared, carried, node_out, new):
    half = carried.shape[1] // 2
    rank = 2 * half
    width = rows // count

    def child(at):
        return [
            interleaved(*both_cores(shared, at + j * width, width), half) for j in range(count)
        ]

    own, sib = child(0), child(rows)
    z, node = solve_node(
        own[0],
        sib[0],
        jnp.concatenate([v[:rank] for v in own[1:]], axis=0),
        jnp.concatenate([v[:rank] for v in sib[1:]], axis=0),
        jnp.concatenate([v[rank:] + w[rank:] for v, w in zip(own[1:], sib[1:])], axis=0),
    )
    node_out[...] = node
    below = both_cores(shared, 2 * rows, shared.shape[1] - 2 * rows)
    new[...] = updated(updated(carried, interleaved(*below, half)), z)


def last_kernel(bit, pair, carried, out):
    side = bit_of("gx", bit)
    rank = carried.shape[1]
    own, sib = pair[side], pair[1 - side]
    z = solve_own(own[:rank], sib[:rank], own[rank:], sib[rank:])
    out[...] = updated(carried, z)


def call(kernel, outs, *args):
    rows = sum(a.size // 128 for a in args)
    return pl.pallas_call(
        kernel,
        out_shape=[jax.ShapeDtypeStruct(o, jnp.float32) for o in outs],
        compiler_params=pltpu.CompilerParams(vmem_limit_bytes=VMEM_BYTES),
        cost_estimate=pl.CostEstimate(
            flops=6 * 128 * 128 * (rows + 14 * 128),
            bytes_accessed=512 * rows,
            transcendentals=0,
        ),
    )(*args)


def bit_groups(count, bits):
    mask = sum(1 << b for b in bits)
    return [
        [
            base | sum(((i >> q) & 1) << b for q, b in enumerate(bits))
            for i in range(1 << len(bits))
        ]
        for base in range(count)
        if not base & mask
    ]


def swap_cores(value):
    return lax.ppermute(value, "gy", [(s, s ^ 1) for s in range(lax.axis_size("gy"))])


def pair_gather(value, axis, bit, tiled=False):
    groups = bit_groups(lax.axis_size(axis), [bit])
    return lax.all_gather(value, axis, axis_index_groups=groups, tiled=tiled)


def exchange(value, axis, bits):
    count = lax.axis_size(axis)
    return lax.all_to_all(value, axis, 0, 0, axis_index_groups=bit_groups(count, bits))


def to_all(value, axis, bits):
    return exchange(jnp.broadcast_to(value, (1 << len(bits),) + value.shape), axis, bits)


def up8(value):
    return -(-value // 8) * 8


def shards(right_sides, factor_u, factor_v):
    levels, _, rank = factor_u.shape
    half = rank // 2
    near_chips = [1, 2]

    packed = jnp.concatenate(
        [factor_u.reshape(-1, rank), factor_v.reshape(-1, rank), right_sides.T], axis=0
    )
    rest = ((levels - 2) * rank + right_sides.shape[1]) // 2
    rows = 2 * rank + rest
    held, low, up, next_v, top_v = call(
        functools.partial(first_pair_kernel, levels),
        [
            (rows, 2 * rank),
            (rows, rank),
            (rows, rank),
            (2, 2 * rank, rank),
            (levels - 4, 2 * rank, rank),
        ],
        packed,
        swap_cores(packed),
    )
    z_low, node = call(
        functools.partial(first_node_kernel, 1),
        [(rank + rest, rank), (rank + rest, rank)],
        pair_gather(low, "gy", 1),
        up,
    )
    pair = pair_gather(node, "gy", 1)
    pair = pair_gather(pair[0] + pair[1], "gy", 2)

    rows = rest
    rest -= rank
    n_both, n_sums = (rows + half) // 4, (rows - half) // 4
    held, sent = call(
        functools.partial(between_kernel, 2, 4),
        [(rows, 2 * rank), (4, n_both + n_sums, rank)],
        pair,
        z_low,
        held,
        next_v,
    )
    piece = exchange(sent, "gy", near_chips).sum(axis=0)
    share = call(
        functools.partial(share_kernel, n_both),
        [(4, 2 * n_both + n_sums, rank)],
        pair_gather(piece, "gy", 3),
    )[0]
    pieces = exchange(share, "gy", near_chips)
    shared = call(
        functools.partial(second_shared_kernel, n_both, n_sums, rows),
        [(11 * half, rank)],
        pieces,
        held,
    )[0]
    shared = pair_gather(shared, "gy", 0)
    z_low, node = call(
        functools.partial(second_node_kernel, 3, n_both, n_sums, rows),
        [(rank + rest, rank), (rank + rest, rank)],
        pieces,
        shared,
    )

    count = levels - 4
    n_both = (rest + (count - 1) * half) // 4
    n_sums = (count - 1) * (rest - half) // 4
    s_both, s_sums = up8(-(-n_both // 8)), up8(-(-n_sums // 8))
    mine, other, sent = call(
        functools.partial(upper_kernel, 4, s_both),
        [(rest, rank), (rest, rank), (32, s_both + s_sums, rank)],
        pair_gather(node, "gy", 4),
        z_low,
        shared,
        held,
        top_v,
    )
    far = [3, 4, 5]
    sides = exchange(sent, ("gx", "gy"), near_chips + far)
    sides = sides.reshape((2, 16) + sides.shape[1:]).sum(axis=1)
    share = jnp.concatenate(
        [sides[0, :s_both], sides[1, :s_both], sides[0, s_both:] + sides[1, s_both:]], axis=0
    )
    pieces = to_all(share, ("gx", "gy"), far)
    share = jnp.concatenate(
        [
            pieces[:, :s_both].reshape(-1, rank)[:n_both],
            pieces[:, s_both : 2 * s_both].reshape(-1, rank)[:n_both],
            pieces[:, 2 * s_both :].reshape(-1, rank)[:n_sums],
        ],
        axis=0,
    )
    gathered = to_all(share, "gy", near_chips)
    shared = call(
        functools.partial(top_shared_kernel, n_both, rest),
        [(2 * count * half + rest, rank)],
        gathered,
        other,
    )[0]
    width = rest - half
    z, node, part, carried = call(
        functools.partial(top_node_kernel, count, n_both, n_sums),
        [
            (width, rank),
            ((count - 1) * width, rank),
            ((count - 1) * width // 4, rank),
            (2 * rest, rank),
        ],
        gathered,
        pair_gather(shared, "gy", 0),
        mine,
    )

    count -= 1
    rows = 2 * rest
    near = call(
        functools.partial(sibling_kernel, 1), [(4,) + part.shape], pair_gather(part, "gx", 1)
    )[0]
    near = exchange(near, "gy", near_chips)
    shared = call(
        functools.partial(quarter_shared_kernel, count),
        [(2 * count * half + width, rank)],
        node,
        near,
        z,
    )[0]
    width -= half
    rows -= rank
    z, node, carried = call(
        functools.partial(quarter_node_kernel, count),
        [(width, rank), ((count - 1) * width, rank), (rows, rank)],
        node,
        near,
        pair_gather(shared, "gy", 0),
        carried,
    )

    count -= 1
    shared = call(
        functools.partial(whole_shared_kernel, 2),
        [(2 * node.shape[0] + width, rank)],
        node,
        pair_gather(node, "gx", 2),
        z,
    )[0]
    rows -= 2 * rank
    node, carried = call(
        functools.partial(whole_node_kernel, count, node.shape[0]),
        [((count - 1) * rows, rank), (rows, rank)],
        pair_gather(shared, "gy", 0),
        carried,
    )

    return call(
        functools.partial(last_kernel, 3),
        [right_sides.shape[::-1]],
        pair_gather(node, "gx", 3),
        carried,
    )[0].T


def solution(mesh):
    placed = (P(("gx", "gy"), None), P(None, ("gx", "gy"), None), P(None, ("gx", "gy"), None))
    return jax.shard_map(
        shards, mesh=mesh, in_specs=placed, out_specs=P(("gx", "gy"), None), check_vma=False
    )
```

```python
import functools

import jax
import jax.numpy as jnp
from jax import lax
from jax.experimental import pallas as pl
from jax.experimental.pallas import tpu as pltpu
from jax.sharding import PartitionSpec as P

VMEM_BYTES = 40 * 2**20


def split(value):
    high = value.astype(jnp.bfloat16)
    low = (value - high.astype(jnp.float32)).astype(jnp.bfloat16)
    return high, low


def dot_split(a, b):
    def part(x, y):
        return jnp.dot(x, y, preferred_element_type=jnp.float32)

    return part(a[0], b[0]) + (part(a[0], b[1]) + part(a[1], b[0]))


def kdot(a, b):
    return dot_split(split(a), split(b))


def inverse_of(error):
    total = jnp.eye(error.shape[0], dtype=jnp.float32) + error
    power = error
    for step in range(6):
        parts = split(power)
        power = dot_split(parts, parts)
        total = total + kdot(total, power)
    return total


def solve_own(gram_own, gram_sib, proj_own, proj_sib):
    inverse = inverse_of(kdot(gram_own, gram_sib))
    return kdot(proj_sib - kdot(proj_own, gram_sib), inverse)


def solve_node(own, sib, ops_own, ops_sib, sums):
    rank = own.shape[1]
    width = own.shape[0] - rank
    gram_own, proj_own = split(own[:rank]), split(own[rank:])
    base, lefts = [], []
    for j in range(ops_own.shape[0] // rank):
        at = slice(j * rank, (j + 1) * rank)
        op_sib = split(ops_sib[at])
        base.append(sums[j * width : (j + 1) * width] - dot_split(proj_own, op_sib))
        lefts.append(split(ops_own[at] - dot_split(gram_own, op_sib)))
    z = solve_own(own[:rank], sib[:rank], own[rank:], sib[rank:])
    parts = split(z)
    node = [b - dot_split(parts, left) for b, left in zip(base, lefts)]
    return z, jnp.concatenate(node, axis=0)


def put_rows(out, base, size, start, value):
    at, rows = 0, value.shape[0]
    while at < rows:
        i, r = divmod(start + at, size)
        n = min(size - r, rows - at)
        out[i, base + r : base + r + n] = value[at : at + n]
        at += n


def get_rows(ref, base, size):
    return jnp.concatenate([ref[i, pl.ds(base, size)] for i in range(ref.shape[0])], axis=0)


def bit_of(axis, bit):
    return (lax.axis_index(axis) >> bit) & 1


def times8(value, rows):
    return pl.multiple_of(value * rows, 8)


def first_pair_kernel(levels, mine, other, held, low, up, next_v, top_v):
    rank = mine.shape[1]
    half = rank // 2
    core = bit_of("gy", 0)
    last = (mine.shape[0] - 2 * levels * rank) // 2
    rows = pl.ds(2 * levels * rank + times8(core, last), last)
    for c, ref in enumerate((mine, other)):
        lane = slice(c * rank, (c + 1) * rank)
        for j in range(levels):
            value = ref[j * rank : (j + 1) * rank].T
            if j < 2:
                held[j * rank : (j + 1) * rank, lane] = value
            else:
                at = 2 * rank + (j - 2) * half
                held[at : at + half, lane] = jnp.where(core == 0, value[:half], value[half:])
        held[held.shape[0] - last :, lane] = ref[rows]
    factors = [
        jnp.concatenate([ref[j * rank : (j + 1) * rank] for ref in (mine, other)], axis=0)
        for j in range(levels, 2 * levels)
    ]
    parts = split(held[...])
    low[...] = dot_split(parts, split(factors[0]))
    up[...] = dot_split(parts, split(factors[1]))
    for j in range(2, 4):
        next_v[j - 2] = factors[j]
    for j in range(4, levels):
        top_v[j - 4] = factors[j]


def first_node_kernel(bit, pair, up, z_out, out):
    side = bit_of("gy", bit)
    rank = up.shape[1]
    own, sib = pair[side], pair[1 - side]
    z = solve_own(own[:rank], sib[:rank], own[rank:], sib[rank:])
    z_out[...] = z
    out[...] = up[rank:] - kdot(z, up[:rank])


def after_pair(own, sib, z_low, held):
    rank = own.shape[1]
    z_up = solve_own(own[:rank], sib[:rank], own[rank:], sib[rank:])
    left = held[:rank]
    next_left = held[rank : 2 * rank] - kdot(z_low[:rank], left)
    z_both = jnp.concatenate([z_low[rank:], z_up], axis=1)
    return held[2 * rank :] - kdot(z_both, jnp.concatenate([left, next_left], axis=0))


def between_kernel(bit, shares, pair, z_low, held, v, rest, sent):
    side = bit_of("gy", bit)
    value = after_pair(pair[side], pair[1 - side], z_low, held)
    rest[...] = value
    rows = value.shape[0]
    half = v.shape[2] // 2
    parts = split(value)
    low = dot_split(parts, split(v[0]))
    up = dot_split(parts, split(v[1]))
    n_both = (rows + half) // shares
    put_rows(sent, 0, n_both, 0, low)
    put_rows(sent, 0, n_both, rows, up[:half])
    put_rows(sent, n_both, (rows - half) // shares, 0, up[half:])


def second_shared_kernel(n_both, n_sums, rows, pieces, rest, out):
    rank = out.shape[1]
    half = rank // 2
    for c in range(2):
        both = get_rows(pieces, c * n_both, n_both)
        out[3 * half * c : 3 * half * c + rank] = both[:rank]
        out[3 * half * c + rank : 3 * half * (c + 1)] = both[rows:]
    out[6 * half : 7 * half] = get_rows(pieces, 2 * n_both, n_sums)[:half]
    out[7 * half : 9 * half] = rest[:rank, :rank]
    out[9 * half : 11 * half] = rest[:rank, rank:]


def both_cores(ref, at, n):
    return [ref[c, pl.ds(at, n)] for c in range(2)]


def full_rows(ref, at, n):
    return jnp.concatenate(both_cores(ref, at, n), axis=0)


def second_node_kernel(bit, n_both, n_sums, rows, pieces, shared, z_out, node_out):
    side = bit_of("gy", bit)
    rank = z_out.shape[1]
    half = rank // 2
    children = []
    for which in (side, 1 - side):
        at = times8(which, 3 * half)
        both = get_rows(pieces, times8(which, n_both), n_both)
        children.append(
            (
                jnp.concatenate(
                    [
                        full_rows(shared, at, half),
                        full_rows(shared, at + half, half),
                        both[rank:rows],
                    ],
                    axis=0,
                ),
                full_rows(shared, at + rank, half),
            )
        )
    (own, ops_own), (sib, ops_sib) = children
    sums = get_rows(pieces, 2 * n_both, n_sums)
    sums = jnp.concatenate([full_rows(shared, 6 * half, half), sums[half:]], axis=0)
    z, node = solve_node(own, sib, ops_own, ops_sib, sums)
    z_out[...] = z
    node_out[...] = node


def upper_kernel(bit, s_both, pair, z_low, shared, rest, v, mine, other, sent):
    rank = v.shape[2]
    half = rank // 2
    core = bit_of("gy", 0)
    factors = []
    for c in range(2):
        a, b = shared[c, 7 * half : 9 * half], shared[c, 9 * half : 11 * half]
        here = core == c
        factors.append(
            jnp.concatenate([jnp.where(here, a, b), jnp.where(here, b, a)], axis=1)
        )
    held = jnp.concatenate(
        [factors[0][:half], factors[1][:half], factors[0][half:], factors[1][half:], rest[rank:]],
        axis=0,
    )
    side = bit_of("gy", bit)
    value = after_pair(pair[side], pair[1 - side], z_low, held)
    mine[...] = value[:, :rank]
    other[...] = value[:, rank:]
    count, width = v.shape[0], value.shape[0]
    parts = split(value)
    rows = [dot_split(parts, split(v[j])) for j in range(count)]
    both = jnp.concatenate([rows[0]] + [r[:half] for r in rows[1:]], axis=0)
    sums = jnp.concatenate([r[half:] for r in rows[1:]], axis=0)
    far = sent.shape[0] // 4
    for value, base, size in ((both, 0, s_both), (sums, s_both, sent.shape[1] - s_both)):
        n = value.shape[0] // 4
        for c in range(4):
            for f in range(far):
                at, end = min(f * size, n), min((f + 1) * size, n)
                to = base + end - at
                if end > at:
                    sent[4 * f + c, base:to] = value[c * n + at : c * n + end]
                if to < base + size:
                    sent[4 * f + c, to : base + size] = jnp.zeros(
                        (base + size - to, rank), jnp.float32
                    )


def share_kernel(n_both, pair, out):
    rows = [pair[0, :n_both], pair[1, :n_both], pair[0, n_both:] + pair[1, n_both:]]
    value = jnp.concatenate(rows, axis=0)
    for i in range(out.shape[0]):
        out[i] = value


def interleaved(first, second, block):
    out, at, rows = [], 0, first.shape[0]
    while at < rows:
        n = min(block, rows - at)
        out += [first[at : at + n], second[at : at + n]]
        at += n
    return jnp.concatenate(out, axis=0)


def updated(carried, z):
    rank = z.shape[1]
    return carried[rank:] - kdot(z, carried[:rank])


def top_shared_kernel(n_both, width, gathered, other, out):
    half = out.shape[1] // 2
    n = half + 4 * n_both - width
    for c in range(2):
        both = get_rows(gathered, c * n_both, n_both)
        out[n * c : n * c + half] = both[:half]
        out[n * c + half : n * (c + 1)] = both[width:]
    out[2 * n :] = other[...]


def child_rows(shared, at, half, count, projections):
    own = jnp.concatenate([full_rows(shared, at, half), projections], axis=0)
    ops = [full_rows(shared, at + half * j, half) for j in range(1, count)]
    return own, jnp.concatenate(ops, axis=0)


def top_node_kernel(count, n_both, n_sums, gathered, shared, held, z_out, node_out, part, carried):
    rank = held.shape[1]
    half = rank // 2
    width = held.shape[0]
    core = bit_of("gy", 0)
    side = bit_of("gx", 0)
    children = []
    for which in (side, 1 - side):
        both = get_rows(gathered, times8(which, n_both), n_both)
        at = times8(which, half * count)
        children.append(child_rows(shared, at, half, count, both[half:width]))
    (own, ops_own), (sib, ops_sib) = children
    sums = get_rows(gathered, 2 * n_both, n_sums)
    z, node = solve_node(own, sib, ops_own, ops_sib, sums)
    z_out[...] = z
    node_out[...] = node
    n = part.shape[0]
    part[...] = node_out[pl.ds(times8(((lax.axis_index("gy") >> 1) & 3) ^ 1, n), n)]
    swapped = [shared[c, 2 * half * count :] for c in range(2)]
    halves = [jnp.where(core == c, held[...], swapped[c]) for c in range(2)]
    carried[...] = interleaved(halves[0], halves[1], half)


def sibling_kernel(bit, pair, out):
    value = pair[1 - bit_of("gx", bit)]
    for i in range(out.shape[0]):
        out[i] = value


def quarter_shared_kernel(count, own, sib, z, out):
    half = out.shape[1] // 2
    width = own.shape[0] // count
    value = sib[...].reshape(own.shape)
    for j in range(count):
        at = slice(j * width, j * width + half)
        out[j * half : (j + 1) * half] = own[at]
        out[(count + j) * half : (count + j + 1) * half] = value[at]
    out[2 * count * half :] = z[...]


def quarter_node_kernel(count, own, sib, shared, carried, z_out, node_out, new):
    half = own.shape[1] // 2
    width = own.shape[0] // count
    here, there = own[...], sib[...].reshape(own.shape)
    rows_own, ops_own = child_rows(shared, 0, half, count, here[half:width])
    rows_sib, ops_sib = child_rows(shared, half * count, half, count, there[half:width])
    sums = jnp.concatenate(
        [
            here[j * width + half : (j + 1) * width] + there[j * width + half : (j + 1) * width]
            for j in range(1, count)
        ],
        axis=0,
    )
    z, node = solve_node(rows_own, rows_sib, ops_own, ops_sib, sums)
    z_out[...] = z
    node_out[...] = node
    below = both_cores(shared, 2 * count * half, shared.shape[1] - 2 * count * half)
    new[...] = updated(carried, interleaved(*below, half))


def whole_shared_kernel(bit, own, pair, z, out):
    rows = own.shape[0]
    out[:rows] = own[...]
    out[rows : 2 * rows] = pair[1 - bit_of("gx", bit)]
    out[2 * rows :] = z[...]


def whole_node_kernel(count, rows, shared, carried, node_out, new):
    half = carried.shape[1] // 2
    rank = 2 * half
    width = rows // count

    def child(at):
        return [
            interleaved(*both_cores(shared, at + j * width, width), half) for j in range(count)
        ]

    own, sib = child(0), child(rows)
    z, node = solve_node(
        own[0],
        sib[0],
        jnp.concatenate([v[:rank] for v in own[1:]], axis=0),
        jnp.concatenate([v[:rank] for v in sib[1:]], axis=0),
        jnp.concatenate([v[rank:] + w[rank:] for v, w in zip(own[1:], sib[1:])], axis=0),
    )
    node_out[...] = node
    below = both_cores(shared, 2 * rows, shared.shape[1] - 2 * rows)
    new[...] = updated(updated(carried, interleaved(*below, half)), z)


def last_kernel(bit, pair, carried, out):
    side = bit_of("gx", bit)
    rank = carried.shape[1]
    own, sib = pair[side], pair[1 - side]
    z = solve_own(own[:rank], sib[:rank], own[rank:], sib[rank:])
    out[...] = updated(carried, z)


def call(kernel, outs, *args):
    rows = sum(a.size // 128 for a in args)
    return pl.pallas_call(
        kernel,
        out_shape=[jax.ShapeDtypeStruct(o, jnp.float32) for o in outs],
        compiler_params=pltpu.CompilerParams(vmem_limit_bytes=VMEM_BYTES),
        cost_estimate=pl.CostEstimate(
            flops=6 * 128 * 128 * (rows + 14 * 128),
            bytes_accessed=512 * rows,
            transcendentals=0,
        ),
    )(*args)


def bit_groups(count, bits):
    mask = sum(1 << b for b in bits)
    return [
        [
            base | sum(((i >> q) & 1) << b for q, b in enumerate(bits))
            for i in range(1 << len(bits))
        ]
        for base in range(count)
        if not base & mask
    ]


def swap_cores(value):
    return lax.ppermute(value, "gy", [(s, s ^ 1) for s in range(lax.axis_size("gy"))])


def pair_gather(value, axis, bit, also=()):
    mask = sum(1 << b for b in (bit, *also))
    groups = [[d, d ^ mask] for d in range(lax.axis_size(axis)) if not (d >> bit) & 1]
    return lax.all_gather(value, axis, axis_index_groups=groups)


def exchange(value, axis, bits):
    count = lax.axis_size(axis)
    return lax.all_to_all(value, axis, 0, 0, axis_index_groups=bit_groups(count, bits))


def to_all(value, axis, bits):
    return exchange(jnp.broadcast_to(value, (1 << len(bits),) + value.shape), axis, bits)


def up8(value):
    return -(-value // 8) * 8


def shards(right_sides, factor_u, factor_v):
    levels, _, rank = factor_u.shape
    half = rank // 2
    near_chips = [1, 2]

    packed = jnp.concatenate(
        [factor_u.reshape(-1, rank), factor_v.reshape(-1, rank), right_sides.T], axis=0
    )
    rest = ((levels - 2) * rank + right_sides.shape[1]) // 2
    rows = 2 * rank + rest
    held, low, up, next_v, top_v = call(
        functools.partial(first_pair_kernel, levels),
        [
            (rows, 2 * rank),
            (rows, rank),
            (rows, rank),
            (2, 2 * rank, rank),
            (levels - 4, 2 * rank, rank),
        ],
        packed,
        swap_cores(packed),
    )
    z_low, node = call(
        functools.partial(first_node_kernel, 1),
        [(rank + rest, rank), (rank + rest, rank)],
        pair_gather(low, "gy", 1),
        up,
    )
    pair = pair_gather(node, "gy", 1)
    pair = pair_gather(pair[0] + pair[1], "gy", 2)

    rows = rest
    rest -= rank
    n_both, n_sums = (rows + half) // 4, (rows - half) // 4
    held, sent = call(
        functools.partial(between_kernel, 2, 4),
        [(rows, 2 * rank), (4, n_both + n_sums, rank)],
        pair,
        z_low,
        held,
        next_v,
    )
    piece = exchange(sent, "gy", near_chips).sum(axis=0)
    share = call(
        functools.partial(share_kernel, n_both),
        [(4, 2 * n_both + n_sums, rank)],
        pair_gather(piece, "gy", 3),
    )[0]
    pieces = exchange(share, "gy", near_chips)
    shared = call(
        functools.partial(second_shared_kernel, n_both, n_sums, rows),
        [(11 * half, rank)],
        pieces,
        held,
    )[0]
    shared = pair_gather(shared, "gy", 0)
    z_low, node = call(
        functools.partial(second_node_kernel, 3, n_both, n_sums, rows),
        [(rank + rest, rank), (rank + rest, rank)],
        pieces,
        shared,
    )

    count = levels - 4
    n_both = (rest + (count - 1) * half) // 4
    n_sums = (count - 1) * (rest - half) // 4
    s_both, s_sums = up8(-(-n_both // 8)), up8(-(-n_sums // 8))
    mine, other, sent = call(
        functools.partial(upper_kernel, 4, s_both),
        [(rest, rank), (rest, rank), (32, s_both + s_sums, rank)],
        pair_gather(node, "gy", 4, (2, 3)),
        z_low,
        shared,
        held,
        top_v,
    )
    far = [3, 4, 5]
    sides = exchange(sent, ("gx", "gy"), near_chips + far)
    sides = sides.reshape((2, 16) + sides.shape[1:]).sum(axis=1)
    share = jnp.concatenate(
        [sides[0, :s_both], sides[1, :s_both], sides[0, s_both:] + sides[1, s_both:]], axis=0
    )
    pieces = to_all(share, ("gx", "gy"), far)
    share = jnp.concatenate(
        [
            pieces[:, :s_both].reshape(-1, rank)[:n_both],
            pieces[:, s_both : 2 * s_both].reshape(-1, rank)[:n_both],
            pieces[:, 2 * s_both :].reshape(-1, rank)[:n_sums],
        ],
        axis=0,
    )
    gathered = to_all(share, "gy", near_chips)
    shared = call(
        functools.partial(top_shared_kernel, n_both, rest),
        [(2 * count * half + rest, rank)],
        gathered,
        other,
    )[0]
    width = rest - half
    z, node, part, carried = call(
        functools.partial(top_node_kernel, count, n_both, n_sums),
        [
            (width, rank),
            ((count - 1) * width, rank),
            ((count - 1) * width // 4, rank),
            (2 * rest, rank),
        ],
        gathered,
        pair_gather(shared, "gy", 0),
        mine,
    )

    count -= 1
    rows = 2 * rest
    near = call(
        functools.partial(sibling_kernel, 1), [(4,) + part.shape], pair_gather(part, ("gx", "gy"), 6, (5, 1))
    )[0]
    near = exchange(near, "gy", near_chips)
    shared = call(
        functools.partial(quarter_shared_kernel, count),
        [(2 * count * half + width, rank)],
        node,
        near,
        z,
    )[0]
    width -= half
    rows -= rank
    z, node, carried = call(
        functools.partial(quarter_node_kernel, count),
        [(width, rank), ((count - 1) * width, rank), (rows, rank)],
        node,
        near,
        pair_gather(shared, "gy", 0),
        carried,
    )

    count -= 1
    shared = call(
        functools.partial(whole_shared_kernel, 2),
        [(2 * node.shape[0] + width, rank)],
        node,
        pair_gather(node, "gx", 2),
        z,
    )[0]
    rows -= 2 * rank
    node, carried = call(
        functools.partial(whole_node_kernel, count, node.shape[0]),
        [((count - 1) * rows, rank), (rows, rank)],
        pair_gather(shared, "gy", 0),
        carried,
    )

    return call(
        functools.partial(last_kernel, 3),
        [right_sides.shape[::-1]],
        pair_gather(node, "gx", 3, (2,)),
        carried,
    )[0].T


def solution(mesh):
    placed = (P(("gx", "gy"), None), P(None, ("gx", "gy"), None), P(None, ("gx", "gy"), None))
    return jax.shard_map(
        shards, mesh=mesh, in_specs=placed, out_specs=P(("gx", "gy"), None), check_vma=False
    )
```

```python
import functools

import jax
import jax.numpy as jnp
from jax import lax
from jax.experimental import pallas as pl
from jax.experimental.pallas import tpu as pltpu
from jax.sharding import PartitionSpec as P

VMEM_BYTES = 40 * 2**20


def split(value):
    high = value.astype(jnp.bfloat16)
    low = (value - high.astype(jnp.float32)).astype(jnp.bfloat16)
    return high, low


def dot_split(a, b):
    def part(x, y):
        return jnp.dot(x, y, preferred_element_type=jnp.float32)

    return part(a[0], b[0]) + (part(a[0], b[1]) + part(a[1], b[0]))


def kdot(a, b):
    return dot_split(split(a), split(b))


def inverse_of(error):
    total = jnp.eye(error.shape[0], dtype=jnp.float32) + error
    power = error
    for step in range(6):
        parts = split(power)
        power = dot_split(parts, parts)
        total = total + kdot(total, power)
    return total


def solve_own(gram_own, gram_sib, proj_own, proj_sib):
    inverse = inverse_of(kdot(gram_own, gram_sib))
    return kdot(proj_sib - kdot(proj_own, gram_sib), inverse)


def solve_node(own, sib, ops_own, ops_sib, sums):
    rank = own.shape[1]
    width = own.shape[0] - rank
    gram_own, proj_own = split(own[:rank]), split(own[rank:])
    base, lefts = [], []
    for j in range(ops_own.shape[0] // rank):
        at = slice(j * rank, (j + 1) * rank)
        op_sib = split(ops_sib[at])
        base.append(sums[j * width : (j + 1) * width] - dot_split(proj_own, op_sib))
        lefts.append(split(ops_own[at] - dot_split(gram_own, op_sib)))
    z = solve_own(own[:rank], sib[:rank], own[rank:], sib[rank:])
    parts = split(z)
    node = [b - dot_split(parts, left) for b, left in zip(base, lefts)]
    return z, jnp.concatenate(node, axis=0)


def put_rows(out, base, size, start, value):
    at, rows = 0, value.shape[0]
    while at < rows:
        i, r = divmod(start + at, size)
        n = min(size - r, rows - at)
        out[i, base + r : base + r + n] = value[at : at + n]
        at += n


def get_rows(ref, base, size):
    return jnp.concatenate([ref[i, pl.ds(base, size)] for i in range(ref.shape[0])], axis=0)


def bit_of(axis, bit):
    return (lax.axis_index(axis) >> bit) & 1


def times8(value, rows):
    return pl.multiple_of(value * rows, 8)


def first_pair_kernel(levels, mine, other, held, low, up, next_v, top_v):
    rank = mine.shape[1]
    half = rank // 2
    core = bit_of("gy", 0)
    last = (mine.shape[0] - 2 * levels * rank) // 2
    rows = pl.ds(2 * levels * rank + times8(core, last), last)
    for c, ref in enumerate((mine, other)):
        lane = slice(c * rank, (c + 1) * rank)
        for j in range(levels):
            value = ref[j * rank : (j + 1) * rank].T
            if j < 2:
                held[j * rank : (j + 1) * rank, lane] = value
            else:
                at = 2 * rank + (j - 2) * half
                held[at : at + half, lane] = jnp.where(core == 0, value[:half], value[half:])
        held[held.shape[0] - last :, lane] = ref[rows]
    factors = [
        jnp.concatenate([ref[j * rank : (j + 1) * rank] for ref in (mine, other)], axis=0)
        for j in range(levels, 2 * levels)
    ]
    parts = split(held[...])
    low[...] = dot_split(parts, split(factors[0]))
    up[...] = dot_split(parts, split(factors[1]))
    for j in range(2, 4):
        next_v[j - 2] = factors[j]
    for j in range(4, levels):
        top_v[j - 4] = factors[j]


def first_node_kernel(bit, pair, up, z_out, out):
    side = bit_of("gy", bit)
    rank = up.shape[1]
    own, sib = pair[side], pair[1 - side]
    z = solve_own(own[:rank], sib[:rank], own[rank:], sib[rank:])
    z_out[...] = z
    out[...] = up[rank:] - kdot(z, up[:rank])


def after_pair(own, sib, z_low, held):
    rank = own.shape[1]
    z_up = solve_own(own[:rank], sib[:rank], own[rank:], sib[rank:])
    left = held[:rank]
    next_left = held[rank : 2 * rank] - kdot(z_low[:rank], left)
    z_both = jnp.concatenate([z_low[rank:], z_up], axis=1)
    return held[2 * rank :] - kdot(z_both, jnp.concatenate([left, next_left], axis=0))


def between_kernel(bit, shares, pair, z_low, held, v, rest, sent):
    side = bit_of("gy", bit)
    value = after_pair(pair[side], pair[1 - side], z_low, held)
    rest[...] = value
    rows = value.shape[0]
    half = v.shape[2] // 2
    parts = split(value)
    low = dot_split(parts, split(v[0]))
    up = dot_split(parts, split(v[1]))
    n_both = (rows + half) // shares
    put_rows(sent, 0, n_both, 0, low)
    put_rows(sent, 0, n_both, rows, up[:half])
    put_rows(sent, n_both, (rows - half) // shares, 0, up[half:])


def second_shared_kernel(n_both, n_sums, rows, pieces, rest, out):
    rank = out.shape[1]
    half = rank // 2
    for c in range(2):
        both = get_rows(pieces, c * n_both, n_both)
        out[3 * half * c : 3 * half * c + rank] = both[:rank]
        out[3 * half * c + rank : 3 * half * (c + 1)] = both[rows:]
    out[6 * half : 7 * half] = get_rows(pieces, 2 * n_both, n_sums)[:half]
    out[7 * half : 9 * half] = rest[:rank, :rank]
    out[9 * half : 11 * half] = rest[:rank, rank:]


def both_cores(ref, at, n):
    return [ref[c, pl.ds(at, n)] for c in range(2)]


def full_rows(ref, at, n):
    return jnp.concatenate(both_cores(ref, at, n), axis=0)


def second_node_kernel(bit, n_both, n_sums, rows, pieces, shared, z_out, node_out):
    side = bit_of("gy", bit)
    rank = z_out.shape[1]
    half = rank // 2
    children = []
    for which in (side, 1 - side):
        at = times8(which, 3 * half)
        both = get_rows(pieces, times8(which, n_both), n_both)
        children.append(
            (
                jnp.concatenate(
                    [
                        full_rows(shared, at, half),
                        full_rows(shared, at + half, half),
                        both[rank:rows],
                    ],
                    axis=0,
                ),
                full_rows(shared, at + rank, half),
            )
        )
    (own, ops_own), (sib, ops_sib) = children
    sums = get_rows(pieces, 2 * n_both, n_sums)
    sums = jnp.concatenate([full_rows(shared, 6 * half, half), sums[half:]], axis=0)
    z, node = solve_node(own, sib, ops_own, ops_sib, sums)
    z_out[...] = z
    node_out[...] = node


def next_level_rows(rows, half):
    both = jnp.concatenate([rows[0]] + [r[:half] for r in rows[1:]], axis=0)
    return both, jnp.concatenate([r[half:] for r in rows[1:]], axis=0)


def quarter(value, c):
    n = value.shape[0] // 4
    return value[c * n : (c + 1) * n]


def upper_kernel(bit, s_both, pair, z_low, shared, rest, v, mine, other, sent):
    rank = v.shape[2]
    half = rank // 2
    core = bit_of("gy", 0)
    factors = []
    for c in range(2):
        a, b = shared[c, 7 * half : 9 * half], shared[c, 9 * half : 11 * half]
        here = core == c
        factors.append(
            jnp.concatenate([jnp.where(here, a, b), jnp.where(here, b, a)], axis=1)
        )
    held = jnp.concatenate(
        [factors[0][:half], factors[1][:half], factors[0][half:], factors[1][half:], rest[rank:]],
        axis=0,
    )
    side = bit_of("gy", bit)
    value = after_pair(pair[side], pair[1 - side], z_low, held)
    mine[...] = value[:, :rank]
    other[...] = value[:, rank:]
    count, width = v.shape[0], value.shape[0]
    parts = split(value)
    rows = [dot_split(parts, split(v[j])) for j in range(count)]
    both = jnp.concatenate([rows[0]] + [r[:half] for r in rows[1:]], axis=0)
    rest_rows = [r[half:] for r in rows[1:]]
    next_both, next_sums = next_level_rows(rest_rows, half)
    sums = jnp.concatenate(
        [v for c in range(4) for v in (quarter(next_both, c), quarter(next_sums, c))], axis=0
    )
    far = sent.shape[0] // 4
    for value, base, size in ((both, 0, s_both), (sums, s_both, sent.shape[1] - s_both)):
        n = value.shape[0] // 4
        for c in range(4):
            for f in range(far):
                at, end = min(f * size, n), min((f + 1) * size, n)
                to = base + end - at
                if end > at:
                    sent[4 * f + c, base:to] = value[c * n + at : c * n + end]
                if to < base + size:
                    sent[4 * f + c, to : base + size] = jnp.zeros(
                        (base + size - to, rank), jnp.float32
                    )


def share_kernel(n_both, pair, out):
    rows = [pair[0, :n_both], pair[1, :n_both], pair[0, n_both:] + pair[1, n_both:]]
    value = jnp.concatenate(rows, axis=0)
    for i in range(out.shape[0]):
        out[i] = value


def interleaved(first, second, block):
    out, at, rows = [], 0, first.shape[0]
    while at < rows:
        n = min(block, rows - at)
        out += [first[at : at + n], second[at : at + n]]
        at += n
    return jnp.concatenate(out, axis=0)


def updated(carried, z):
    rank = z.shape[1]
    return carried[rank:] - kdot(z, carried[:rank])


def top_shared_kernel(n_both, width, gathered, other, out):
    half = out.shape[1] // 2
    n = half + 4 * n_both - width
    for c in range(2):
        both = get_rows(gathered, c * n_both, n_both)
        out[n * c : n * c + half] = both[:half]
        out[n * c + half : n * (c + 1)] = both[width:]
    out[2 * n :] = other[...]


def child_rows(shared, at, half, count, projections):
    own = jnp.concatenate([full_rows(shared, at, half), projections], axis=0)
    ops = [full_rows(shared, at + half * j, half) for j in range(1, count)]
    return own, jnp.concatenate(ops, axis=0)


def half_children(bit, count, n_both, width, gathered, shared):
    half = gathered.shape[2] // 2
    side = bit_of("gx", bit)
    out = []
    for which in (side, 1 - side):
        both = get_rows(gathered, times8(which, n_both), n_both)
        at = times8(which, half * count)
        out.append(child_rows(shared, at, half, count, both[half:width]))
    return out


def top_node_kernel(count, n_both, gathered, shared, held, sums, z_out, part, carried, change):
    rank = held.shape[1]
    half = rank // 2
    width = held.shape[0]
    core = bit_of("gy", 0)
    (own, ops_own), (sib, ops_sib) = half_children(0, count, n_both, width, gathered, shared)
    nothing = jnp.zeros(change.shape, jnp.float32)
    z, node = solve_node(own, sib, ops_own, ops_sib, nothing)
    z_out[...] = z
    w = width - half
    both, rest = next_level_rows([node[j * w : (j + 1) * w] for j in range(count - 1)], half)
    change[: both.shape[0]] = both
    change[both.shape[0] :] = rest
    at = (lax.axis_index("gy") >> 1) & 3
    n, m = both.shape[0] // 4, rest.shape[0] // 4
    part[:n] = sums[:n] + change[pl.ds(times8(at, n), n)]
    part[n:] = sums[n:] + change[pl.ds(both.shape[0] + times8(at, m), m)]
    swapped = [shared[c, 2 * half * count :] for c in range(2)]
    halves = [jnp.where(core == c, held[...], swapped[c]) for c in range(2)]
    carried[...] = interleaved(halves[0], halves[1], half)


def quarter_node_kernel(count, n_both, gathered, shared, carried, z_out, node_out, new):
    half = gathered.shape[2] // 2
    width = z_out.shape[0] + half
    (own, ops_own), (sib, ops_sib) = half_children(1, count, n_both, width, gathered, shared)
    sums = get_rows(gathered, 2 * n_both, gathered.shape[1] - 2 * n_both)
    z, node = solve_node(own, sib, ops_own, ops_sib, sums)
    z_out[...] = z
    node_out[...] = node
    below = both_cores(shared, 2 * count * half, shared.shape[1] - 2 * count * half)
    new[...] = updated(carried, interleaved(*below, half))


def whole_shared_kernel(bit, own, pair, z, out):
    rows = own.shape[0]
    out[:rows] = own[...]
    out[rows : 2 * rows] = pair[1 - bit_of("gx", bit)]
    out[2 * rows :] = z[...]


def whole_node_kernel(count, rows, shared, carried, node_out, new):
    half = carried.shape[1] // 2
    rank = 2 * half
    width = rows // count

    def child(at):
        return [
            interleaved(*both_cores(shared, at + j * width, width), half) for j in range(count)
        ]

    own, sib = child(0), child(rows)
    z, node = solve_node(
        own[0],
        sib[0],
        jnp.concatenate([v[:rank] for v in own[1:]], axis=0),
        jnp.concatenate([v[:rank] for v in sib[1:]], axis=0),
        jnp.concatenate([v[rank:] + w[rank:] for v, w in zip(own[1:], sib[1:])], axis=0),
    )
    node_out[...] = node
    below = both_cores(shared, 2 * rows, shared.shape[1] - 2 * rows)
    new[...] = updated(updated(carried, interleaved(*below, half)), z)


def last_kernel(bit, pair, carried, out):
    side = bit_of("gx", bit)
    rank = carried.shape[1]
    own, sib = pair[side], pair[1 - side]
    z = solve_own(own[:rank], sib[:rank], own[rank:], sib[rank:])
    out[...] = updated(carried, z)


def call(kernel, outs, *args):
    rows = sum(a.size // 128 for a in args)
    return pl.pallas_call(
        kernel,
        out_shape=[jax.ShapeDtypeStruct(o, jnp.float32) for o in outs],
        compiler_params=pltpu.CompilerParams(vmem_limit_bytes=VMEM_BYTES),
        cost_estimate=pl.CostEstimate(
            flops=6 * 128 * 128 * (rows + 14 * 128),
            bytes_accessed=512 * rows,
            transcendentals=0,
        ),
    )(*args)


def bit_groups(count, bits):
    mask = sum(1 << b for b in bits)
    return [
        [
            base | sum(((i >> q) & 1) << b for q, b in enumerate(bits))
            for i in range(1 << len(bits))
        ]
        for base in range(count)
        if not base & mask
    ]


def swap_cores(value):
    return lax.ppermute(value, "gy", [(s, s ^ 1) for s in range(lax.axis_size("gy"))])


def pair_gather(value, axis, bit, also=()):
    mask = sum(1 << b for b in (bit, *also))
    groups = [[d, d ^ mask] for d in range(lax.axis_size(axis)) if not (d >> bit) & 1]
    return lax.all_gather(value, axis, axis_index_groups=groups)


def exchange(value, axis, bits):
    count = lax.axis_size(axis)
    return lax.all_to_all(value, axis, 0, 0, axis_index_groups=bit_groups(count, bits))


def to_all(value, axis, bits):
    return exchange(jnp.broadcast_to(value, (1 << len(bits),) + value.shape), axis, bits)


def up8(value):
    return -(-value // 8) * 8


def shards(right_sides, factor_u, factor_v):
    levels, _, rank = factor_u.shape
    half = rank // 2
    near_chips = [1, 2]

    packed = jnp.concatenate(
        [factor_u.reshape(-1, rank), factor_v.reshape(-1, rank), right_sides.T], axis=0
    )
    rest = ((levels - 2) * rank + right_sides.shape[1]) // 2
    rows = 2 * rank + rest
    held, low, up, next_v, top_v = call(
        functools.partial(first_pair_kernel, levels),
        [
            (rows, 2 * rank),
            (rows, rank),
            (rows, rank),
            (2, 2 * rank, rank),
            (levels - 4, 2 * rank, rank),
        ],
        packed,
        swap_cores(packed),
    )
    z_low, node = call(
        functools.partial(first_node_kernel, 1),
        [(rank + rest, rank), (rank + rest, rank)],
        pair_gather(low, "gy", 1),
        up,
    )
    pair = pair_gather(node, "gy", 1)
    pair = pair_gather(pair[0] + pair[1], "gy", 2)

    rows = rest
    rest -= rank
    n_both, n_sums = (rows + half) // 4, (rows - half) // 4
    held, sent = call(
        functools.partial(between_kernel, 2, 4),
        [(rows, 2 * rank), (4, n_both + n_sums, rank)],
        pair,
        z_low,
        held,
        next_v,
    )
    piece = exchange(sent, "gy", near_chips).sum(axis=0)
    share = call(
        functools.partial(share_kernel, n_both),
        [(4, 2 * n_both + n_sums, rank)],
        pair_gather(piece, "gy", 3),
    )[0]
    pieces = exchange(share, "gy", near_chips)
    shared = call(
        functools.partial(second_shared_kernel, n_both, n_sums, rows),
        [(11 * half, rank)],
        pieces,
        held,
    )[0]
    shared = pair_gather(shared, "gy", 0)
    z_low, node = call(
        functools.partial(second_node_kernel, 3, n_both, n_sums, rows),
        [(rank + rest, rank), (rank + rest, rank)],
        pieces,
        shared,
    )

    count = levels - 4
    n_both = (rest + (count - 1) * half) // 4
    n_sums = (count - 1) * (rest - half) // 4
    s_both, s_sums = up8(-(-n_both // 8)), up8(-(-n_sums // 8))
    mine, other, sent = call(
        functools.partial(upper_kernel, 4, s_both),
        [(rest, rank), (rest, rank), (32, s_both + s_sums, rank)],
        pair_gather(node, "gy", 4, (3,)),
        z_low,
        shared,
        held,
        top_v,
    )
    far = [3, 4, 5]
    sides = exchange(sent, ("gx", "gy"), near_chips + far)
    sides = sides.reshape((2, 16) + sides.shape[1:]).sum(axis=1)
    share = jnp.concatenate(
        [sides[0, :s_both], sides[1, :s_both], sides[0, s_both:] + sides[1, s_both:]], axis=0
    )
    pieces = to_all(share, ("gx", "gy"), far)
    share = jnp.concatenate(
        [
            pieces[:, :s_both].reshape(-1, rank)[:n_both],
            pieces[:, s_both : 2 * s_both].reshape(-1, rank)[:n_both],
        ],
        axis=0,
    )
    gathered = to_all(share, "gy", near_chips)
    sums = pieces[:, 2 * s_both :].reshape(-1, rank)[:n_sums]
    shared = call(
        functools.partial(top_shared_kernel, n_both, rest),
        [(2 * count * half + rest, rank)],
        gathered,
        other,
    )[0]
    width = rest - half
    rows = 2 * rest
    z, part, carried, _ = call(
        functools.partial(top_node_kernel, count, n_both),
        [(width, rank), (n_sums, rank), (rows, rank), (4 * n_sums, rank)],
        gathered,
        pair_gather(shared, "gy", 0),
        mine,
        sums,
    )

    count -= 1
    n_both = (width + (count - 1) * half) // 4
    share = call(
        functools.partial(share_kernel, n_both),
        [(4, n_both + n_sums, rank)],
        pair_gather(part, ("gx", "gy"), 6, (5,)),
    )[0]
    gathered = exchange(share, "gy", near_chips)
    shared = call(
        functools.partial(top_shared_kernel, n_both, width),
        [(2 * count * half + width, rank)],
        gathered,
        z,
    )[0]
    width -= half
    rows -= rank
    z, node, carried = call(
        functools.partial(quarter_node_kernel, count, n_both),
        [(width, rank), ((count - 1) * width, rank), (rows, rank)],
        gathered,
        pair_gather(shared, "gy", 0),
        carried,
    )

    count -= 1
    shared = call(
        functools.partial(whole_shared_kernel, 2),
        [(2 * node.shape[0] + width, rank)],
        node,
        pair_gather(node, "gx", 2),
        z,
    )[0]
    rows -= 2 * rank
    node, carried = call(
        functools.partial(whole_node_kernel, count, node.shape[0]),
        [((count - 1) * rows, rank), (rows, rank)],
        pair_gather(shared, "gy", 0),
        carried,
    )

    return call(
        functools.partial(last_kernel, 3),
        [right_sides.shape[::-1]],
        pair_gather(node, "gx", 3, (2,)),
        carried,
    )[0].T


def solution(mesh):
    placed = (P(("gx", "gy"), None), P(None, ("gx", "gy"), None), P(None, ("gx", "gy"), None))
    return jax.shard_map(
        shards, mesh=mesh, in_specs=placed, out_specs=P(("gx", "gy"), None), check_vma=False
    )
```

```python
import functools

import jax
import jax.numpy as jnp
from jax import lax
from jax.experimental import pallas as pl
from jax.experimental.pallas import tpu as pltpu
from jax.sharding import PartitionSpec as P

VMEM_BYTES = 40 * 2**20


def split(value):
    high = value.astype(jnp.bfloat16)
    low = (value - high.astype(jnp.float32)).astype(jnp.bfloat16)
    return high, low


def dot_split(a, b):
    def part(x, y):
        return jnp.dot(x, y, preferred_element_type=jnp.float32)

    return part(a[0], b[0]) + (part(a[0], b[1]) + part(a[1], b[0]))


def kdot(a, b):
    return dot_split(split(a), split(b))


def inverse_of(error):
    total = jnp.eye(error.shape[0], dtype=jnp.float32) + error
    power = error
    for step in range(6):
        parts = split(power)
        power = dot_split(parts, parts)
        total = total + kdot(total, power)
    return total


def solve_own(gram_own, gram_sib, proj_own, proj_sib):
    inverse = inverse_of(kdot(gram_own, gram_sib))
    return kdot(proj_sib - kdot(proj_own, gram_sib), inverse)


def solve_node(own, sib, ops_own, ops_sib, sums):
    rank = own.shape[1]
    width = own.shape[0] - rank
    gram_own, proj_own = split(own[:rank]), split(own[rank:])
    base, lefts = [], []
    for j in range(ops_own.shape[0] // rank):
        at = slice(j * rank, (j + 1) * rank)
        op_sib = split(ops_sib[at])
        base.append(sums[j * width : (j + 1) * width] - dot_split(proj_own, op_sib))
        lefts.append(split(ops_own[at] - dot_split(gram_own, op_sib)))
    z = solve_own(own[:rank], sib[:rank], own[rank:], sib[rank:])
    parts = split(z)
    node = [b - dot_split(parts, left) for b, left in zip(base, lefts)]
    return z, jnp.concatenate(node, axis=0)


def put_rows(out, base, size, start, value):
    at, rows = 0, value.shape[0]
    while at < rows:
        i, r = divmod(start + at, size)
        n = min(size - r, rows - at)
        out[i, base + r : base + r + n] = value[at : at + n]
        at += n


def get_rows(ref, base, size):
    return jnp.concatenate([ref[i, pl.ds(base, size)] for i in range(ref.shape[0])], axis=0)


def bit_of(axis, bit):
    return (lax.axis_index(axis) >> bit) & 1


def times8(value, rows):
    return pl.multiple_of(value * rows, 8)


def first_pair_kernel(levels, mine, other, held, low, up, next_v, top_v):
    rank = mine.shape[1]
    half = rank // 2
    core = bit_of("gy", 0)
    last = (mine.shape[0] - 2 * levels * rank) // 2
    rows = pl.ds(2 * levels * rank + times8(core, last), last)
    for c, ref in enumerate((mine, other)):
        lane = slice(c * rank, (c + 1) * rank)
        for j in range(levels):
            value = ref[j * rank : (j + 1) * rank].T
            if j < 2:
                held[j * rank : (j + 1) * rank, lane] = value
            else:
                at = 2 * rank + (j - 2) * half
                held[at : at + half, lane] = jnp.where(core == 0, value[:half], value[half:])
        held[held.shape[0] - last :, lane] = ref[rows]
    factors = [
        jnp.concatenate([ref[j * rank : (j + 1) * rank] for ref in (mine, other)], axis=0)
        for j in range(levels, 2 * levels)
    ]
    parts = split(held[...])
    low[...] = dot_split(parts, split(factors[0]))
    up[...] = dot_split(parts, split(factors[1]))
    for j in range(2, 4):
        next_v[j - 2] = factors[j]
    for j in range(4, levels):
        top_v[j - 4] = factors[j]


def first_node_kernel(bit, pair, up, z_out, out):
    side = bit_of("gy", bit)
    rank = up.shape[1]
    own, sib = pair[side], pair[1 - side]
    z = solve_own(own[:rank], sib[:rank], own[rank:], sib[rank:])
    z_out[...] = z
    out[...] = up[rank:] - kdot(z, up[:rank])


def after_pair(own, sib, z_low, held):
    rank = own.shape[1]
    z_up = solve_own(own[:rank], sib[:rank], own[rank:], sib[rank:])
    left = held[:rank]
    next_left = held[rank : 2 * rank] - kdot(z_low[:rank], left)
    z_both = jnp.concatenate([z_low[rank:], z_up], axis=1)
    return held[2 * rank :] - kdot(z_both, jnp.concatenate([left, next_left], axis=0))


def between_kernel(bit, shares, pair, z_low, held, v, rest, sent):
    side = bit_of("gy", bit)
    value = after_pair(pair[side], pair[1 - side], z_low, held)
    rest[...] = value
    rows = value.shape[0]
    half = v.shape[2] // 2
    parts = split(value)
    low = dot_split(parts, split(v[0]))
    up = dot_split(parts, split(v[1]))
    n_both = (rows + half) // shares
    put_rows(sent, 0, n_both, 0, low)
    put_rows(sent, 0, n_both, rows, up[:half])
    put_rows(sent, n_both, (rows - half) // shares, 0, up[half:])


def second_shared_kernel(n_both, n_sums, rows, pieces, rest, out):
    rank = out.shape[1]
    half = rank // 2
    for c in range(2):
        both = get_rows(pieces, c * n_both, n_both)
        out[3 * half * c : 3 * half * c + rank] = both[:rank]
        out[3 * half * c + rank : 3 * half * (c + 1)] = both[rows:]
    out[6 * half : 7 * half] = get_rows(pieces, 2 * n_both, n_sums)[:half]
    out[7 * half : 9 * half] = rest[:rank, :rank]
    out[9 * half : 11 * half] = rest[:rank, rank:]


def both_cores(ref, at, n):
    return [ref[c, pl.ds(at, n)] for c in range(2)]


def full_rows(ref, at, n):
    return jnp.concatenate(both_cores(ref, at, n), axis=0)


def second_node_kernel(bit, n_both, n_sums, rows, pieces, shared, z_out, node_out):
    side = bit_of("gy", bit)
    rank = z_out.shape[1]
    half = rank // 2
    children = []
    for which in (side, 1 - side):
        at = times8(which, 3 * half)
        both = get_rows(pieces, times8(which, n_both), n_both)
        children.append(
            (
                jnp.concatenate(
                    [
                        full_rows(shared, at, half),
                        full_rows(shared, at + half, half),
                        both[rank:rows],
                    ],
                    axis=0,
                ),
                full_rows(shared, at + rank, half),
            )
        )
    (own, ops_own), (sib, ops_sib) = children
    sums = get_rows(pieces, 2 * n_both, n_sums)
    sums = jnp.concatenate([full_rows(shared, 6 * half, half), sums[half:]], axis=0)
    z, node = solve_node(own, sib, ops_own, ops_sib, sums)
    z_out[...] = z
    node_out[...] = node


def upper_kernel(bit, s_both, pair, z_low, shared, rest, v, mine, other, sent):
    rank = v.shape[2]
    half = rank // 2
    core = bit_of("gy", 0)
    factors = []
    for c in range(2):
        a, b = shared[c, 7 * half : 9 * half], shared[c, 9 * half : 11 * half]
        here = core == c
        factors.append(
            jnp.concatenate([jnp.where(here, a, b), jnp.where(here, b, a)], axis=1)
        )
    held = jnp.concatenate(
        [factors[0][:half], factors[1][:half], factors[0][half:], factors[1][half:], rest[rank:]],
        axis=0,
    )
    side = bit_of("gy", bit)
    value = after_pair(pair[side], pair[1 - side], z_low, held)
    mine[...] = value[:, :rank]
    other[...] = value[:, rank:]
    count, width = v.shape[0], value.shape[0]
    parts = split(value)
    rows = [dot_split(parts, split(v[j])) for j in range(count)]
    both = jnp.concatenate([rows[0]] + [r[:half] for r in rows[1:]], axis=0)
    sums = jnp.concatenate([r[half:] for r in rows[1:]], axis=0)
    far = sent.shape[0] // 4
    for value, base, size in ((both, 0, s_both), (sums, s_both, sent.shape[1] - s_both)):
        n = value.shape[0] // 4
        for c in range(4):
            for f in range(far):
                at, end = min(f * size, n), min((f + 1) * size, n)
                to = base + end - at
                if end > at:
                    sent[4 * f + c, base:to] = value[c * n + at : c * n + end]
                if to < base + size:
                    sent[4 * f + c, to : base + size] = jnp.zeros(
                        (base + size - to, rank), jnp.float32
                    )


def share_kernel(n_both, pair, out):
    rows = [pair[0, :n_both], pair[1, :n_both], pair[0, n_both:] + pair[1, n_both:]]
    value = jnp.concatenate(rows, axis=0)
    for i in range(out.shape[0]):
        out[i] = value


def interleaved(first, second, block):
    out, at, rows = [], 0, first.shape[0]
    while at < rows:
        n = min(block, rows - at)
        out += [first[at : at + n], second[at : at + n]]
        at += n
    return jnp.concatenate(out, axis=0)


def updated(carried, z):
    rank = z.shape[1]
    return carried[rank:] - kdot(z, carried[:rank])


def top_shared_kernel(n_both, width, gathered, other, out):
    half = out.shape[1] // 2
    n = half + 4 * n_both - width
    for c in range(2):
        both = get_rows(gathered, c * n_both, n_both)
        out[n * c : n * c + half] = both[:half]
        out[n * c + half : n * (c + 1)] = both[width:]
    out[2 * n :] = other[...]


def child_rows(shared, at, half, count, projections):
    own = jnp.concatenate([full_rows(shared, at, half), projections], axis=0)
    ops = [full_rows(shared, at + half * j, half) for j in range(1, count)]
    return own, jnp.concatenate(ops, axis=0)


def top_node_kernel(count, n_both, n_sums, gathered, shared, held, z_out, node_out, part, carried):
    rank = held.shape[1]
    half = rank // 2
    width = held.shape[0]
    core = bit_of("gy", 0)
    side = bit_of("gx", 0)
    children = []
    for which in (side, 1 - side):
        both = get_rows(gathered, times8(which, n_both), n_both)
        at = times8(which, half * count)
        children.append(child_rows(shared, at, half, count, both[half:width]))
    (own, ops_own), (sib, ops_sib) = children
    sums = get_rows(gathered, 2 * n_both, n_sums)
    z, node = solve_node(own, sib, ops_own, ops_sib, sums)
    z_out[...] = z
    node_out[...] = node
    n = part.shape[0]
    part[...] = node_out[pl.ds(times8((lax.axis_index("gy") >> 1) & 3, n), n)]
    swapped = [shared[c, 2 * half * count :] for c in range(2)]
    halves = [jnp.where(core == c, held[...], swapped[c]) for c in range(2)]
    carried[...] = interleaved(halves[0], halves[1], half)


def sibling_kernel(bit, pair, out):
    value = pair[1 - bit_of("gx", bit)]
    for i in range(out.shape[0]):
        out[i] = value


def quarter_shared_kernel(count, own, sib, z, out):
    half = out.shape[1] // 2
    width = own.shape[0] // count
    value = sib[...].reshape(own.shape)
    for j in range(count):
        at = slice(j * width, j * width + half)
        out[j * half : (j + 1) * half] = own[at]
        out[(count + j) * half : (count + j + 1) * half] = value[at]
    out[2 * count * half :] = z[...]


def quarter_node_kernel(count, own, sib, shared, carried, z_out, node_out, new):
    half = own.shape[1] // 2
    width = own.shape[0] // count
    here, there = own[...], sib[...].reshape(own.shape)
    rows_own, ops_own = child_rows(shared, 0, half, count, here[half:width])
    rows_sib, ops_sib = child_rows(shared, half * count, half, count, there[half:width])
    sums = jnp.concatenate(
        [
            here[j * width + half : (j + 1) * width] + there[j * width + half : (j + 1) * width]
            for j in range(1, count)
        ],
        axis=0,
    )
    z, node = solve_node(rows_own, rows_sib, ops_own, ops_sib, sums)
    z_out[...] = z
    node_out[...] = node
    below = both_cores(shared, 2 * count * half, shared.shape[1] - 2 * count * half)
    new[...] = updated(carried, interleaved(*below, half))


def whole_shared_kernel(bit, own, pair, z, out):
    rows = own.shape[0]
    out[:rows] = own[...]
    out[rows : 2 * rows] = pair[1 - bit_of("gx", bit)]
    out[2 * rows :] = z[...]


def whole_node_kernel(count, rows, shared, carried, node_out, new):
    half = carried.shape[1] // 2
    rank = 2 * half
    width = rows // count

    def child(at):
        return [
            interleaved(*both_cores(shared, at + j * width, width), half) for j in range(count)
        ]

    own, sib = child(0), child(rows)
    z, node = solve_node(
        own[0],
        sib[0],
        jnp.concatenate([v[:rank] for v in own[1:]], axis=0),
        jnp.concatenate([v[:rank] for v in sib[1:]], axis=0),
        jnp.concatenate([v[rank:] + w[rank:] for v, w in zip(own[1:], sib[1:])], axis=0),
    )
    node_out[...] = node
    below = both_cores(shared, 2 * rows, shared.shape[1] - 2 * rows)
    new[...] = updated(updated(carried, interleaved(*below, half)), z)


def last_kernel(bit, pair, carried, out):
    side = bit_of("gx", bit)
    rank = carried.shape[1]
    own, sib = pair[side], pair[1 - side]
    z = solve_own(own[:rank], sib[:rank], own[rank:], sib[rank:])
    out[...] = updated(carried, z)


def call(kernel, outs, *args):
    rows = sum(a.size // 128 for a in args)
    return pl.pallas_call(
        kernel,
        out_shape=[jax.ShapeDtypeStruct(o, jnp.float32) for o in outs],
        compiler_params=pltpu.CompilerParams(vmem_limit_bytes=VMEM_BYTES),
        cost_estimate=pl.CostEstimate(
            flops=6 * 128 * 128 * (rows + 14 * 128),
            bytes_accessed=512 * rows,
            transcendentals=0,
        ),
    )(*args)


def bit_groups(count, bits):
    mask = sum(1 << b for b in bits)
    return [
        [
            base | sum(((i >> q) & 1) << b for q, b in enumerate(bits))
            for i in range(1 << len(bits))
        ]
        for base in range(count)
        if not base & mask
    ]


def swap_cores(value):
    return lax.ppermute(value, "gy", [(s, s ^ 1) for s in range(lax.axis_size("gy"))])


def pair_gather(value, axis, bit, also=()):
    mask = sum(1 << b for b in (bit, *also))
    groups = [[d, d ^ mask] for d in range(lax.axis_size(axis)) if not (d >> bit) & 1]
    return lax.all_gather(value, axis, axis_index_groups=groups)


def exchange(value, axis, bits):
    count = lax.axis_size(axis)
    return lax.all_to_all(value, axis, 0, 0, axis_index_groups=bit_groups(count, bits))


def to_all(value, axis, bits):
    return exchange(jnp.broadcast_to(value, (1 << len(bits),) + value.shape), axis, bits)


def up8(value):
    return -(-value // 8) * 8


def shards(right_sides, factor_u, factor_v):
    levels, _, rank = factor_u.shape
    half = rank // 2
    near_chips = [1, 2]

    packed = jnp.concatenate(
        [factor_u.reshape(-1, rank), factor_v.reshape(-1, rank), right_sides.T], axis=0
    )
    rest = ((levels - 2) * rank + right_sides.shape[1]) // 2
    rows = 2 * rank + rest
    held, low, up, next_v, top_v = call(
        functools.partial(first_pair_kernel, levels),
        [
            (rows, 2 * rank),
            (rows, rank),
            (rows, rank),
            (2, 2 * rank, rank),
            (levels - 4, 2 * rank, rank),
        ],
        packed,
        swap_cores(packed),
    )
    z_low, node = call(
        functools.partial(first_node_kernel, 1),
        [(rank + rest, rank), (rank + rest, rank)],
        pair_gather(low, "gy", 1),
        up,
    )
    pair = pair_gather(node, "gy", 1)
    pair = pair_gather(pair[0] + pair[1], "gy", 2)

    rows = rest
    rest -= rank
    n_both, n_sums = (rows + half) // 4, (rows - half) // 4
    held, sent = call(
        functools.partial(between_kernel, 2, 4),
        [(rows, 2 * rank), (4, n_both + n_sums, rank)],
        pair,
        z_low,
        held,
        next_v,
    )
    piece = exchange(sent, "gy", near_chips).sum(axis=0)
    share = call(
        functools.partial(share_kernel, n_both),
        [(4, 2 * n_both + n_sums, rank)],
        pair_gather(piece, "gy", 3),
    )[0]
    pieces = exchange(share, "gy", near_chips)
    shared = call(
        functools.partial(second_shared_kernel, n_both, n_sums, rows),
        [(11 * half, rank)],
        pieces,
        held,
    )[0]
    shared = pair_gather(shared, "gy", 0)
    z_low, node = call(
        functools.partial(second_node_kernel, 3, n_both, n_sums, rows),
        [(rank + rest, rank), (rank + rest, rank)],
        pieces,
        shared,
    )

    count = levels - 4
    n_both = (rest + (count - 1) * half) // 4
    n_sums = (count - 1) * (rest - half) // 4
    s_both, s_sums = up8(-(-n_both // 8)), up8(-(-n_sums // 8))
    mine, other, sent = call(
        functools.partial(upper_kernel, 4, s_both),
        [(rest, rank), (rest, rank), (32, s_both + s_sums, rank)],
        pair_gather(node, "gy", 4, (3,)),
        z_low,
        shared,
        held,
        top_v,
    )
    far = [3, 4, 5]
    sides = exchange(sent, ("gx", "gy"), near_chips + far)
    sides = sides.reshape((2, 16) + sides.shape[1:]).sum(axis=1)
    share = jnp.concatenate(
        [sides[0, :s_both], sides[1, :s_both], sides[0, s_both:] + sides[1, s_both:]], axis=0
    )
    pieces = to_all(share, ("gx", "gy"), far)
    share = jnp.concatenate(
        [
            pieces[:, :s_both].reshape(-1, rank)[:n_both],
            pieces[:, s_both : 2 * s_both].reshape(-1, rank)[:n_both],
            pieces[:, 2 * s_both :].reshape(-1, rank)[:n_sums],
        ],
        axis=0,
    )
    gathered = to_all(share, "gy", near_chips)
    shared = call(
        functools.partial(top_shared_kernel, n_both, rest),
        [(2 * count * half + rest, rank)],
        gathered,
        other,
    )[0]
    width = rest - half
    z, node, part, carried = call(
        functools.partial(top_node_kernel, count, n_both, n_sums),
        [
            (width, rank),
            ((count - 1) * width, rank),
            ((count - 1) * width // 4, rank),
            (2 * rest, rank),
        ],
        gathered,
        pair_gather(shared, "gy", 0),
        mine,
    )

    count -= 1
    rows = 2 * rest
    near = call(
        functools.partial(sibling_kernel, 1), [(4,) + part.shape], pair_gather(part, "gx", 1, (0,))
    )[0]
    near = exchange(near, "gy", near_chips)
    shared = call(
        functools.partial(quarter_shared_kernel, count),
        [(2 * count * half + width, rank)],
        node,
        near,
        z,
    )[0]
    width -= half
    rows -= rank
    z, node, carried = call(
        functools.partial(quarter_node_kernel, count),
        [(width, rank), ((count - 1) * width, rank), (rows, rank)],
        node,
        near,
        pair_gather(shared, "gy", 0),
        carried,
    )

    count -= 1
    shared = call(
        functools.partial(whole_shared_kernel, 2),
        [(2 * node.shape[0] + width, rank)],
        node,
        pair_gather(node, "gx", 2),
        z,
    )[0]
    rows -= 2 * rank
    node, carried = call(
        functools.partial(whole_node_kernel, count, node.shape[0]),
        [((count - 1) * rows, rank), (rows, rank)],
        pair_gather(shared, "gy", 0),
        carried,
    )

    return call(
        functools.partial(last_kernel, 3),
        [right_sides.shape[::-1]],
        pair_gather(node, "gx", 3, (2,)),
        carried,
    )[0].T


def solution(mesh):
    placed = (P(("gx", "gy"), None), P(None, ("gx", "gy"), None), P(None, ("gx", "gy"), None))
    return jax.shard_map(
        shards, mesh=mesh, in_specs=placed, out_specs=P(("gx", "gy"), None), check_vma=False
    )
```

```python
import functools

import jax
import jax.numpy as jnp
from jax import lax
from jax.experimental import pallas as pl
from jax.experimental.pallas import tpu as pltpu
from jax.sharding import PartitionSpec as P

VMEM_BYTES = 40 * 2**20


def split(value):
    high = value.astype(jnp.bfloat16)
    low = (value - high.astype(jnp.float32)).astype(jnp.bfloat16)
    return high, low


def dot_split(a, b):
    def part(x, y):
        return jnp.dot(x, y, preferred_element_type=jnp.float32)

    return part(a[0], b[0]) + (part(a[0], b[1]) + part(a[1], b[0]))


def kdot(a, b):
    return dot_split(split(a), split(b))


def inverse_of(error):
    total = jnp.eye(error.shape[0], dtype=jnp.float32) + error
    power = error
    for step in range(6):
        parts = split(power)
        power = dot_split(parts, parts)
        total = total + kdot(total, power)
    return total


def solve_own(gram_own, gram_sib, proj_own, proj_sib):
    inverse = inverse_of(kdot(gram_own, gram_sib))
    return kdot(proj_sib - kdot(proj_own, gram_sib), inverse)


def solve_node(own, sib, ops_own, ops_sib, sums):
    rank = own.shape[1]
    width = own.shape[0] - rank
    gram_own, proj_own = split(own[:rank]), split(own[rank:])
    base, lefts = [], []
    for j in range(ops_own.shape[0] // rank):
        at = slice(j * rank, (j + 1) * rank)
        op_sib = split(ops_sib[at])
        base.append(sums[j * width : (j + 1) * width] - dot_split(proj_own, op_sib))
        lefts.append(split(ops_own[at] - dot_split(gram_own, op_sib)))
    z = solve_own(own[:rank], sib[:rank], own[rank:], sib[rank:])
    parts = split(z)
    node = [b - dot_split(parts, left) for b, left in zip(base, lefts)]
    return z, jnp.concatenate(node, axis=0)


def put_rows(out, base, size, start, value):
    at, rows = 0, value.shape[0]
    while at < rows:
        i, r = divmod(start + at, size)
        n = min(size - r, rows - at)
        out[i, base + r : base + r + n] = value[at : at + n]
        at += n


def get_rows(ref, base, size):
    return jnp.concatenate([ref[i, pl.ds(base, size)] for i in range(ref.shape[0])], axis=0)


def bit_of(axis, bit):
    return (lax.axis_index(axis) >> bit) & 1


def times8(value, rows):
    return pl.multiple_of(value * rows, 8)


def first_pair_kernel(levels, mine, other, held, low, up, next_v, top_v):
    rank = mine.shape[1]
    half = rank // 2
    core = bit_of("gy", 0)
    last = (mine.shape[0] - 2 * levels * rank) // 2
    rows = pl.ds(2 * levels * rank + times8(core, last), last)
    for c, ref in enumerate((mine, other)):
        lane = slice(c * rank, (c + 1) * rank)
        for j in range(levels):
            value = ref[j * rank : (j + 1) * rank].T
            if j < 2:
                held[j * rank : (j + 1) * rank, lane] = value
            else:
                at = 2 * rank + (j - 2) * half
                held[at : at + half, lane] = jnp.where(core == 0, value[:half], value[half:])
        held[held.shape[0] - last :, lane] = ref[rows]
    factors = [
        jnp.concatenate([ref[j * rank : (j + 1) * rank] for ref in (mine, other)], axis=0)
        for j in range(levels, 2 * levels)
    ]
    parts = split(held[...])
    low[...] = dot_split(parts, split(factors[0]))
    up[...] = dot_split(parts, split(factors[1]))
    for j in range(2, 4):
        next_v[j - 2] = factors[j]
    for j in range(4, levels):
        top_v[j - 4] = factors[j]


def first_node_kernel(bit, pair, up, z_out, out):
    side = bit_of("gy", bit)
    rank = up.shape[1]
    own, sib = pair[side], pair[1 - side]
    z = solve_own(own[:rank], sib[:rank], own[rank:], sib[rank:])
    z_out[...] = z
    out[...] = up[rank:] - kdot(z, up[:rank])


def after_pair(own, sib, z_low, held):
    rank = own.shape[1]
    z_up = solve_own(own[:rank], sib[:rank], own[rank:], sib[rank:])
    left = held[:rank]
    next_left = held[rank : 2 * rank] - kdot(z_low[:rank], left)
    z_both = jnp.concatenate([z_low[rank:], z_up], axis=1)
    return held[2 * rank :] - kdot(z_both, jnp.concatenate([left, next_left], axis=0))


def between_kernel(bit, shares, pair, z_low, held, v, rest, sent):
    side = bit_of("gy", bit)
    value = after_pair(pair[side], pair[1 - side], z_low, held)
    rest[...] = value
    rows = value.shape[0]
    half = v.shape[2] // 2
    parts = split(value)
    low = dot_split(parts, split(v[0]))
    up = dot_split(parts, split(v[1]))
    n_both = (rows + half) // shares
    put_rows(sent, 0, n_both, 0, low)
    put_rows(sent, 0, n_both, rows, up[:half])
    put_rows(sent, n_both, (rows - half) // shares, 0, up[half:])


def second_shared_kernel(n_both, n_sums, rows, pieces, rest, out):
    rank = out.shape[1]
    half = rank // 2
    for c in range(2):
        both = get_rows(pieces, c * n_both, n_both)
        out[3 * half * c : 3 * half * c + rank] = both[:rank]
        out[3 * half * c + rank : 3 * half * (c + 1)] = both[rows:]
    out[6 * half : 7 * half] = get_rows(pieces, 2 * n_both, n_sums)[:half]
    out[7 * half : 9 * half] = rest[:rank, :rank]
    out[9 * half : 11 * half] = rest[:rank, rank:]


def both_cores(ref, at, n):
    return [ref[c, pl.ds(at, n)] for c in range(2)]


def full_rows(ref, at, n):
    return jnp.concatenate(both_cores(ref, at, n), axis=0)


def second_node_kernel(bit, n_both, n_sums, rows, pieces, shared, z_out, node_out):
    side = bit_of("gy", bit)
    rank = z_out.shape[1]
    half = rank // 2
    children = []
    for which in (side, 1 - side):
        at = times8(which, 3 * half)
        both = get_rows(pieces, times8(which, n_both), n_both)
        children.append(
            (
                jnp.concatenate(
                    [
                        full_rows(shared, at, half),
                        full_rows(shared, at + half, half),
                        both[rank:rows],
                    ],
                    axis=0,
                ),
                full_rows(shared, at + rank, half),
            )
        )
    (own, ops_own), (sib, ops_sib) = children
    sums = get_rows(pieces, 2 * n_both, n_sums)
    sums = jnp.concatenate([full_rows(shared, 6 * half, half), sums[half:]], axis=0)
    z, node = solve_node(own, sib, ops_own, ops_sib, sums)
    z_out[...] = z
    node_out[...] = node


def upper_kernel(bit, s_both, pair, z_low, shared, rest, v, mine, other, sent):
    rank = v.shape[2]
    half = rank // 2
    core = bit_of("gy", 0)
    factors = []
    for c in range(2):
        a, b = shared[c, 7 * half : 9 * half], shared[c, 9 * half : 11 * half]
        here = core == c
        factors.append(
            jnp.concatenate([jnp.where(here, a, b), jnp.where(here, b, a)], axis=1)
        )
    held = jnp.concatenate(
        [factors[0][:half], factors[1][:half], factors[0][half:], factors[1][half:], rest[rank:]],
        axis=0,
    )
    side = bit_of("gy", bit)
    value = after_pair(pair[side], pair[1 - side], z_low, held)
    mine[...] = value[:, :rank]
    other[...] = value[:, rank:]
    count, width = v.shape[0], value.shape[0]
    parts = split(value)
    rows = [dot_split(parts, split(v[j])) for j in range(count)]
    both = jnp.concatenate([rows[0]] + [r[:half] for r in rows[1:]], axis=0)
    sums = jnp.concatenate([r[half:] for r in rows[1:]], axis=0)
    far = sent.shape[0] // 4
    for value, base, size in ((both, 0, s_both), (sums, s_both, sent.shape[1] - s_both)):
        n = value.shape[0] // 4
        for c in range(4):
            for f in range(far):
                at, end = min(f * size, n), min((f + 1) * size, n)
                to = base + end - at
                if end > at:
                    sent[4 * f + c, base:to] = value[c * n + at : c * n + end]
                if to < base + size:
                    sent[4 * f + c, to : base + size] = jnp.zeros(
                        (base + size - to, rank), jnp.float32
                    )


def share_kernel(n_both, pair, out):
    rows = [pair[0, :n_both], pair[1, :n_both], pair[0, n_both:] + pair[1, n_both:]]
    value = jnp.concatenate(rows, axis=0)
    for i in range(out.shape[0]):
        out[i] = value


def interleaved(first, second, block):
    out, at, rows = [], 0, first.shape[0]
    while at < rows:
        n = min(block, rows - at)
        out += [first[at : at + n], second[at : at + n]]
        at += n
    return jnp.concatenate(out, axis=0)


def updated(carried, z):
    rank = z.shape[1]
    return carried[rank:] - kdot(z, carried[:rank])


def top_shared_kernel(n_both, width, gathered, other, out):
    half = out.shape[1] // 2
    n = half + 4 * n_both - width
    for c in range(2):
        both = get_rows(gathered, c * n_both, n_both)
        out[n * c : n * c + half] = both[:half]
        out[n * c + half : n * (c + 1)] = both[width:]
    out[2 * n :] = other[...]


def child_rows(shared, at, half, count, projections):
    own = jnp.concatenate([full_rows(shared, at, half), projections], axis=0)
    ops = [full_rows(shared, at + half * j, half) for j in range(1, count)]
    return own, jnp.concatenate(ops, axis=0)


def top_node_kernel(count, n_both, n_sums, gathered, shared, held, z_out, node_out, part, carried):
    rank = held.shape[1]
    half = rank // 2
    width = held.shape[0]
    core = bit_of("gy", 0)
    side = bit_of("gx", 0)
    children = []
    for which in (side, 1 - side):
        both = get_rows(gathered, times8(which, n_both), n_both)
        at = times8(which, half * count)
        children.append(child_rows(shared, at, half, count, both[half:width]))
    (own, ops_own), (sib, ops_sib) = children
    sums = get_rows(gathered, 2 * n_both, n_sums)
    z, node = solve_node(own, sib, ops_own, ops_sib, sums)
    z_out[...] = z
    node_out[...] = node
    n = part.shape[0]
    part[...] = node_out[pl.ds(times8(((lax.axis_index("gy") >> 1) & 3) ^ 1, n), n)]
    swapped = [shared[c, 2 * half * count :] for c in range(2)]
    halves = [jnp.where(core == c, held[...], swapped[c]) for c in range(2)]
    carried[...] = interleaved(halves[0], halves[1], half)


def sibling_kernel(bit, pair, out):
    value = pair[1 - bit_of("gx", bit)]
    for i in range(out.shape[0]):
        out[i] = value


def quarter_shared_kernel(count, own, sib, z, out):
    half = out.shape[1] // 2
    width = own.shape[0] // count
    value = sib[...].reshape(own.shape)
    for j in range(count):
        at = slice(j * width, j * width + half)
        out[j * half : (j + 1) * half] = own[at]
        out[(count + j) * half : (count + j + 1) * half] = value[at]
    out[2 * count * half :] = z[...]


def quarter_node_kernel(count, own, sib, shared, carried, z_out, node_out, new):
    half = own.shape[1] // 2
    width = own.shape[0] // count
    here, there = own[...], sib[...].reshape(own.shape)
    rows_own, ops_own = child_rows(shared, 0, half, count, here[half:width])
    rows_sib, ops_sib = child_rows(shared, half * count, half, count, there[half:width])
    sums = jnp.concatenate(
        [
            here[j * width + half : (j + 1) * width] + there[j * width + half : (j + 1) * width]
            for j in range(1, count)
        ],
        axis=0,
    )
    z, node = solve_node(rows_own, rows_sib, ops_own, ops_sib, sums)
    z_out[...] = z
    node_out[...] = node
    below = both_cores(shared, 2 * count * half, shared.shape[1] - 2 * count * half)
    new[...] = updated(carried, interleaved(*below, half))


def whole_shared_kernel(bit, own, pair, z, out):
    rows = own.shape[0]
    out[:rows] = own[...]
    out[rows : 2 * rows] = pair[1 - bit_of("gx", bit)]
    out[2 * rows :] = z[...]


def whole_node_kernel(count, rows, shared, carried, node_out, new):
    half = carried.shape[1] // 2
    rank = 2 * half
    width = rows // count

    def child(at):
        return [
            interleaved(*both_cores(shared, at + j * width, width), half) for j in range(count)
        ]

    own, sib = child(0), child(rows)
    z, node = solve_node(
        own[0],
        sib[0],
        jnp.concatenate([v[:rank] for v in own[1:]], axis=0),
        jnp.concatenate([v[:rank] for v in sib[1:]], axis=0),
        jnp.concatenate([v[rank:] + w[rank:] for v, w in zip(own[1:], sib[1:])], axis=0),
    )
    node_out[...] = node
    below = both_cores(shared, 2 * rows, shared.shape[1] - 2 * rows)
    new[...] = updated(updated(carried, interleaved(*below, half)), z)


def last_kernel(bit, pair, carried, out):
    side = bit_of("gx", bit)
    rank = carried.shape[1]
    own, sib = pair[side], pair[1 - side]
    z = solve_own(own[:rank], sib[:rank], own[rank:], sib[rank:])
    out[...] = updated(carried, z)


def call(kernel, outs, *args):
    rows = sum(a.size // 128 for a in args)
    return pl.pallas_call(
        kernel,
        out_shape=[jax.ShapeDtypeStruct(o, jnp.float32) for o in outs],
        compiler_params=pltpu.CompilerParams(vmem_limit_bytes=VMEM_BYTES),
        cost_estimate=pl.CostEstimate(
            flops=6 * 128 * 128 * (rows + 14 * 128),
            bytes_accessed=512 * rows,
            transcendentals=0,
        ),
    )(*args)


def bit_groups(count, bits):
    mask = sum(1 << b for b in bits)
    return [
        [
            base | sum(((i >> q) & 1) << b for q, b in enumerate(bits))
            for i in range(1 << len(bits))
        ]
        for base in range(count)
        if not base & mask
    ]


def swap_cores(value):
    return lax.ppermute(value, "gy", [(s, s ^ 1) for s in range(lax.axis_size("gy"))])


def pair_gather(value, axis, bit, also=()):
    mask = sum(1 << b for b in (bit, *also))
    groups = [[d, d ^ mask] for d in range(lax.axis_size(axis)) if not (d >> bit) & 1]
    return lax.all_gather(value, axis, axis_index_groups=groups)


def exchange(value, axis, bits):
    count = lax.axis_size(axis)
    return lax.all_to_all(value, axis, 0, 0, axis_index_groups=bit_groups(count, bits))


def to_all(value, axis, bits):
    return exchange(jnp.broadcast_to(value, (1 << len(bits),) + value.shape), axis, bits)


def up8(value):
    return -(-value // 8) * 8


def shards(right_sides, factor_u, factor_v):
    levels, _, rank = factor_u.shape
    half = rank // 2
    near_chips = [1, 2]

    n = levels * rank
    packed = jnp.zeros((2 * n + right_sides.shape[1], rank), jnp.float32)
    packed = packed.at[:n].set(factor_u.reshape(-1, rank))
    packed = packed.at[n : 2 * n].set(factor_v.reshape(-1, rank))
    packed = packed.at[2 * n :].set(right_sides.T)
    rest = ((levels - 2) * rank + right_sides.shape[1]) // 2
    rows = 2 * rank + rest
    held, low, up, next_v, top_v = call(
        functools.partial(first_pair_kernel, levels),
        [
            (rows, 2 * rank),
            (rows, rank),
            (rows, rank),
            (2, 2 * rank, rank),
            (levels - 4, 2 * rank, rank),
        ],
        packed,
        swap_cores(packed),
    )
    z_low, node = call(
        functools.partial(first_node_kernel, 1),
        [(rank + rest, rank), (rank + rest, rank)],
        pair_gather(low, "gy", 1),
        up,
    )
    pair = pair_gather(node, "gy", 1)
    pair = pair_gather(pair[0] + pair[1], "gy", 2)

    rows = rest
    rest -= rank
    n_both, n_sums = (rows + half) // 4, (rows - half) // 4
    held, sent = call(
        functools.partial(between_kernel, 2, 4),
        [(rows, 2 * rank), (4, n_both + n_sums, rank)],
        pair,
        z_low,
        held,
        next_v,
    )
    piece = exchange(sent, "gy", near_chips).sum(axis=0)
    share = call(
        functools.partial(share_kernel, n_both),
        [(4, 2 * n_both + n_sums, rank)],
        pair_gather(piece, "gy", 3),
    )[0]
    pieces = exchange(share, "gy", near_chips)
    shared = call(
        functools.partial(second_shared_kernel, n_both, n_sums, rows),
        [(11 * half, rank)],
        pieces,
        held,
    )[0]
    shared = pair_gather(shared, "gy", 0)
    z_low, node = call(
        functools.partial(second_node_kernel, 3, n_both, n_sums, rows),
        [(rank + rest, rank), (rank + rest, rank)],
        pieces,
        shared,
    )

    count = levels - 4
    n_both = (rest + (count - 1) * half) // 4
    n_sums = (count - 1) * (rest - half) // 4
    s_both, s_sums = up8(-(-n_both // 8)), up8(-(-n_sums // 8))
    mine, other, sent = call(
        functools.partial(upper_kernel, 4, s_both),
        [(rest, rank), (rest, rank), (32, s_both + s_sums, rank)],
        pair_gather(node, "gy", 4, (3,)),
        z_low,
        shared,
        held,
        top_v,
    )
    far = [3, 4, 5]
    sides = exchange(sent, ("gx", "gy"), near_chips + far)
    sides = sides.reshape((2, 16) + sides.shape[1:]).sum(axis=1)
    share = jnp.concatenate(
        [sides[0, :s_both], sides[1, :s_both], sides[0, s_both:] + sides[1, s_both:]], axis=0
    )
    pieces = to_all(share, ("gx", "gy"), far)
    share = jnp.concatenate(
        [
            pieces[:, :s_both].reshape(-1, rank)[:n_both],
            pieces[:, s_both : 2 * s_both].reshape(-1, rank)[:n_both],
            pieces[:, 2 * s_both :].reshape(-1, rank)[:n_sums],
        ],
        axis=0,
    )
    gathered = to_all(share, "gy", near_chips)
    shared = call(
        functools.partial(top_shared_kernel, n_both, rest),
        [(2 * count * half + rest, rank)],
        gathered,
        other,
    )[0]
    width = rest - half
    z, node, part, carried = call(
        functools.partial(top_node_kernel, count, n_both, n_sums),
        [
            (width, rank),
            ((count - 1) * width, rank),
            ((count - 1) * width // 4, rank),
            (2 * rest, rank),
        ],
        gathered,
        pair_gather(shared, "gy", 0),
        mine,
    )

    count -= 1
    rows = 2 * rest
    near = call(
        functools.partial(sibling_kernel, 1), [(4,) + part.shape], pair_gather(part, ("gx", "gy"), 6, (5, 1))
    )[0]
    near = exchange(near, "gy", near_chips)
    shared = call(
        functools.partial(quarter_shared_kernel, count),
        [(2 * count * half + width, rank)],
        node,
        near,
        z,
    )[0]
    width -= half
    rows -= rank
    z, node, carried = call(
        functools.partial(quarter_node_kernel, count),
        [(width, rank), ((count - 1) * width, rank), (rows, rank)],
        node,
        near,
        pair_gather(shared, "gy", 0),
        carried,
    )

    count -= 1
    shared = call(
        functools.partial(whole_shared_kernel, 2),
        [(2 * node.shape[0] + width, rank)],
        node,
        pair_gather(node, "gx", 2),
        z,
    )[0]
    rows -= 2 * rank
    node, carried = call(
        functools.partial(whole_node_kernel, count, node.shape[0]),
        [((count - 1) * rows, rank), (rows, rank)],
        pair_gather(shared, "gy", 0),
        carried,
    )

    return call(
        functools.partial(last_kernel, 3),
        [right_sides.shape[::-1]],
        pair_gather(node, "gx", 3, (2,)),
        carried,
    )[0].T


def solution(mesh):
    placed = (P(("gx", "gy"), None), P(None, ("gx", "gy"), None), P(None, ("gx", "gy"), None))
    return jax.shard_map(
        shards, mesh=mesh, in_specs=placed, out_specs=P(("gx", "gy"), None), check_vma=False
    )
```

```python
import functools

import jax
import jax.numpy as jnp
from jax import lax
from jax.experimental import pallas as pl
from jax.experimental.pallas import tpu as pltpu
from jax.sharding import PartitionSpec as P

VMEM_BYTES = 40 * 2**20


def split(value):
    high = value.astype(jnp.bfloat16)
    low = (value - high.astype(jnp.float32)).astype(jnp.bfloat16)
    return high, low


def dot_split(a, b):
    def part(x, y):
        return jnp.dot(x, y, preferred_element_type=jnp.float32)

    return part(a[0], b[0]) + (part(a[0], b[1]) + part(a[1], b[0]))


def kdot(a, b):
    return dot_split(split(a), split(b))


def inverse_of(error):
    total = jnp.eye(error.shape[0], dtype=jnp.float32) + error
    power = error
    for step in range(6):
        parts = split(power)
        power = dot_split(parts, parts)
        total = total + kdot(total, power)
    return total


def solve_own(gram_own, gram_sib, proj_own, proj_sib):
    inverse = inverse_of(kdot(gram_own, gram_sib))
    return kdot(proj_sib - kdot(proj_own, gram_sib), inverse)


def solve_node(own, sib, ops_own, ops_sib, sums):
    rank = own.shape[1]
    width = own.shape[0] - rank
    gram_own, proj_own = split(own[:rank]), split(own[rank:])
    base, lefts = [], []
    for j in range(ops_own.shape[0] // rank):
        at = slice(j * rank, (j + 1) * rank)
        op_sib = split(ops_sib[at])
        base.append(sums[j * width : (j + 1) * width] - dot_split(proj_own, op_sib))
        lefts.append(split(ops_own[at] - dot_split(gram_own, op_sib)))
    z = solve_own(own[:rank], sib[:rank], own[rank:], sib[rank:])
    parts = split(z)
    node = [b - dot_split(parts, left) for b, left in zip(base, lefts)]
    return z, jnp.concatenate(node, axis=0)


def put_rows(out, base, size, start, value):
    at, rows = 0, value.shape[0]
    while at < rows:
        i, r = divmod(start + at, size)
        n = min(size - r, rows - at)
        out[i, base + r : base + r + n] = value[at : at + n]
        at += n


def get_rows(ref, base, size):
    return jnp.concatenate([ref[i, pl.ds(base, size)] for i in range(ref.shape[0])], axis=0)


def bit_of(axis, bit):
    return (lax.axis_index(axis) >> bit) & 1


def times8(value, rows):
    return pl.multiple_of(value * rows, 8)


def first_pair_kernel(levels, mine, other, held, low, up, next_v, top_v):
    rank = mine.shape[1]
    half = rank // 2
    core = bit_of("gy", 0)
    last = (mine.shape[0] - 2 * levels * rank) // 2
    rows = pl.ds(2 * levels * rank + times8(core, last), last)
    for c, ref in enumerate((mine, other)):
        lane = slice(c * rank, (c + 1) * rank)
        for j in range(levels):
            value = ref[j * rank : (j + 1) * rank].T
            if j < 2:
                held[j * rank : (j + 1) * rank, lane] = value
            else:
                at = 2 * rank + (j - 2) * half
                held[at : at + half, lane] = jnp.where(core == 0, value[:half], value[half:])
        held[held.shape[0] - last :, lane] = ref[rows]
    factors = [
        jnp.concatenate([ref[j * rank : (j + 1) * rank] for ref in (mine, other)], axis=0)
        for j in range(levels, 2 * levels)
    ]
    parts = split(held[...])
    low[...] = dot_split(parts, split(factors[0]))
    up[...] = dot_split(parts, split(factors[1]))
    for j in range(2, 4):
        next_v[j - 2] = factors[j]
    for j in range(4, levels):
        top_v[j - 4] = factors[j]


def first_node_kernel(bit, pair, up, z_out, out):
    side = bit_of("gy", bit)
    rank = up.shape[1]
    own, sib = pair[side], pair[1 - side]
    z = solve_own(own[:rank], sib[:rank], own[rank:], sib[rank:])
    z_out[...] = z
    out[...] = up[rank:] - kdot(z, up[:rank])


def after_pair(own, sib, z_low, held):
    rank = own.shape[1]
    z_up = solve_own(own[:rank], sib[:rank], own[rank:], sib[rank:])
    left = held[:rank]
    next_left = held[rank : 2 * rank] - kdot(z_low[:rank], left)
    z_both = jnp.concatenate([z_low[rank:], z_up], axis=1)
    return held[2 * rank :] - kdot(z_both, jnp.concatenate([left, next_left], axis=0))


def between_kernel(bit, shares, pair, z_low, held, v, rest, sent):
    side = bit_of("gy", bit)
    value = after_pair(pair[side], pair[1 - side], z_low, held)
    rest[...] = value
    rows = value.shape[0]
    half = v.shape[2] // 2
    parts = split(value)
    low = dot_split(parts, split(v[0]))
    up = dot_split(parts, split(v[1]))
    n_both = (rows + half) // shares
    put_rows(sent, 0, n_both, 0, low)
    put_rows(sent, 0, n_both, rows, up[:half])
    put_rows(sent, n_both, (rows - half) // shares, 0, up[half:])


def second_shared_kernel(n_both, n_sums, rows, pieces, rest, out):
    rank = out.shape[1]
    half = rank // 2
    for c in range(2):
        both = get_rows(pieces, c * n_both, n_both)
        out[3 * half * c : 3 * half * c + rank] = both[:rank]
        out[3 * half * c + rank : 3 * half * (c + 1)] = both[rows:]
    out[6 * half : 7 * half] = get_rows(pieces, 2 * n_both, n_sums)[:half]
    out[7 * half : 9 * half] = rest[:rank, :rank]
    out[9 * half : 11 * half] = rest[:rank, rank:]


def both_cores(ref, at, n):
    return [ref[c, pl.ds(at, n)] for c in range(2)]


def full_rows(ref, at, n):
    return jnp.concatenate(both_cores(ref, at, n), axis=0)


def second_node_kernel(bit, n_both, n_sums, rows, pieces, shared, z_out, node_out):
    side = bit_of("gy", bit)
    rank = z_out.shape[1]
    half = rank // 2
    children = []
    for which in (side, 1 - side):
        at = times8(which, 3 * half)
        both = get_rows(pieces, times8(which, n_both), n_both)
        children.append(
            (
                jnp.concatenate(
                    [
                        full_rows(shared, at, half),
                        full_rows(shared, at + half, half),
                        both[rank:rows],
                    ],
                    axis=0,
                ),
                full_rows(shared, at + rank, half),
            )
        )
    (own, ops_own), (sib, ops_sib) = children
    sums = get_rows(pieces, 2 * n_both, n_sums)
    sums = jnp.concatenate([full_rows(shared, 6 * half, half), sums[half:]], axis=0)
    z, node = solve_node(own, sib, ops_own, ops_sib, sums)
    z_out[...] = z
    node_out[...] = node


def upper_kernel(bit, shares, pair, z_low, shared, rest, v, mine, other, sent):
    rank = v.shape[2]
    half = rank // 2
    core = bit_of("gy", 0)
    factors = []
    for c in range(2):
        a, b = shared[c, 7 * half : 9 * half], shared[c, 9 * half : 11 * half]
        here = core == c
        factors.append(
            jnp.concatenate([jnp.where(here, a, b), jnp.where(here, b, a)], axis=1)
        )
    held = jnp.concatenate(
        [factors[0][:half], factors[1][:half], factors[0][half:], factors[1][half:], rest[rank:]],
        axis=0,
    )
    side = bit_of("gy", bit)
    value = after_pair(pair[side], pair[1 - side], z_low, held)
    mine[...] = value[:, :rank]
    other[...] = value[:, rank:]
    count, width = v.shape[0], value.shape[0]
    n_both = (width + (count - 1) * half) // shares
    n_sums = (count - 1) * (width - half) // shares
    parts = split(value)
    put_rows(sent, 0, n_both, 0, dot_split(parts, split(v[0])))
    for j in range(1, count):
        rows = dot_split(parts, split(v[j]))
        put_rows(sent, 0, n_both, width + (j - 1) * half, rows[:half])
        put_rows(sent, n_both, n_sums, (j - 1) * (width - half), rows[half:])


def share_kernel(n_both, pair, out):
    rows = [pair[0, :n_both], pair[1, :n_both], pair[0, n_both:] + pair[1, n_both:]]
    value = jnp.concatenate(rows, axis=0)
    for i in range(out.shape[0]):
        out[i] = value


def interleaved(first, second, block):
    out, at, rows = [], 0, first.shape[0]
    while at < rows:
        n = min(block, rows - at)
        out += [first[at : at + n], second[at : at + n]]
        at += n
    return jnp.concatenate(out, axis=0)


def updated(carried, z):
    rank = z.shape[1]
    return carried[rank:] - kdot(z, carried[:rank])


def top_shared_kernel(n_both, width, gathered, other, out):
    half = out.shape[1] // 2
    n = half + 4 * n_both - width
    for c in range(2):
        both = get_rows(gathered, c * n_both, n_both)
        out[n * c : n * c + half] = both[:half]
        out[n * c + half : n * (c + 1)] = both[width:]
    out[2 * n :] = other[...]


def child_rows(shared, at, half, count, projections):
    own = jnp.concatenate([full_rows(shared, at, half), projections], axis=0)
    ops = [full_rows(shared, at + half * j, half) for j in range(1, count)]
    return own, jnp.concatenate(ops, axis=0)


def top_node_kernel(count, n_both, n_sums, gathered, shared, held, z_out, node_out, part, carried):
    rank = held.shape[1]
    half = rank // 2
    width = held.shape[0]
    core = bit_of("gy", 0)
    side = bit_of("gx", 0)
    children = []
    for which in (side, 1 - side):
        both = get_rows(gathered, times8(which, n_both), n_both)
        at = times8(which, half * count)
        children.append(child_rows(shared, at, half, count, both[half:width]))
    (own, ops_own), (sib, ops_sib) = children
    sums = get_rows(gathered, 2 * n_both, n_sums)
    z, node = solve_node(own, sib, ops_own, ops_sib, sums)
    z_out[...] = z
    node_out[...] = node
    n = part.shape[0]
    part[...] = node_out[pl.ds(times8(((lax.axis_index("gy") >> 1) & 3) ^ 1, n), n)]
    swapped = [shared[c, 2 * half * count :] for c in range(2)]
    halves = [jnp.where(core == c, held[...], swapped[c]) for c in range(2)]
    carried[...] = interleaved(halves[0], halves[1], half)


def sibling_kernel(bit, pair, out):
    value = pair[1 - bit_of("gx", bit)]
    for i in range(out.shape[0]):
        out[i] = value


def quarter_shared_kernel(count, own, sib, z, out):
    half = out.shape[1] // 2
    width = own.shape[0] // count
    value = sib[...].reshape(own.shape)
    for j in range(count):
        at = slice(j * width, j * width + half)
        out[j * half : (j + 1) * half] = own[at]
        out[(count + j) * half : (count + j + 1) * half] = value[at]
    out[2 * count * half :] = z[...]


def quarter_node_kernel(count, own, sib, shared, carried, z_out, node_out, new):
    half = own.shape[1] // 2
    width = own.shape[0] // count
    here, there = own[...], sib[...].reshape(own.shape)
    rows_own, ops_own = child_rows(shared, 0, half, count, here[half:width])
    rows_sib, ops_sib = child_rows(shared, half * count, half, count, there[half:width])
    sums = jnp.concatenate(
        [
            here[j * width + half : (j + 1) * width] + there[j * width + half : (j + 1) * width]
            for j in range(1, count)
        ],
        axis=0,
    )
    z, node = solve_node(rows_own, rows_sib, ops_own, ops_sib, sums)
    z_out[...] = z
    node_out[...] = node
    below = both_cores(shared, 2 * count * half, shared.shape[1] - 2 * count * half)
    new[...] = updated(carried, interleaved(*below, half))


def whole_shared_kernel(bit, own, pair, z, out):
    rows = own.shape[0]
    out[:rows] = own[...]
    out[rows : 2 * rows] = pair[1 - bit_of("gx", bit)]
    out[2 * rows :] = z[...]


def whole_node_kernel(count, rows, shared, carried, node_out, new):
    half = carried.shape[1] // 2
    rank = 2 * half
    width = rows // count

    def child(at):
        return [
            interleaved(*both_cores(shared, at + j * width, width), half) for j in range(count)
        ]

    own, sib = child(0), child(rows)
    z, node = solve_node(
        own[0],
        sib[0],
        jnp.concatenate([v[:rank] for v in own[1:]], axis=0),
        jnp.concatenate([v[:rank] for v in sib[1:]], axis=0),
        jnp.concatenate([v[rank:] + w[rank:] for v, w in zip(own[1:], sib[1:])], axis=0),
    )
    node_out[...] = node
    below = both_cores(shared, 2 * rows, shared.shape[1] - 2 * rows)
    new[...] = updated(updated(carried, interleaved(*below, half)), z)


def last_kernel(bit, pair, carried, out):
    side = bit_of("gx", bit)
    rank = carried.shape[1]
    own, sib = pair[side], pair[1 - side]
    z = solve_own(own[:rank], sib[:rank], own[rank:], sib[rank:])
    out[...] = updated(carried, z)


def call(kernel, outs, *args):
    rows = sum(a.size // 128 for a in args)
    return pl.pallas_call(
        kernel,
        out_shape=[jax.ShapeDtypeStruct(o, jnp.float32) for o in outs],
        compiler_params=pltpu.CompilerParams(vmem_limit_bytes=VMEM_BYTES),
        cost_estimate=pl.CostEstimate(
            flops=6 * 128 * 128 * (rows + 14 * 128),
            bytes_accessed=512 * rows,
            transcendentals=0,
        ),
    )(*args)


def bit_groups(count, bits):
    mask = sum(1 << b for b in bits)
    return [
        [
            base | sum(((i >> q) & 1) << b for q, b in enumerate(bits))
            for i in range(1 << len(bits))
        ]
        for base in range(count)
        if not base & mask
    ]


def swap_cores(value):
    return lax.ppermute(value, "gy", [(s, s ^ 1) for s in range(lax.axis_size("gy"))])


def pair_gather(value, axis, bit, also=()):
    mask = sum(1 << b for b in (bit, *also))
    groups = [[d, d ^ mask] for d in range(lax.axis_size(axis)) if not (d >> bit) & 1]
    return lax.all_gather(value, axis, axis_index_groups=groups)


def exchange(value, axis, bits):
    count = lax.axis_size(axis)
    return lax.all_to_all(value, axis, 0, 0, axis_index_groups=bit_groups(count, bits))


def to_all(value, axis, bits):
    return exchange(jnp.broadcast_to(value, (1 << len(bits),) + value.shape), axis, bits)


def pad_rows(value, rows):
    return jnp.pad(value, ((0, rows - value.shape[0]), (0, 0)))


def up8(value):
    return -(-value // 8) * 8


def shards(right_sides, factor_u, factor_v):
    levels, _, rank = factor_u.shape
    half = rank // 2
    near_chips = [1, 2]

    packed = jnp.concatenate(
        [factor_u.reshape(-1, rank), factor_v.reshape(-1, rank), right_sides.T], axis=0
    )
    rest = ((levels - 2) * rank + right_sides.shape[1]) // 2
    rows = 2 * rank + rest
    held, low, up, next_v, top_v = call(
        functools.partial(first_pair_kernel, levels),
        [
            (rows, 2 * rank),
            (rows, rank),
            (rows, rank),
            (2, 2 * rank, rank),
            (levels - 4, 2 * rank, rank),
        ],
        packed,
        swap_cores(packed),
    )
    z_low, node = call(
        functools.partial(first_node_kernel, 1),
        [(rank + rest, rank), (rank + rest, rank)],
        pair_gather(low, "gy", 1),
        up,
    )
    pair = pair_gather(node, "gy", 1)
    pair = pair_gather(pair[0] + pair[1], "gy", 2)

    rows = rest
    rest -= rank
    n_both, n_sums = (rows + half) // 4, (rows - half) // 4
    held, sent = call(
        functools.partial(between_kernel, 2, 4),
        [(rows, 2 * rank), (4, n_both + n_sums, rank)],
        pair,
        z_low,
        held,
        next_v,
    )
    piece = exchange(sent, "gy", near_chips).sum(axis=0)
    share = call(
        functools.partial(share_kernel, n_both),
        [(4, 2 * n_both + n_sums, rank)],
        pair_gather(piece, "gy", 3),
    )[0]
    pieces = exchange(share, "gy", near_chips)
    shared = call(
        functools.partial(second_shared_kernel, n_both, n_sums, rows),
        [(11 * half, rank)],
        pieces,
        held,
    )[0]
    shared = pair_gather(shared, "gy", 0)
    z_low, node = call(
        functools.partial(second_node_kernel, 3, n_both, n_sums, rows),
        [(rank + rest, rank), (rank + rest, rank)],
        pieces,
        shared,
    )

    count = levels - 4
    n_both = (rest + (count - 1) * half) // 4
    n_sums = (count - 1) * (rest - half) // 4
    mine, other, sent = call(
        functools.partial(upper_kernel, 4, 4),
        [(rest, rank), (rest, rank), (4, n_both + n_sums, rank)],
        pair_gather(node, "gy", 4, (3,)),
        z_low,
        shared,
        held,
        top_v,
    )
    piece = exchange(sent, "gy", near_chips).sum(axis=0)
    s_both, s_sums = up8(-(-n_both // 8)), up8(-(-n_sums // 8))
    sent = jnp.concatenate(
        [
            pad_rows(piece[:n_both], 8 * s_both).reshape(8, s_both, rank),
            pad_rows(piece[n_both:], 8 * s_sums).reshape(8, s_sums, rank),
        ],
        axis=1,
    )
    far = [3, 4, 5]
    sides = exchange(sent, ("gx", "gy"), far)
    sides = sides.reshape((2, 4) + sides.shape[1:]).sum(axis=1)
    share = jnp.concatenate(
        [sides[0, :s_both], sides[1, :s_both], sides[0, s_both:] + sides[1, s_both:]], axis=0
    )
    pieces = to_all(share, ("gx", "gy"), far)
    share = jnp.concatenate(
        [
            pieces[:, :s_both].reshape(-1, rank)[:n_both],
            pieces[:, s_both : 2 * s_both].reshape(-1, rank)[:n_both],
            pieces[:, 2 * s_both :].reshape(-1, rank)[:n_sums],
        ],
        axis=0,
    )
    gathered = to_all(share, "gy", near_chips)
    shared = call(
        functools.partial(top_shared_kernel, n_both, rest),
        [(2 * count * half + rest, rank)],
        gathered,
        other,
    )[0]
    width = rest - half
    z, node, part, carried = call(
        functools.partial(top_node_kernel, count, n_both, n_sums),
        [
            (width, rank),
            ((count - 1) * width, rank),
            ((count - 1) * width // 4, rank),
            (2 * rest, rank),
        ],
        gathered,
        pair_gather(shared, "gy", 0),
        mine,
    )

    count -= 1
    rows = 2 * rest
    near = call(
        functools.partial(sibling_kernel, 1), [(4,) + part.shape], pair_gather(part, ("gx", "gy"), 6, (5, 1))
    )[0]
    near = exchange(near, "gy", near_chips)
    shared = call(
        functools.partial(quarter_shared_kernel, count),
        [(2 * count * half + width, rank)],
        node,
        near,
        z,
    )[0]
    width -= half
    rows -= rank
    z, node, carried = call(
        functools.partial(quarter_node_kernel, count),
        [(width, rank), ((count - 1) * width, rank), (rows, rank)],
        node,
        near,
        pair_gather(shared, "gy", 0),
        carried,
    )

    count -= 1
    shared = call(
        functools.partial(whole_shared_kernel, 2),
        [(2 * node.shape[0] + width, rank)],
        node,
        pair_gather(node, "gx", 2),
        z,
    )[0]
    rows -= 2 * rank
    node, carried = call(
        functools.partial(whole_node_kernel, count, node.shape[0]),
        [((count - 1) * rows, rank), (rows, rank)],
        pair_gather(shared, "gy", 0),
        carried,
    )

    return call(
        functools.partial(last_kernel, 3),
        [right_sides.shape[::-1]],
        pair_gather(node, "gx", 3, (2,)),
        carried,
    )[0].T


def solution(mesh):
    placed = (P(("gx", "gy"), None), P(None, ("gx", "gy"), None), P(None, ("gx", "gy"), None))
    return jax.shard_map(
        shards, mesh=mesh, in_specs=placed, out_specs=P(("gx", "gy"), None), check_vma=False
    )
```

```python
import functools

import jax
import jax.numpy as jnp
from jax import lax
from jax.experimental import pallas as pl
from jax.experimental.pallas import tpu as pltpu
from jax.sharding import PartitionSpec as P

VMEM_BYTES = 40 * 2**20


def split(value):
    high = value.astype(jnp.bfloat16)
    low = (value - high.astype(jnp.float32)).astype(jnp.bfloat16)
    return high, low


def dot_split(a, b):
    def part(x, y):
        return jnp.dot(x, y, preferred_element_type=jnp.float32)

    return part(a[0], b[0]) + (part(a[0], b[1]) + part(a[1], b[0]))


def kdot(a, b):
    return dot_split(split(a), split(b))


def inverse_of(error):
    total = jnp.eye(error.shape[0], dtype=jnp.float32) + error
    power = error
    for step in range(6):
        parts = split(power)
        power = dot_split(parts, parts)
        total = total + kdot(total, power)
    return total


def solve_own(gram_own, gram_sib, proj_own, proj_sib):
    inverse = inverse_of(kdot(gram_own, gram_sib))
    return kdot(proj_sib - kdot(proj_own, gram_sib), inverse)


def solve_node(own, sib, ops_own, ops_sib, sums):
    rank = own.shape[1]
    width = own.shape[0] - rank
    gram_own, proj_own = split(own[:rank]), split(own[rank:])
    base, lefts = [], []
    for j in range(ops_own.shape[0] // rank):
        at = slice(j * rank, (j + 1) * rank)
        op_sib = split(ops_sib[at])
        base.append(sums[j * width : (j + 1) * width] - dot_split(proj_own, op_sib))
        lefts.append(split(ops_own[at] - dot_split(gram_own, op_sib)))
    z = solve_own(own[:rank], sib[:rank], own[rank:], sib[rank:])
    parts = split(z)
    node = [b - dot_split(parts, left) for b, left in zip(base, lefts)]
    return z, jnp.concatenate(node, axis=0)


def put_rows(out, base, size, start, value):
    at, rows = 0, value.shape[0]
    while at < rows:
        i, r = divmod(start + at, size)
        n = min(size - r, rows - at)
        out[i, base + r : base + r + n] = value[at : at + n]
        at += n


def get_rows(ref, base, size):
    return jnp.concatenate([ref[i, pl.ds(base, size)] for i in range(ref.shape[0])], axis=0)


def bit_of(axis, bit):
    return (lax.axis_index(axis) >> bit) & 1


def times8(value, rows):
    return pl.multiple_of(value * rows, 8)


def first_pair_kernel(levels, mine, other, held, low, up, next_v, top_v):
    rank = mine.shape[1]
    half = rank // 2
    core = bit_of("gy", 0)
    last = (mine.shape[0] - 2 * levels * rank) // 2
    rows = pl.ds(2 * levels * rank + times8(core, last), last)
    for c, ref in enumerate((mine, other)):
        lane = slice(c * rank, (c + 1) * rank)
        for j in range(levels):
            value = ref[j * rank : (j + 1) * rank].T
            if j < 2:
                held[j * rank : (j + 1) * rank, lane] = value
            else:
                at = 2 * rank + (j - 2) * half
                held[at : at + half, lane] = jnp.where(core == 0, value[:half], value[half:])
        held[held.shape[0] - last :, lane] = ref[rows]
    factors = [
        jnp.concatenate([ref[j * rank : (j + 1) * rank] for ref in (mine, other)], axis=0)
        for j in range(levels, 2 * levels)
    ]
    parts = split(held[...])
    low[...] = dot_split(parts, split(factors[0]))
    up[...] = dot_split(parts, split(factors[1]))
    for j in range(2, 4):
        next_v[j - 2] = factors[j]
    for j in range(4, levels):
        top_v[j - 4] = factors[j]


def first_node_kernel(bit, pair, up, z_out, out):
    side = bit_of("gy", bit)
    rank = up.shape[1]
    own, sib = pair[side], pair[1 - side]
    z = solve_own(own[:rank], sib[:rank], own[rank:], sib[rank:])
    z_out[...] = z
    out[...] = up[rank:] - kdot(z, up[:rank])


def after_pair(own, sib, z_low, held):
    rank = own.shape[1]
    z_up = solve_own(own[:rank], sib[:rank], own[rank:], sib[rank:])
    left = held[:rank]
    next_left = held[rank : 2 * rank] - kdot(z_low[:rank], left)
    z_both = jnp.concatenate([z_low[rank:], z_up], axis=1)
    return held[2 * rank :] - kdot(z_both, jnp.concatenate([left, next_left], axis=0))


def between_kernel(bit, shares, pair, z_low, held, v, rest, sent):
    side = bit_of("gy", bit)
    value = after_pair(pair[side], pair[1 - side], z_low, held)
    rest[...] = value
    rows = value.shape[0]
    half = v.shape[2] // 2
    parts = split(value)
    low = dot_split(parts, split(v[0]))
    up = dot_split(parts, split(v[1]))
    n_both = (rows + half) // shares
    put_rows(sent, 0, n_both, 0, low)
    put_rows(sent, 0, n_both, rows, up[:half])
    put_rows(sent, n_both, (rows - half) // shares, 0, up[half:])


def second_shared_kernel(n_both, n_sums, rows, pieces, rest, out):
    rank = out.shape[1]
    half = rank // 2
    for c in range(2):
        both = get_rows(pieces, c * n_both, n_both)
        out[3 * half * c : 3 * half * c + rank] = both[:rank]
        out[3 * half * c + rank : 3 * half * (c + 1)] = both[rows:]
    out[6 * half : 7 * half] = get_rows(pieces, 2 * n_both, n_sums)[:half]
    out[7 * half : 9 * half] = rest[:rank, :rank]
    out[9 * half : 11 * half] = rest[:rank, rank:]


def both_cores(ref, at, n):
    return [ref[c, pl.ds(at, n)] for c in range(2)]


def full_rows(ref, at, n):
    return jnp.concatenate(both_cores(ref, at, n), axis=0)


def second_node_kernel(bit, n_both, n_sums, rows, pieces, shared, z_out, node_out):
    side = bit_of("gy", bit)
    rank = z_out.shape[1]
    half = rank // 2
    children = []
    for which in (side, 1 - side):
        at = times8(which, 3 * half)
        both = get_rows(pieces, times8(which, n_both), n_both)
        children.append(
            (
                jnp.concatenate(
                    [
                        full_rows(shared, at, half),
                        full_rows(shared, at + half, half),
                        both[rank:rows],
                    ],
                    axis=0,
                ),
                full_rows(shared, at + rank, half),
            )
        )
    (own, ops_own), (sib, ops_sib) = children
    sums = get_rows(pieces, 2 * n_both, n_sums)
    sums = jnp.concatenate([full_rows(shared, 6 * half, half), sums[half:]], axis=0)
    z, node = solve_node(own, sib, ops_own, ops_sib, sums)
    z_out[...] = z
    node_out[...] = node


def upper_kernel(bit, shares, pair, z_low, shared, rest, v, mine, other, sent):
    rank = v.shape[2]
    half = rank // 2
    core = bit_of("gy", 0)
    factors = []
    for c in range(2):
        a, b = shared[c, 7 * half : 9 * half], shared[c, 9 * half : 11 * half]
        here = core == c
        factors.append(
            jnp.concatenate([jnp.where(here, a, b), jnp.where(here, b, a)], axis=1)
        )
    held = jnp.concatenate(
        [factors[0][:half], factors[1][:half], factors[0][half:], factors[1][half:], rest[rank:]],
        axis=0,
    )
    side = bit_of("gy", bit)
    value = after_pair(pair[side], pair[1 - side], z_low, held)
    mine[...] = value[:, :rank]
    other[...] = value[:, rank:]
    count, width = v.shape[0], value.shape[0]
    n_both = (width + (count - 1) * half) // shares
    n_sums = (count - 1) * (width - half) // shares
    parts = split(value)
    put_rows(sent, 0, n_both, 0, dot_split(parts, split(v[0])))
    for j in range(1, count):
        rows = dot_split(parts, split(v[j]))
        put_rows(sent, 0, n_both, width + (j - 1) * half, rows[:half])
        put_rows(sent, n_both, n_sums, (j - 1) * (width - half), rows[half:])


def share_kernel(n_both, pair, out):
    rows = [pair[0, :n_both], pair[1, :n_both], pair[0, n_both:] + pair[1, n_both:]]
    value = jnp.concatenate(rows, axis=0)
    for i in range(out.shape[0]):
        out[i] = value


def interleaved(first, second, block):
    out, at, rows = [], 0, first.shape[0]
    while at < rows:
        n = min(block, rows - at)
        out += [first[at : at + n], second[at : at + n]]
        at += n
    return jnp.concatenate(out, axis=0)


def updated(carried, z):
    rank = z.shape[1]
    return carried[rank:] - kdot(z, carried[:rank])


def top_shared_kernel(n_both, width, gathered, other, out):
    half = out.shape[1] // 2
    n = half + 4 * n_both - width
    for c in range(2):
        both = get_rows(gathered, c * n_both, n_both)
        out[n * c : n * c + half] = both[:half]
        out[n * c + half : n * (c + 1)] = both[width:]
    out[2 * n :] = other[...]


def child_rows(shared, at, half, count, projections):
    own = jnp.concatenate([full_rows(shared, at, half), projections], axis=0)
    ops = [full_rows(shared, at + half * j, half) for j in range(1, count)]
    return own, jnp.concatenate(ops, axis=0)


def top_node_kernel(count, n_both, n_sums, gathered, shared, held, z_out, node_out, part, carried):
    rank = held.shape[1]
    half = rank // 2
    width = held.shape[0]
    core = bit_of("gy", 0)
    side = bit_of("gx", 0)
    children = []
    for which in (side, 1 - side):
        both = get_rows(gathered, times8(which, n_both), n_both)
        at = times8(which, half * count)
        children.append(child_rows(shared, at, half, count, both[half:width]))
    (own, ops_own), (sib, ops_sib) = children
    sums = get_rows(gathered, 2 * n_both, n_sums)
    z, node = solve_node(own, sib, ops_own, ops_sib, sums)
    z_out[...] = z
    node_out[...] = node
    n = part.shape[0]
    part[...] = node_out[pl.ds(times8((lax.axis_index("gy") >> 1) & 3, n), n)]
    swapped = [shared[c, 2 * half * count :] for c in range(2)]
    halves = [jnp.where(core == c, held[...], swapped[c]) for c in range(2)]
    carried[...] = interleaved(halves[0], halves[1], half)


def sibling_kernel(bit, pair, out):
    value = pair[1 - bit_of("gx", bit)]
    for i in range(out.shape[0]):
        out[i] = value


def quarter_shared_kernel(count, own, sib, z, out):
    half = out.shape[1] // 2
    width = own.shape[0] // count
    value = sib[...].reshape(own.shape)
    for j in range(count):
        at = slice(j * width, j * width + half)
        out[j * half : (j + 1) * half] = own[at]
        out[(count + j) * half : (count + j + 1) * half] = value[at]
    out[2 * count * half :] = z[...]


def quarter_node_kernel(count, own, sib, shared, carried, z_out, node_out, new):
    half = own.shape[1] // 2
    width = own.shape[0] // count
    here, there = own[...], sib[...].reshape(own.shape)
    rows_own, ops_own = child_rows(shared, 0, half, count, here[half:width])
    rows_sib, ops_sib = child_rows(shared, half * count, half, count, there[half:width])
    sums = jnp.concatenate(
        [
            here[j * width + half : (j + 1) * width] + there[j * width + half : (j + 1) * width]
            for j in range(1, count)
        ],
        axis=0,
    )
    z, node = solve_node(rows_own, rows_sib, ops_own, ops_sib, sums)
    z_out[...] = z
    node_out[...] = node
    below = both_cores(shared, 2 * count * half, shared.shape[1] - 2 * count * half)
    new[...] = updated(carried, interleaved(*below, half))


def whole_shared_kernel(bit, own, pair, z, out):
    rows = own.shape[0]
    out[:rows] = own[...]
    out[rows : 2 * rows] = pair[1 - bit_of("gx", bit)]
    out[2 * rows :] = z[...]


def whole_node_kernel(count, rows, shared, carried, node_out, new):
    half = carried.shape[1] // 2
    rank = 2 * half
    width = rows // count

    def child(at):
        return [
            interleaved(*both_cores(shared, at + j * width, width), half) for j in range(count)
        ]

    own, sib = child(0), child(rows)
    z, node = solve_node(
        own[0],
        sib[0],
        jnp.concatenate([v[:rank] for v in own[1:]], axis=0),
        jnp.concatenate([v[:rank] for v in sib[1:]], axis=0),
        jnp.concatenate([v[rank:] + w[rank:] for v, w in zip(own[1:], sib[1:])], axis=0),
    )
    node_out[...] = node
    below = both_cores(shared, 2 * rows, shared.shape[1] - 2 * rows)
    new[...] = updated(updated(carried, interleaved(*below, half)), z)


def last_kernel(bit, pair, carried, out):
    side = bit_of("gx", bit)
    rank = carried.shape[1]
    own, sib = pair[side], pair[1 - side]
    z = solve_own(own[:rank], sib[:rank], own[rank:], sib[rank:])
    out[...] = updated(carried, z)


def call(kernel, outs, *args):
    rows = sum(a.size // 128 for a in args)
    return pl.pallas_call(
        kernel,
        out_shape=[jax.ShapeDtypeStruct(o, jnp.float32) for o in outs],
        compiler_params=pltpu.CompilerParams(vmem_limit_bytes=VMEM_BYTES),
        cost_estimate=pl.CostEstimate(
            flops=6 * 128 * 128 * (rows + 14 * 128),
            bytes_accessed=512 * rows,
            transcendentals=0,
        ),
    )(*args)


def bit_groups(count, bits):
    mask = sum(1 << b for b in bits)
    return [
        [
            base | sum(((i >> q) & 1) << b for q, b in enumerate(bits))
            for i in range(1 << len(bits))
        ]
        for base in range(count)
        if not base & mask
    ]


def swap_cores(value):
    return lax.ppermute(value, "gy", [(s, s ^ 1) for s in range(lax.axis_size("gy"))])


def pair_gather(value, axis, bit, also=()):
    mask = sum(1 << b for b in (bit, *also))
    groups = [[d, d ^ mask] for d in range(lax.axis_size(axis)) if not (d >> bit) & 1]
    return lax.all_gather(value, axis, axis_index_groups=groups)


def exchange(value, axis, bits):
    count = lax.axis_size(axis)
    return lax.all_to_all(value, axis, 0, 0, axis_index_groups=bit_groups(count, bits))


def to_all(value, axis, bits):
    return exchange(jnp.broadcast_to(value, (1 << len(bits),) + value.shape), axis, bits)


def pad_rows(value, rows):
    return jnp.pad(value, ((0, rows - value.shape[0]), (0, 0)))


def up8(value):
    return -(-value // 8) * 8


def shards(right_sides, factor_u, factor_v):
    levels, _, rank = factor_u.shape
    half = rank // 2
    near_chips = [1, 2]

    packed = jnp.concatenate(
        [factor_u.reshape(-1, rank), factor_v.reshape(-1, rank), right_sides.T], axis=0
    )
    rest = ((levels - 2) * rank + right_sides.shape[1]) // 2
    rows = 2 * rank + rest
    held, low, up, next_v, top_v = call(
        functools.partial(first_pair_kernel, levels),
        [
            (rows, 2 * rank),
            (rows, rank),
            (rows, rank),
            (2, 2 * rank, rank),
            (levels - 4, 2 * rank, rank),
        ],
        packed,
        swap_cores(packed),
    )
    z_low, node = call(
        functools.partial(first_node_kernel, 1),
        [(rank + rest, rank), (rank + rest, rank)],
        pair_gather(low, "gy", 1),
        up,
    )
    pair = pair_gather(node, "gy", 1)
    pair = pair_gather(pair[0] + pair[1], "gy", 2)

    rows = rest
    rest -= rank
    n_both, n_sums = (rows + half) // 4, (rows - half) // 4
    held, sent = call(
        functools.partial(between_kernel, 2, 4),
        [(rows, 2 * rank), (4, n_both + n_sums, rank)],
        pair,
        z_low,
        held,
        next_v,
    )
    piece = exchange(sent, "gy", near_chips).sum(axis=0)
    share = call(
        functools.partial(share_kernel, n_both),
        [(4, 2 * n_both + n_sums, rank)],
        pair_gather(piece, "gy", 3),
    )[0]
    pieces = exchange(share, "gy", near_chips)
    shared = call(
        functools.partial(second_shared_kernel, n_both, n_sums, rows),
        [(11 * half, rank)],
        pieces,
        held,
    )[0]
    shared = pair_gather(shared, "gy", 0)
    z_low, node = call(
        functools.partial(second_node_kernel, 3, n_both, n_sums, rows),
        [(rank + rest, rank), (rank + rest, rank)],
        pieces,
        shared,
    )

    count = levels - 4
    n_both = (rest + (count - 1) * half) // 4
    n_sums = (count - 1) * (rest - half) // 4
    mine, other, sent = call(
        functools.partial(upper_kernel, 4, 4),
        [(rest, rank), (rest, rank), (4, n_both + n_sums, rank)],
        pair_gather(node, "gy", 4, (3,)),
        z_low,
        shared,
        held,
        top_v,
    )
    piece = exchange(sent, "gy", near_chips).sum(axis=0)
    s_both, s_sums = up8(-(-n_both // 8)), up8(-(-n_sums // 8))
    sent = jnp.concatenate(
        [
            pad_rows(piece[:n_both], 8 * s_both).reshape(8, s_both, rank),
            pad_rows(piece[n_both:], 8 * s_sums).reshape(8, s_sums, rank),
        ],
        axis=1,
    )
    far = [3, 4, 5]
    sides = exchange(sent, ("gx", "gy"), far)
    sides = sides.reshape((2, 4) + sides.shape[1:]).sum(axis=1)
    share = jnp.concatenate(
        [sides[0, :s_both], sides[1, :s_both], sides[0, s_both:] + sides[1, s_both:]], axis=0
    )
    pieces = to_all(share, ("gx", "gy"), far)
    share = jnp.concatenate(
        [
            pieces[:, :s_both].reshape(-1, rank)[:n_both],
            pieces[:, s_both : 2 * s_both].reshape(-1, rank)[:n_both],
            pieces[:, 2 * s_both :].reshape(-1, rank)[:n_sums],
        ],
        axis=0,
    )
    gathered = to_all(share, "gy", near_chips)
    shared = call(
        functools.partial(top_shared_kernel, n_both, rest),
        [(2 * count * half + rest, rank)],
        gathered,
        other,
    )[0]
    width = rest - half
    z, node, part, carried = call(
        functools.partial(top_node_kernel, count, n_both, n_sums),
        [
            (width, rank),
            ((count - 1) * width, rank),
            ((count - 1) * width // 4, rank),
            (2 * rest, rank),
        ],
        gathered,
        pair_gather(shared, "gy", 0),
        mine,
    )

    count -= 1
    rows = 2 * rest
    near = call(
        functools.partial(sibling_kernel, 1), [(4,) + part.shape], pair_gather(part, "gx", 1, (0,))
    )[0]
    near = exchange(near, "gy", near_chips)
    shared = call(
        functools.partial(quarter_shared_kernel, count),
        [(2 * count * half + width, rank)],
        node,
        near,
        z,
    )[0]
    width -= half
    rows -= rank
    z, node, carried = call(
        functools.partial(quarter_node_kernel, count),
        [(width, rank), ((count - 1) * width, rank), (rows, rank)],
        node,
        near,
        pair_gather(shared, "gy", 0),
        carried,
    )

    count -= 1
    shared = call(
        functools.partial(whole_shared_kernel, 2),
        [(2 * node.shape[0] + width, rank)],
        node,
        pair_gather(node, "gx", 2),
        z,
    )[0]
    rows -= 2 * rank
    node, carried = call(
        functools.partial(whole_node_kernel, count, node.shape[0]),
        [((count - 1) * rows, rank), (rows, rank)],
        pair_gather(shared, "gy", 0),
        carried,
    )

    return call(
        functools.partial(last_kernel, 3),
        [right_sides.shape[::-1]],
        pair_gather(node, "gx", 3, (2,)),
        carried,
    )[0].T


def solution(mesh):
    placed = (P(("gx", "gy"), None), P(None, ("gx", "gy"), None), P(None, ("gx", "gy"), None))
    return jax.shard_map(
        shards, mesh=mesh, in_specs=placed, out_specs=P(("gx", "gy"), None), check_vma=False
    )
```
